768 devices in a mesh: gx: 64 (over y, x, core), gy: 12 (over z).
Axes of the slice: x: 4, y: 8, z: 12, core: 2. Of those that a mesh axis runs over, the one named last changes fastest.
Arguments:
- density: float32 [512, 96, 128], P('gx', 'gy'), may hold values from 0.05 to 1
- solid: int32 [512, 96, 128], P('gx', 'gy'), may hold values 0 or 1
- void: int32 [512, 96, 128], P('gx', 'gy'), may hold values 0 or 1
- fixed: int32 [3, 512, 96, 128], P(None, 'gx', 'gy'), may hold values 0 or 1
- residual: float32 [3, 512, 96, 128], P(None, 'gx', 'gy'), may hold values from -6 to 6
Outputs:
- update: float32 [3, 512, 96, 128], P(None, 'gx', 'gy')
- next_residual: float32 [3, 512, 96, 128], P(None, 'gx', 'gy')
The draws below stay inside these ranges and needn't reach their ends.
All inputs are finite; a program needn't handle non-finite values. No bound on the sum of `solid` or of `void` or of `fixed` on one device may be relied on, other than what follows from the above.
Results may differ from the reference program's by a relative error of at most 0.0003.
Values sent between devices are 32-bit elements; how exact they have to be, the bound alone decides.
No kernel may reach another device: no remote copies, remote signals or barrier semaphores. Data moves between devices by JAX's collectives and lax.ppermute only.
A program may use at most 64 MiB of HBM per device.

```python
import math
import jax
import jax.numpy as jnp
import numpy as np
from jax import lax

NZ = 128
LEVELS = 4
COARSE_ITERS = 4
NX = 512
NY = 96


def place_ends(values, own_key, low, top_value):
    longest = values.shape.index(max(values.shape))
    spots = []
    for shift in (0, 1):
        where = [jax.random.randint(jax.random.fold_in(own_key, axis), (), 0, length) for axis, length in enumerate(values.shape)]
        where[longest] = (where[longest] + shift) % values.shape[longest]
        spots.append(tuple(where))
    return values.at[spots[0]].set(low).at[spots[1]].set(top_value)


def steps_of(stream_key, dims, cuts, smallest, largest):
    def one(position, blocks):
        heights = jax.random.uniform(jax.random.fold_in(jax.random.fold_in(stream_key, 6), position), (blocks,), jnp.float32, smallest / len(cuts), largest / len(cuts))
        return jnp.repeat(jnp.exp(heights), dims[position] // blocks).reshape((-1,) + (1,) * (len(dims) - position - 1))

    level = one(*cuts[0])
    for cut in cuts[1:]:
        level = level * one(*cut)
    return level


def normal_values(rng, dims, width, bound, cuts=(), kind=jnp.bfloat16):
    loudness = steps_of(rng, dims, cuts, -0.22, 0.18) if cuts else 1.0
    values = jax.random.normal(rng, dims, jnp.float32) * width * loudness
    return jnp.minimum(jnp.maximum(values, -bound), bound).astype(kind)


def setup_inputs(seed: int = 0) -> dict:
    seeds = jax.random.split(jax.random.key(seed), 6)
    density = jnp.clip(0.05 + 0.95 * jax.random.uniform(seeds[0], (NX, NY, NZ), jnp.float32) ** steps_of(seeds[0], (NX, NY, NZ), ((0, 64), (1, 12)), -0.2, 0.2), 0.05, 1.0)
    solid = place_ends((jax.random.randint(seeds[1], (NX, NY, NZ), 0, 16) < 1).astype(jnp.int32), jax.random.fold_in(seeds[1], 1), 0, 1)
    void = place_ends((jax.random.randint(seeds[2], (NX, NY, NZ), 0, 16) < 1).astype(jnp.int32), jax.random.fold_in(seeds[2], 1), 0, 1)
    fixed = place_ends((jax.random.randint(seeds[3], (3, NX, NY, NZ), 0, 32) < 1).astype(jnp.int32), jax.random.fold_in(seeds[3], 1), 0, 1)
    residual = normal_values(seeds[4], (3, NX, NY, NZ), 1.0, 6.0, ((1, 64), (2, 12)), jnp.float32)
    return {"density": density, "solid": solid, "void": void, "fixed": fixed, "residual": residual}


damping = 0.6
void_modulus = 0.001

def corner_list():
    return [(a, b, c) for a in (0, 1) for b in (0, 1) for c in (0, 1)]

def element_stiffness():
    poisson = 0.3
    lame_first = poisson / ((1.0 + poisson) * (1.0 - 2.0 * poisson))
    shear = 0.5 / (1.0 + poisson)
    elastic = np.zeros((6, 6))
    elastic[:3, :3] = lame_first
    for i in range(3):
        elastic[i, i] += 2.0 * shear
        elastic[i + 3, i + 3] = shear
    points = [0.5 - 0.5 / math.sqrt(3.0), 0.5 + 0.5 / math.sqrt(3.0)]
    gauss = [(u, v, w) for u in points for v in points for w in points]
    stiffness = np.zeros((24, 24))
    for coord in gauss:
        strain = np.zeros((6, 24))
        for k, corner in enumerate(corner_list()):
            values = [coord[d] if corner[d] else 1.0 - coord[d] for d in range(3)]
            slopes = [2.0 * corner[d] - 1.0 for d in range(3)]
            grad_x = slopes[0] * values[1] * values[2]
            grad_y = values[0] * slopes[1] * values[2]
            grad_z = values[0] * values[1] * slopes[2]
            strain[0, 3 * k] = grad_x
            strain[1, 3 * k + 1] = grad_y
            strain[2, 3 * k + 2] = grad_z
            strain[3, 3 * k] = grad_y
            strain[3, 3 * k + 1] = grad_x
            strain[4, 3 * k + 1] = grad_z
            strain[4, 3 * k + 2] = grad_y
            strain[5, 3 * k] = grad_z
            strain[5, 3 * k + 2] = grad_x
        stiffness += strain.T @ elastic @ strain / 8.0
    return stiffness

def stiffness_diagonal():
    full = element_stiffness()
    return np.array([full[i, i] for i in range(24)])

def pad_last(field):
    return jnp.pad(field, ((0, 0), (0, 0), (0, 0), (1, 1)))

def pad_sides(field):
    return jnp.pad(field, ((0, 0), (1, 1), (1, 1), (0, 0)))

def element_forces(wide, moduli_ext):
    stiffness = jnp.asarray(element_stiffness(), dtype=jnp.float32)
    nodes_x = wide.shape[1] - 2
    nodes_y = wide.shape[2] - 2
    nodes_z = wide.shape[3] - 2
    pieces = [wide[:, a:a + nodes_x + 1, b:b + nodes_y + 1, c:c + nodes_z + 1] for a, b, c in corner_list()]
    stacked = jnp.concatenate(pieces, axis=0)
    layout = stacked.shape
    forces = jnp.dot(stiffness, stacked.reshape(24, -1), precision=lax.Precision.HIGHEST).reshape(layout)
    forces = forces * moduli_ext[None, :nodes_x + 1, :nodes_y + 1, :nodes_z + 1]
    total = jnp.zeros((3, nodes_x, nodes_y, nodes_z), jnp.float32)
    for k, (a, b, c) in enumerate(corner_list()):
        total = total + forces[3 * k:3 * k + 3, 1 - a:1 - a + nodes_x, 1 - b:1 - b + nodes_y, 1 - c:1 - c + nodes_z]
    return total

def blocked_forces(wide, moduli_ext):
    nodes_x = wide.shape[1] - 2
    block = math.gcd(nodes_x, 16)
    count = nodes_x // block

    def one_block(index):
        start = (index * block).astype(jnp.int32)
        part = lax.dynamic_slice_in_dim(wide, start, block + 2, 1)
        mods = lax.dynamic_slice_in_dim(moduli_ext, start, block + 2, 0)
        return element_forces(part, mods)
    blocks = lax.map(one_block, jnp.arange(count, dtype=jnp.int32))
    return jnp.transpose(blocks, (1, 0, 2, 3, 4)).reshape(3, nodes_x, wide.shape[2] - 2, wide.shape[3] - 2)

def apply_operator(field, moduli_ext, free, grow, forces_fn):
    wide = pad_last(grow(field * free))
    return free * forces_fn(wide, moduli_ext) + (1.0 - free) * field

def diagonal_of(moduli_ext, free):
    diag_table = stiffness_diagonal()
    nodes_x, nodes_y, nodes_z = (free.shape[1], free.shape[2], free.shape[3])
    total = jnp.zeros(free.shape, jnp.float32)
    for k, (a, b, c) in enumerate(corner_list()):
        entries = jnp.asarray(diag_table[3 * k:3 * k + 3], dtype=jnp.float32)
        total = total + entries[:, None, None, None] * moduli_ext[None, 1 - a:1 - a + nodes_x, 1 - b:1 - b + nodes_y, 1 - c:1 - c + nodes_z]
    return free * total + (1.0 - free)

def restrict_field(field, grow):
    wide = pad_last(grow(field))
    for axis in (1, 2, 3):
        length = wide.shape[axis] - 2
        centre = lax.slice_in_dim(wide, 1, length + 1, 2, axis)
        lower = lax.slice_in_dim(wide, 0, length, 2, axis)
        upper = lax.slice_in_dim(wide, 2, length + 2, 2, axis)
        wide = centre + 0.5 * (lower + upper)
    return wide

def prolong_field(coarse, grow):
    wide = pad_last(grow(coarse))
    for axis in (1, 2, 3):
        length = wide.shape[axis] - 2
        base = lax.slice_in_dim(wide, 1, length + 1, 1, axis)
        after = lax.slice_in_dim(wide, 2, length + 2, 1, axis)
        middle = 0.5 * (base + after)
        joined = jnp.stack([base, middle], axis=axis + 1)
        target = list(base.shape)
        target[axis] = 2 * length
        wide = joined.reshape(target)
    return wide

def filter_density(density, grow):
    stacked = jnp.stack([density, jnp.ones_like(density)])
    wide = pad_last(grow(stacked))
    size_x, size_y, size_z = density.shape
    numer = jnp.zeros(density.shape, jnp.float32)
    denom = jnp.zeros(density.shape, jnp.float32)
    for dx in (-1, 0, 1):
        for dy in (-1, 0, 1):
            for dz in (-1, 0, 1):
                weight = 2.0 - math.sqrt(dx * dx + dy * dy + dz * dz)
                part = wide[:, 1 + dx:1 + dx + size_x, 1 + dy:1 + dy + size_y, 1 + dz:1 + dz + size_z]
                numer = numer + weight * part[0]
                denom = denom + weight * part[1]
    return numer / denom

def coarsen_moduli(moduli):
    size_x, size_y, size_z = moduli.shape
    grouped = moduli.reshape(size_x // 2, 2, size_y // 2, 2, size_z // 2, 2)
    return 0.25 * lax.optimization_barrier(jnp.sum(grouped, axis=(1, 3, 5)))

def build_levels(moduli, free, grow):
    levels = []
    frees = [free]
    for level in range(LEVELS - 1):
        moduli_ext = pad_last(grow(moduli[None]))[0]
        levels.append((moduli_ext, diagonal_of(moduli_ext, frees[-1])))
        moduli = coarsen_moduli(moduli)
        frees.append(frees[-1][:, ::2, ::2, ::2])
    return (levels, frees, moduli)

def coarse_cg(rhs, moduli, free, grow, total, forces_fn):
    moduli_ext = pad_last(grow(moduli[None]))[0]
    diag = diagonal_of(moduli_ext, free)
    solution = jnp.zeros(rhs.shape, jnp.float32)
    resid = rhs
    precond = resid / diag
    direction = precond
    inner = total(jnp.sum(resid * precond))
    for step in range(COARSE_ITERS):
        image = apply_operator(direction, moduli_ext, free, grow, forces_fn)
        alpha = inner / total(jnp.sum(direction * image))
        solution = solution + alpha * direction
        resid = resid - alpha * image
        if step + 1 < COARSE_ITERS:
            precond = resid / diag
            inner_new = total(jnp.sum(resid * precond))
            direction = precond + inner_new / inner * direction
            inner = inner_new
    return solution

def vcycle(level, rhs, levels, frees, grow, forces_fn, coarse_solve):
    if level == len(levels):
        return coarse_solve(rhs)
    moduli_ext, diag = levels[level]
    free = frees[level]
    smooth = damping * rhs / diag
    defect = rhs - apply_operator(smooth, moduli_ext, free, grow, forces_fn)
    coarse_rhs = frees[level + 1] * restrict_field(defect, grow)
    correction = vcycle(level + 1, coarse_rhs, levels, frees, grow, forces_fn, coarse_solve)
    smooth = smooth + free * prolong_field(correction, grow)
    smooth = smooth + damping * (rhs - apply_operator(smooth, moduli_ext, free, grow, forces_fn)) / diag
    return smooth

def reference(density, solid, void, fixed, residual):
    free = 1.0 - fixed.astype(jnp.float32)
    filtered = filter_density(density, pad_sides)
    solid_f = solid.astype(jnp.float32)
    void_f = void.astype(jnp.float32)
    physical = (1.0 - void_f) * (solid_f + (1.0 - solid_f) * filtered)
    moduli = void_modulus + (1.0 - void_modulus) * physical ** 3
    levels, frees, coarse_moduli = build_levels(moduli, free, pad_sides)

    def coarse_solve(rhs):
        return coarse_cg(rhs, coarse_moduli, frees[-1], pad_sides, jnp.sum, blocked_forces)
    precond = vcycle(0, residual, levels, frees, pad_sides, blocked_forces, coarse_solve)
    image = apply_operator(precond, levels[0][0], free, pad_sides, blocked_forces)
    alpha = jnp.sum(residual * precond) / jnp.sum(precond * image)
    return (alpha * precond, residual - alpha * image)
```

```python
import math

import jax
import jax.numpy as jnp
import numpy as np
from jax import lax
from jax.sharding import PartitionSpec as P

LEVELS = 4
COARSE_ITERS = 4


damping = 0.6
void_modulus = 0.001


def with_halo(shard, sides, width):
    for axis, dim in sides:
        peers, length = (lax.axis_size(axis), shard.shape[dim])
        up = [(i, (i + 1) % peers) for i in range(peers - 1)]
        down = [(j, i) for i, j in up]
        last = lax.slice_in_dim(shard, length - width, length, axis=dim)
        initial = lax.slice_in_dim(shard, 0, width, axis=dim)
        before = lax.ppermute(last, axis, up)
        after = lax.ppermute(initial, axis, down)
        shard = jnp.concatenate([before, shard, after], axis=dim)
    return shard


def corner_list():
    return [(a, b, c) for a in (0, 1) for b in (0, 1) for c in (0, 1)]


def element_stiffness():
    poisson = 0.3
    lame_first = poisson / ((1.0 + poisson) * (1.0 - 2.0 * poisson))
    shear = 0.5 / (1.0 + poisson)
    elastic = np.zeros((6, 6))
    elastic[:3, :3] = lame_first
    for i in range(3):
        elastic[i, i] += 2.0 * shear
        elastic[i + 3, i + 3] = shear
    points = [0.5 - 0.5 / math.sqrt(3.0), 0.5 + 0.5 / math.sqrt(3.0)]
    gauss = [(u, v, w) for u in points for v in points for w in points]
    stiffness = np.zeros((24, 24))
    for coord in gauss:
        strain = np.zeros((6, 24))
        for k, corner in enumerate(corner_list()):
            values = [coord[d] if corner[d] else 1.0 - coord[d] for d in range(3)]
            slopes = [2.0 * corner[d] - 1.0 for d in range(3)]
            grad_x = slopes[0] * values[1] * values[2]
            grad_y = values[0] * slopes[1] * values[2]
            grad_z = values[0] * values[1] * slopes[2]
            strain[0, 3 * k] = grad_x
            strain[1, 3 * k + 1] = grad_y
            strain[2, 3 * k + 2] = grad_z
            strain[3, 3 * k] = grad_y
            strain[3, 3 * k + 1] = grad_x
            strain[4, 3 * k + 1] = grad_z
            strain[4, 3 * k + 2] = grad_y
            strain[5, 3 * k] = grad_z
            strain[5, 3 * k + 2] = grad_x
        stiffness += strain.T @ elastic @ strain / 8.0
    return stiffness


def stiffness_diagonal():
    full = element_stiffness()
    return np.array([full[i, i] for i in range(24)])


def pad_last(field):
    return jnp.pad(field, ((0, 0), (0, 0), (0, 0), (1, 1)))


def grow_rims(field):
    return with_halo(field, (("gx", 1), ("gy", 2)), 1)


def pad_sides(field):
    return jnp.pad(field, ((0, 0), (1, 1), (1, 1), (0, 0)))


def spread(row, axis):
    peers = lax.axis_size(axis)
    return lax.all_to_all(
        jnp.broadcast_to(row[None], (peers,) + row.shape), axis, 0, 0, tiled=True
    )


def grid_totals(values):
    row = jnp.pad(jnp.stack(values), (0, 128 - len(values)))
    row = jnp.sum(spread(row, "gx"), axis=0)
    row = jnp.sum(spread(row, "gy"), axis=0)
    return [row[k] for k in range(len(values))]


def element_forces(wide, moduli_ext):
    stiffness = jnp.asarray(element_stiffness(), dtype=jnp.float32)
    nodes_x = wide.shape[1] - 2
    nodes_y = wide.shape[2] - 2
    nodes_z = wide.shape[3] - 2
    pieces = [
        wide[:, a : a + nodes_x + 1, b : b + nodes_y + 1, c : c + nodes_z + 1]
        for a, b, c in corner_list()
    ]
    stacked = jnp.concatenate(pieces, axis=0)
    layout = stacked.shape
    forces = jnp.dot(stiffness, stacked.reshape(24, -1), precision=lax.Precision.HIGHEST).reshape(
        layout
    )
    forces = forces * moduli_ext[None, : nodes_x + 1, : nodes_y + 1, : nodes_z + 1]
    total = jnp.zeros((3, nodes_x, nodes_y, nodes_z), jnp.float32)
    for k, (a, b, c) in enumerate(corner_list()):
        total = (
            total
            + forces[
                3 * k : 3 * k + 3,
                1 - a : 1 - a + nodes_x,
                1 - b : 1 - b + nodes_y,
                1 - c : 1 - c + nodes_z,
            ]
        )
    return total


def apply_operator(field, moduli_ext, free, grow):
    wide = pad_last(grow(field * free))
    return free * element_forces(wide, moduli_ext) + (1.0 - free) * field


def diagonal_of(moduli_ext, free):
    diag_table = stiffness_diagonal()
    nodes_x, nodes_y, nodes_z = (free.shape[1], free.shape[2], free.shape[3])
    total = jnp.zeros(free.shape, jnp.float32)
    for k, (a, b, c) in enumerate(corner_list()):
        entries = jnp.asarray(diag_table[3 * k : 3 * k + 3], dtype=jnp.float32)
        total = (
            total
            + entries[:, None, None, None]
            * moduli_ext[
                None, 1 - a : 1 - a + nodes_x, 1 - b : 1 - b + nodes_y, 1 - c : 1 - c + nodes_z
            ]
        )
    return free * total + (1.0 - free)


def restrict_field(field):
    wide = pad_last(grow_rims(field))
    for axis in (1, 2, 3):
        length = wide.shape[axis] - 2
        centre = lax.slice_in_dim(wide, 1, length + 1, 2, axis)
        lower = lax.slice_in_dim(wide, 0, length, 2, axis)
        upper = lax.slice_in_dim(wide, 2, length + 2, 2, axis)
        wide = centre + 0.5 * (lower + upper)
    return wide


def prolong_field(coarse):
    wide = pad_last(grow_rims(coarse))
    for axis in (1, 2, 3):
        length = wide.shape[axis] - 2
        base = lax.slice_in_dim(wide, 1, length + 1, 1, axis)
        after = lax.slice_in_dim(wide, 2, length + 2, 1, axis)
        middle = 0.5 * (base + after)
        joined = jnp.stack([base, middle], axis=axis + 1)
        target = list(base.shape)
        target[axis] = 2 * length
        wide = joined.reshape(target)
    return wide


def filter_density(density):
    stacked = jnp.stack([density, jnp.ones_like(density)])
    wide = pad_last(grow_rims(stacked))
    size_x, size_y, size_z = density.shape
    numer = jnp.zeros(density.shape, jnp.float32)
    denom = jnp.zeros(density.shape, jnp.float32)
    for dx in (-1, 0, 1):
        for dy in (-1, 0, 1):
            for dz in (-1, 0, 1):
                weight = 2.0 - math.sqrt(dx * dx + dy * dy + dz * dz)
                part = wide[
                    :, 1 + dx : 1 + dx + size_x, 1 + dy : 1 + dy + size_y, 1 + dz : 1 + dz + size_z
                ]
                numer = numer + weight * part[0]
                denom = denom + weight * part[1]
    return numer / denom


def coarsen_moduli(moduli):
    size_x, size_y, size_z = moduli.shape
    grouped = moduli.reshape(size_x // 2, 2, size_y // 2, 2, size_z // 2, 2)
    return 0.25 * jnp.sum(grouped, axis=(1, 3, 5))


def build_levels(moduli, free):
    levels = []
    frees = [free]
    for level in range(LEVELS - 1):
        moduli_ext = pad_last(grow_rims(moduli[None]))[0]
        levels.append((moduli_ext, diagonal_of(moduli_ext, frees[-1])))
        moduli = coarsen_moduli(moduli)
        frees.append(frees[-1][:, ::2, ::2, ::2])
    return (levels, frees, moduli)


def coarse_cg(rhs, moduli, free):
    moduli_ext = pad_last(pad_sides(moduli[None]))[0]
    diag = diagonal_of(moduli_ext, free)
    solution = jnp.zeros(rhs.shape, jnp.float32)
    resid = rhs
    precond = resid / diag
    direction = precond
    inner = (jnp.sum(resid * precond))
    for step in range(COARSE_ITERS):
        image = apply_operator(direction, moduli_ext, free, pad_sides)
        alpha = inner / (jnp.sum(direction * image))
        solution = solution + alpha * direction
        resid = resid - alpha * image
        if step + 1 < COARSE_ITERS:
            precond = resid / diag
            inner_new = (jnp.sum(resid * precond))
            direction = precond + inner_new / inner * direction
            inner = inner_new
    return solution


def coarse_solution(rhs, moduli, free):
    size_x, size_y, size_z = rhs.shape[1:]
    packed = jnp.concatenate([moduli[None], free, rhs], axis=0).reshape(-1)
    rows = spread(spread(packed, "gx").reshape(-1), "gy")
    peers_x, peers_y = (lax.axis_size("gx"), lax.axis_size("gy"))
    rows = rows.reshape(peers_y, peers_x, 7, size_x, size_y, size_z)
    rows = rows.transpose(2, 1, 3, 0, 4, 5).reshape(7, peers_x * size_x, peers_y * size_y, size_z)
    solved = coarse_cg(rows[4:], rows[0], rows[1:4])
    solved = lax.dynamic_slice_in_dim(solved, lax.axis_index("gx") * size_x, size_x, 1)
    return lax.dynamic_slice_in_dim(solved, lax.axis_index("gy") * size_y, size_y, 2)


def vcycle(level, rhs, levels, frees, coarse_moduli):
    if level == len(levels):
        return coarse_solution(rhs, coarse_moduli, frees[-1])
    moduli_ext, diag = levels[level]
    free = frees[level]
    smooth = damping * rhs / diag
    defect = rhs - apply_operator(smooth, moduli_ext, free, grow_rims)
    coarse_rhs = frees[level + 1] * restrict_field(defect)
    correction = vcycle(level + 1, coarse_rhs, levels, frees, coarse_moduli)
    smooth = smooth + free * prolong_field(correction)
    smooth = smooth + damping * (rhs - apply_operator(smooth, moduli_ext, free, grow_rims)) / diag
    return smooth


def on_device(density, solid, void, fixed, residual):
    free = 1.0 - fixed.astype(jnp.float32)
    filtered = filter_density(density)
    solid_f = solid.astype(jnp.float32)
    void_f = void.astype(jnp.float32)
    physical = (1.0 - void_f) * (solid_f + (1.0 - solid_f) * filtered)
    moduli = void_modulus + (1.0 - void_modulus) * physical**3
    levels, frees, coarse_moduli = build_levels(moduli, free)
    precond = vcycle(0, residual, levels, frees, coarse_moduli)
    image = apply_operator(precond, levels[0][0], free, grow_rims)
    numer, denom = grid_totals([jnp.sum(residual * precond), jnp.sum(precond * image)])
    alpha = numer / denom
    return (alpha * precond, residual - alpha * image)


def solution(mesh):
    return jax.shard_map(
        on_device,
        mesh=mesh,
        in_specs=(
            P("gx", "gy", None),
            P("gx", "gy", None),
            P("gx", "gy", None),
            P(None, "gx", "gy", None),
            P(None, "gx", "gy", None),
        ),
        out_specs=(P(None, "gx", "gy", None), P(None, "gx", "gy", None)),
        check_vma=False,
    )
```

```python
import math

import jax
import jax.numpy as jnp
import numpy as np
from jax import lax
from jax.experimental import pallas as pl
from jax.experimental.pallas import tpu as pltpu
from jax.sharding import PartitionSpec as P

COARSE_ITERS = 4
DAMPING = 0.6
VOID_MODULUS = 0.001
F32 = jnp.float32
PARAMS = pltpu.CompilerParams(vmem_limit_bytes=48 * 1024 * 1024)


def corner_list():
    return [(a, b, c) for a in (0, 1) for b in (0, 1) for c in (0, 1)]


def element_stiffness():
    poisson = 0.3
    lame_first = poisson / ((1.0 + poisson) * (1.0 - 2.0 * poisson))
    shear = 0.5 / (1.0 + poisson)
    elastic = np.zeros((6, 6))
    elastic[:3, :3] = lame_first
    for i in range(3):
        elastic[i, i] += 2.0 * shear
        elastic[i + 3, i + 3] = shear
    points = [0.5 - 0.5 / math.sqrt(3.0), 0.5 + 0.5 / math.sqrt(3.0)]
    gauss = [(u, v, w) for u in points for v in points for w in points]
    stiffness = np.zeros((24, 24))
    for coord in gauss:
        strain = np.zeros((6, 24))
        for k, corner in enumerate(corner_list()):
            values = [coord[d] if corner[d] else 1.0 - coord[d] for d in range(3)]
            slopes = [2.0 * corner[d] - 1.0 for d in range(3)]
            grad_x = slopes[0] * values[1] * values[2]
            grad_y = values[0] * slopes[1] * values[2]
            grad_z = values[0] * values[1] * slopes[2]
            strain[0, 3 * k] = grad_x
            strain[1, 3 * k + 1] = grad_y
            strain[2, 3 * k + 2] = grad_z
            strain[3, 3 * k] = grad_y
            strain[3, 3 * k + 1] = grad_x
            strain[4, 3 * k + 1] = grad_z
            strain[4, 3 * k + 2] = grad_y
            strain[5, 3 * k] = grad_z
            strain[5, 3 * k + 2] = grad_x
        stiffness += strain.T @ elastic @ strain / 8.0
    return stiffness


def mode_table():
    corners = corner_list()
    signs = np.array(
        [[math.prod(2 * c[d] - 1 if m[d] else 1 for d in range(3)) for c in corners] for m in corners],
        float,
    )
    wide = np.kron(signs, np.eye(3))
    table = wide @ element_stiffness() @ wide.T / 64.0
    rows = {}
    for i in range(24):
        row = [
            (corners[j // 3], j % 3, float(table[i, j]))
            for j in range(24)
            if abs(table[i, j]) > 1e-12
        ]
        if row:
            rows[(corners[i // 3], i % 3)] = row
    return rows


MODES = mode_table()
DIAG = float(element_stiffness()[0, 0])
PAIRS = ((0, 0), (1, 0), (0, 1), (1, 1))


def flat_modes(field, z_up, y_up):
    after = z_up(field)
    out = {}
    for k, part in ((0, field + after), (1, after - field)):
        after = y_up(part)
        out[(0, k)] = part + after
        out[(1, k)] = after - part
    return [out[p] for p in PAIRS]


def element_modes(low, high, moduli):
    values = {}
    for c in range(3):
        for q, (j, k) in enumerate(PAIRS):
            if (j, k) != (0, 0):
                values[((0, j, k), c)] = low[c][q] + high[c][q]
            values[((1, j, k), c)] = high[c][q] - low[c][q]
    forces = {}
    for key, row in MODES.items():
        total = None
        for mode, c, weight in row:
            term = weight * values[(mode, c)]
            total = term if total is None else total + term
        forces[key] = total * moduli
    to_low, to_high = [], []
    for c in range(3):
        a, b = [], []
        for j, k in PAIRS:
            slope = forces[((1, j, k), c)]
            mean = forces.get(((0, j, k), c))
            a.append(-slope if mean is None else mean - slope)
            b.append(slope if mean is None else mean + slope)
        to_low.append(a)
        to_high.append(b)
    return to_low, to_high


def node_forces(parts, z_down, y_down):
    out = []
    for k in (0, 1):
        mean, slope = (parts[PAIRS.index((0, k))], parts[PAIRS.index((1, k))])
        out.append((mean - slope) + y_down(mean + slope))
    return (out[0] - out[1]) + z_down(out[0] + out[1])


def shift_up(value, axis):
    return pltpu.roll(value, value.shape[axis] - 1, axis)


def shift_down(value, axis):
    return pltpu.roll(value, 1, axis)


def lanes_of(shape):
    return lax.broadcasted_iota(jnp.int32, shape, len(shape) - 1)


def rows_of(shape):
    return lax.broadcasted_iota(jnp.int32, shape, 0)


def z_shifts(full):
    def up(v):
        s = shift_up(v, 1)
        return jnp.where(lanes_of(v.shape) < v.shape[1] - 1, s, 0.0) if full else s

    def down(v):
        s = shift_down(v, 1)
        return jnp.where(lanes_of(v.shape) > 0, s, 0.0) if full else s

    return up, down


def y_up(v):
    return shift_up(v, 0)


def y_down(v):
    return shift_down(v, 0)


def sweep(load, moduli, first, last, full, emit):
    z_up, z_down = z_shifts(full)

    def modes(x):
        return [flat_modes(load(c, x), z_up, y_up) for c in range(3)]

    high = modes(first + 1)
    _, up = element_modes(modes(first), high, moduli(first))

    def body(x, carry):
        low, before = carry
        high = modes(x + 1)
        own, up = element_modes(low, high, moduli(x))
        forces = [
            node_forces([own[c][q] + before[c][q] for q in range(4)], z_down, y_down)
            for c in range(3)
        ]
        emit(x, forces)
        return (high, up)

    lax.fori_loop(first + 1, last + 1, body, (high, up))


def exact_dot(a, b):
    return jnp.dot(a, b, precision=lax.Precision.HIGHEST, preferred_element_type=F32)


def tent(shape, fine, coarse):
    gap = jnp.abs(fine - 2 * coarse)
    return jnp.where(gap == 0, 1.0, jnp.where(gap == 1, 0.5, 0.0)).astype(F32)


def square(kind, period=128):
    shape = (128, 128)
    fine, coarse = (rows_of(shape), lax.rem(lanes_of(shape), period))
    if kind == "restrict":
        return tent(shape, fine, coarse)
    if kind == "pick":
        return jnp.where(fine == 2 * coarse, 1.0, 0.0).astype(F32)
    return jnp.where((fine == 2 * coarse) | (fine == 2 * coarse + 1), 1.0, 0.0).astype(F32)


def prolong_matrix(period=128):
    shape = (128, 128)
    return tent(shape, lanes_of(shape), lax.rem(rows_of(shape), period))


def smooth_rows(v):
    return v + 0.5 * (y_up(v) + y_down(v))


def corner_sum(v, z_down):
    v = v + z_down(v)
    return v + y_down(v)


def scaled(free, inverse):
    return jnp.where(free > 0.0, inverse, DAMPING)


def first_kernel(
    lo_ref, own_ref, hi_ref,
    m_out, f_out, r_out, s_out, w_out, m1_out, f1_out, c1_out, s1_out, w1_out, pack_out,
    t_ref, b_ref, m_ref, f_ref, r_ref, s_ref, w_ref, u_ref, d_ref, v_ref, m1_ref, u1_ref, d1_ref, v2_ref, m2_ref,
):
    pieces = (lo_ref, own_ref, hi_ref)
    slab = (24, 128)
    z_up, z_down = z_shifts(True)
    gx, gy = (lax.axis_index("gx"), lax.axis_index("gy"))
    nodes_x, nodes_y = (8 * lax.axis_size("gx"), 8 * lax.axis_size("gy"))
    w0, w1, w2, w3 = [2.0 - math.sqrt(n) for n in range(4)]

    def each(first, last, body):
        for p, ref in enumerate(pieces):
            a, b = (max(first, 8 * p), min(last, 8 * p + 7))
            if a <= b:
                lax.fori_loop(a - 8 * p, b - 8 * p + 1, lambda i, _, ref=ref, p=p: body(8 * p + i, ref, i), None)

    def gather_flat(x, ref, i):
        own = ref[0, i]
        ring = z_up(own) + z_down(own)
        c1 = y_up(own) + y_down(own) + ring
        c2 = y_up(ring) + y_down(ring)
        b_ref[x] = w0 * own + w1 * c1 + w2 * c2
        t_ref[x] = w1 * own + w2 * c1 + w3 * c2

    each(0, 23, gather_flat)
    row_at = rows_of(slab) + (8 * gy - 8)
    lane_at = lanes_of(slab)
    inside = ((row_at >= 0) & (row_at < nodes_y)).astype(F32)
    ring_y = (row_at > 0).astype(F32) + (row_at < nodes_y - 1).astype(F32)
    ring_z = (lane_at > 0).astype(F32) + (lane_at < 127).astype(F32)
    plain = w0 + w1 * (ring_y + ring_z) + w2 * ring_y * ring_z
    beside = w1 + w2 * (ring_y + ring_z) + w3 * ring_y * ring_z
    inverse_two, inverse_one = (1.0 / (plain + 2.0 * beside), 1.0 / (plain + beside))

    def moduli_of(x, ref, i):
        at = 8 * gx - 8 + x
        edge = (at == 0) | (at == nodes_x - 1)
        inverse = jnp.where(edge, inverse_one, inverse_two)
        filtered = (b_ref[x] + (t_ref[x - 1] + t_ref[x + 1])) * inverse
        solid, void = (ref[1, i], ref[2, i])
        physical = (1.0 - void) * (solid + (1.0 - solid) * filtered)
        value = VOID_MODULUS + (1.0 - VOID_MODULUS) * (physical * physical * physical)
        mask = jnp.where((at >= 0) & (at < nodes_x), inside, 0.0)
        m_ref[x] = value * mask

    each(1, 22, moduli_of)

    def smooth_of(x, ref, i):
        total = corner_sum(m_ref[x] + m_ref[x - 1], z_down)
        inverse = (DAMPING / DIAG) / total
        for c in range(3):
            free, r = (ref[3 + c, i], ref[6 + c, i])
            w = scaled(free, inverse)
            s = w * r
            f_ref[c, x], r_ref[c, x], w_ref[c, x], s_ref[c, x] = (free, r, w, s)
            u_ref[c, x] = free * s

    each(2, 22, smooth_of)

    def defect_of(x, forces):
        for c in range(3):
            free = f_ref[c, x]
            d_ref[c, x] = r_ref[c, x] - (free * forces[c] + (1.0 - free) * s_ref[c, x])

    sweep(lambda c, x: u_ref[c, x], lambda x: m_ref[x], 2, 21, True, defect_of)

    def keep(x, _):
        m_out[x] = m_ref[x + 6, 4:20, :]
        for c in range(3):
            f_out[c, x] = f_ref[c, x + 6, 4:20, :]
            r_out[c, x] = r_ref[c, x + 6, 4:20, :]
            s_out[c, x] = s_ref[c, x + 6, 4:20, :]
            w_out[c, x] = w_ref[c, x + 6, 4:20, :]

    lax.fori_loop(0, 12, keep, None)

    v_ref[:, 24:32, :] = jnp.zeros((64, 8, 128), F32)

    def to_coarse(n, _):
        x = 2 * n + 4
        for c in range(3):
            v = d_ref[c, x] + 0.5 * (d_ref[c, x - 1] + d_ref[c, x + 1])
            v_ref[9 * c + n, 0:24, :] = smooth_rows(v)
            v_ref[27 + 9 * c + n, 0:24, :] = f_ref[c, x]

    lax.fori_loop(0, 9, to_coarse, None)

    def to_coarse_moduli(n, _):
        x = 2 * n + 2
        v = m_ref[x] + m_ref[x + 1]
        v_ref[54 + n, 0:24, :] = v + y_up(v)

    lax.fori_loop(0, 10, to_coarse_moduli, None)

    def half(first, count, matrix):
        v = v_ref[first : first + count, pl.ds(0, 16, stride=2), :]
        return exact_dot(v.reshape(count * 16, 128), matrix).reshape(count, 16, 128)

    restrict, pick, pair = (square("restrict"), square("pick"), square("pair"))
    m1_ref[...] = 0.25 * half(54, 10, pair)
    m1_out[...] = m1_ref[1:10]
    for c in range(3):
        f1_out[c] = half(27 + 9 * c, 9, pick)
        c1_out[c] = f1_out[c] * half(9 * c, 9, restrict)
    _, plain_down = z_shifts(False)

    def smooth1(n, _):
        inverse = (DAMPING / DIAG) / corner_sum(m1_ref[n + 1] + m1_ref[n], plain_down)
        for c in range(3):
            w = scaled(f1_out[c, n], inverse)
            s = w * c1_out[c, n]
            w1_out[c, n], s1_out[c, n] = (w, s)
            u1_ref[c, n] = f1_out[c, n] * s

    lax.fori_loop(0, 9, smooth1, None)

    def defect1(n, forces):
        for c in range(3):
            free = f1_out[c, n]
            d1_ref[c, n] = c1_out[c, n] - (free * forces[c] + (1.0 - free) * s1_out[c, n])

    sweep(lambda c, n: u1_ref[c, n], lambda n: m1_ref[n + 1], 0, 5, False, defect1)

    for n in range(2):
        x = 2 * n + 2
        for c in range(3):
            v2_ref[2 * c + n] = smooth_rows(d1_ref[c, x] + 0.5 * (d1_ref[c, x - 1] + d1_ref[c, x + 1]))
            v2_ref[6 + 2 * c + n] = f1_out[c, x]
    for n in range(3):
        v = m1_ref[2 * n + 1] + m1_ref[2 * n + 2]
        v2_ref[12 + n] = v + y_up(v)
    v2_ref[15] = jnp.zeros((16, 128), F32)

    def half2(first, count, matrix):
        v = v2_ref[first : first + count, pl.ds(0, 8, stride=2), :]
        return exact_dot(v.reshape(count * 8, 128), matrix).reshape(count, 8, 128)

    free2 = half2(6, 6, pick)
    rhs2 = half2(0, 6, restrict) * free2
    m2_ref[...] = 0.25 * half2(12, 4, pair)
    fields = [[m2_ref[1], m2_ref[2]]]
    fields += [[free2[2 * c], free2[2 * c + 1]] for c in range(3)]
    fields += [[rhs2[2 * c], rhs2[2 * c + 1]] for c in range(3)]
    valid = lanes_of((8, 128)) < 32
    inverse = []
    for n in range(2):
        total = corner_sum(m2_ref[n + 1] + m2_ref[n], plain_down)
        inverse.append(jnp.where(total > 0.0, (DAMPING / DIAG) / total, 0.0))
    fields.append(inverse)
    for f, pairs in enumerate(fields):
        row = None
        for n in range(2):
            v = jnp.where(valid, pairs[n], 0.0)
            for y in range(2):
                piece = v[2 + y : 3 + y]
                q = 2 * n + y
                piece = pltpu.roll(piece, 32 * q, 1) if q else piece
                row = piece if row is None else row + piece
        pack_out[f : f + 1, :] = row


def first_call(lo, own, hi):
    big = lambda *s: jax.ShapeDtypeStruct(s + (16, 128), F32)
    s24 = lambda *s: pltpu.VMEM(s + (24, 128), F32)
    return pl.pallas_call(
        first_kernel,
        out_shape=[big(12), big(3, 12), big(3, 12), big(3, 12), big(3, 12)]
        + [big(9), big(3, 9), big(3, 9), big(3, 9), big(3, 9), jax.ShapeDtypeStruct((8, 128), F32)],
        scratch_shapes=[s24(24), s24(24), s24(24)]
        + [s24(3, 24)] * 6
        + [
            pltpu.VMEM((64, 32, 128), F32),
            pltpu.VMEM((10, 16, 128), F32),
            pltpu.VMEM((3, 9, 16, 128), F32),
            pltpu.VMEM((3, 9, 16, 128), F32),
            pltpu.VMEM((16, 16, 128), F32),
            pltpu.VMEM((4, 8, 128), F32),
        ],
        compiler_params=PARAMS,
    )(lo, own, hi)


def second_kernel(lo_ref, own_ref, hi_ref, hi2_ref, l_out, s_out, w_out, pack_out, u_ref, d_ref, v_ref):
    peers = own_ref.shape[0]
    l_out[...] = jnp.zeros(l_out.shape, F32)
    valid = lanes_of((peers, 128)) < 32
    for ref, base, count in ((lo_ref, 0, 2), (own_ref, 2, 2), (hi_ref, 4, 2), (hi2_ref, 6, 1)):
        for f in range(8):
            rows = ref[:, f, :]
            for n in range(count):
                for y in range(2):
                    q = 2 * n + y
                    v = pltpu.roll(rows, 128 - 32 * q, 1) if q else rows
                    l_out[f, base + n, pl.ds(y, peers, stride=2), :] = jnp.where(valid, v, 0.0)

    def smooth(n, _):
        inverse = l_out[7, n]
        for c in range(3):
            w = scaled(l_out[1 + c, n], inverse)
            s = w * l_out[4 + c, n]
            w_out[c, n], s_out[c, n] = (w, s)
            u_ref[c, n] = l_out[1 + c, n] * s

    lax.fori_loop(0, 7, smooth, None)

    def defect(n, forces):
        for c in range(3):
            free = l_out[1 + c, n]
            d_ref[c, n] = l_out[4 + c, n] - (free * forces[c] + (1.0 - free) * s_out[c, n])

    sweep(lambda c, n: u_ref[c, n], lambda n: l_out[0, n], 0, 3, False, defect)
    for c in range(3):
        v_ref[c] = smooth_rows(d_ref[c, 2] + 0.5 * (d_ref[c, 1] + d_ref[c, 3]))
        v_ref[3 + c] = l_out[1 + c, 2]
    v = l_out[0, 2] + l_out[0, 3]
    v_ref[6] = v + y_up(v)

    def half(first, count, matrix):
        v = v_ref[first : first + count, pl.ds(0, 16, stride=2), :]
        return exact_dot(v.reshape(count * 16, 128), matrix).reshape(count, 16, 128)

    free = half(3, 3, square("pick", 16))
    rhs = half(0, 3, square("restrict", 16)) * free
    moduli = 0.25 * half(6, 1, square("pair", 16))
    shape = (8, 128)
    own_lane = (lanes_of(shape) // 16) == rows_of(shape)
    for f, v in enumerate([moduli[0], free[0], free[1], free[2], rhs[0], rhs[1], rhs[2]]):
        for h in range(2):
            part = jnp.where(own_lane, v[8 * h : 8 * h + 8], 0.0)
            pack_out[f : f + 1, 128 * h : 128 * h + 128] = jnp.sum(part, axis=0, keepdims=True)
    pack_out[7:8, :] = jnp.zeros((1, 256), F32)


def second_call(lo, own, hi, hi2):
    big = lambda *s: jax.ShapeDtypeStruct(s + (32, 128), F32)
    vmem = lambda *s: pltpu.VMEM(s + (32, 128), F32)
    return pl.pallas_call(
        second_kernel,
        out_shape=[big(8, 7), big(3, 7), big(3, 7), jax.ShapeDtypeStruct((8, 256), F32)],
        scratch_shapes=[vmem(3, 7), vmem(3, 7), vmem(7)],
        compiler_params=PARAMS,
    )(lo, own, hi, hi2)


def coarse_solve(rows_ref):
    peers = rows_ref.shape[0]
    shape = (peers + 8, 256)

    def field(f):
        v = rows_ref[:, 256 * f : 256 * f + 256]
        return jnp.concatenate([v, jnp.zeros((8, 256), F32)], axis=0)

    depth = lanes_of(shape) & 15
    z_up = lambda v: jnp.where(depth < 15, shift_up(v, 1), 0.0)
    z_down = lambda v: jnp.where(depth > 0, shift_down(v, 1), 0.0)
    side_up = lambda v: pltpu.roll(v, 240, 1)
    side_down = lambda v: pltpu.roll(v, 16, 1)
    moduli = field(0)
    free = [field(1 + c) for c in range(3)]
    resid = [field(4 + c) for c in range(3)]
    total = moduli + z_down(moduli)
    total = total + side_down(total)
    total = DIAG * (total + shift_down(total, 0))
    inverse = [1.0 / jnp.where(f > 0.0, total, 1.0) for f in free]

    def dot(a, b):
        return jnp.sum(a[0] * b[0] + a[1] * b[1] + a[2] * b[2], keepdims=True)

    def operator(v):
        low = [flat_modes(v[c] * free[c], z_up, side_up) for c in range(3)]
        high = [[shift_up(p, 0) for p in low[c]] for c in range(3)]
        own, up = element_modes(low, high, moduli)
        out = []
        for c in range(3):
            parts = [own[c][q] + shift_down(up[c][q], 0) for q in range(4)]
            forces = node_forces(parts, z_down, side_down)
            out.append(free[c] * forces + (1.0 - free[c]) * v[c])
        return out

    precond = [r * i for r, i in zip(resid, inverse)]
    direction = precond
    inner = dot(resid, precond)
    answer = None
    for step in range(COARSE_ITERS):
        image = operator(direction)
        alpha = inner / dot(direction, image)
        moved = [alpha * d for d in direction]
        answer = moved if answer is None else [s + m for s, m in zip(answer, moved)]
        if step + 1 < COARSE_ITERS:
            resid = [r - alpha * q for r, q in zip(resid, image)]
            precond = [r * i for r, i in zip(resid, inverse)]
            inner_new = dot(resid, precond)
            ratio = inner_new / inner
            direction = [z + ratio * d for z, d in zip(precond, direction)]
            inner = inner_new
    return answer


def third_kernel(
    rows_ref, l2_ref, s2_ref, w2_ref, m1_ref, f1_ref, c1_ref, s1_ref, w1_ref, m_ref, f_ref, r_ref, s_ref, w_ref,
    p_out, q_out, sum_out,
    a_ref, z3_ref, p2_ref, u2_ref, y2_ref, v2_ref, p1_ref, u1_ref, y1_ref, v1_ref, p0_ref, u0_ref, y0_ref,
):
    gx, gy = (lax.axis_index("gx"), lax.axis_index("gy"))
    peers = rows_ref.shape[0]
    answer = coarse_solve(rows_ref)
    for c in range(3):
        a_ref[c, 0:8, :] = jnp.zeros((8, 256), F32)
        a_ref[c, 8 : 16 + peers, :] = answer[c]

    spread3 = prolong_matrix(16)
    shape = (8, 128)
    own_lane = (lanes_of(shape) // 16) == rows_of(shape)
    for c in range(3):
        for i in range(4):
            row = a_ref[c, pl.ds(gx + 7 + i, 1), :]
            halves = [
                jnp.where(own_lane, jnp.broadcast_to(row[:, 128 * h : 128 * h + 128], shape), 0.0)
                for h in range(2)
            ]
            w = exact_dot(jnp.concatenate(halves, axis=0), spread3)
            z3_ref[i, pl.ds(0, 16, stride=2), :] = w
            z3_ref[i, pl.ds(1, 16, stride=2), :] = 0.5 * (w + y_up(w))
        for n in range(7):
            i = n // 2
            p = z3_ref[i] if n % 2 == 0 else 0.5 * (z3_ref[i] + z3_ref[i + 1])
            free = l2_ref[1 + c, n]
            s = s2_ref[c, n] + free * p
            y2_ref[c, n] = s
            u2_ref[c, n] = free * s

    v2_ref[...] = jnp.zeros(v2_ref.shape, F32)

    def level2(n, forces):
        for c in range(3):
            free, s = (l2_ref[1 + c, n], y2_ref[c, n])
            image = free * forces[c] + (1.0 - free) * s
            v2_ref[c, n - 1, 8:40, :] = s + w2_ref[c, n] * (l2_ref[4 + c, n] - image)

    sweep(lambda c, n: u2_ref[c, n], lambda n: l2_ref[0, n], 0, 5, False, level2)

    spread = prolong_matrix()
    for c in range(3):
        for i in range(5):
            w = exact_dot(v2_ref[c, i, pl.ds(2 * gy + 6, 16), :], spread)
            p1_ref[c, i, pl.ds(0, 8, stride=2), :] = w[0:8]
            p1_ref[c, i, pl.ds(1, 8, stride=2), :] = 0.5 * (w[0:8] + w[1:9])
        for n in range(9):
            i = n // 2
            p = p1_ref[c, i] if n % 2 == 0 else 0.5 * (p1_ref[c, i] + p1_ref[c, i + 1])
            free = f1_ref[c, n]
            s = s1_ref[c, n] + free * p
            y1_ref[c, n] = s
            u1_ref[c, n] = free * s

    def level1(n, forces):
        for c in range(3):
            free, s = (f1_ref[c, n], y1_ref[c, n])
            image = free * forces[c] + (1.0 - free) * s
            v1_ref[c, n - 1] = s + w1_ref[c, n] * (c1_ref[c, n] - image)

    sweep(lambda c, n: u1_ref[c, n], lambda n: m1_ref[n], 0, 7, False, level1)

    for c in range(3):
        w = exact_dot(v1_ref[c].reshape(7 * 16, 128), spread).reshape(7, 16, 128)
        for i in range(7):
            p0_ref[c, i, pl.ds(0, 8, stride=2), :] = w[i, 2:10]
            p0_ref[c, i, pl.ds(1, 8, stride=2), :] = 0.5 * (w[i, 2:10] + w[i, 3:11])
        for n in range(12):
            i = n // 2
            p = p0_ref[c, i] if n % 2 == 0 else 0.5 * (p0_ref[c, i] + p0_ref[c, i + 1])
            free = f_ref[c, n]
            s = s_ref[c, n] + free * p
            y0_ref[c, n] = s
            u0_ref[c, n] = free * s

    def level0(n, forces):
        for c in range(3):
            free, s = (f_ref[c, n], y0_ref[c, n])
            image = free * forces[c] + (1.0 - free) * s
            y0_ref[c, n] = s + w_ref[c, n] * (r_ref[c, n] - image)

    sweep(lambda c, n: u0_ref[c, n], lambda n: m_ref[n], 0, 10, True, level0)
    sum_out[...] = jnp.zeros((8, 128), F32)

    def last(n, forces):
        one = two = None
        for c in range(3):
            free, v = (f_ref[c, n], y0_ref[c, n])
            image = (free * forces[c] + (1.0 - free) * v)[4:12]
            v = v[4:12]
            p_out[c, n - 2] = v
            q_out[c, n - 2] = image
            a, b = (r_ref[c, n, 4:12, :] * v, v * image)
            one, two = ((a, b) if one is None else (one + a, two + b))
        sum_out[0:1, :] = sum_out[0:1, :] + jnp.sum(one, axis=0, keepdims=True)
        sum_out[1:2, :] = sum_out[1:2, :] + jnp.sum(two, axis=0, keepdims=True)

    sweep(lambda c, n: f_ref[c, n] * y0_ref[c, n], lambda n: m_ref[n], 1, 9, True, last)
    lane = lanes_of((1, 128))
    one = jnp.sum(sum_out[0:1, :], keepdims=True)
    two = jnp.sum(sum_out[1:2, :], keepdims=True)
    sum_out[0:1, :] = jnp.where(lane == 0, one, jnp.where(lane == 1, two, 0.0))


def third_call(rows, level2, level1, level0):
    own = jax.ShapeDtypeStruct((3, 8, 8, 128), F32)
    peers = rows.shape[0]
    return pl.pallas_call(
        third_kernel,
        out_shape=[own, own, jax.ShapeDtypeStruct((8, 128), F32)],
        scratch_shapes=[
            pltpu.VMEM((3, peers + 16, 256), F32),
            pltpu.VMEM((4, 32, 128), F32),
            pltpu.VMEM((1, 8, 128), F32),
            pltpu.VMEM((3, 7, 32, 128), F32),
            pltpu.VMEM((3, 7, 32, 128), F32),
            pltpu.VMEM((3, 5, 48, 128), F32),
            pltpu.VMEM((3, 5, 16, 128), F32),
            pltpu.VMEM((3, 9, 16, 128), F32),
            pltpu.VMEM((3, 9, 16, 128), F32),
            pltpu.VMEM((3, 7, 16, 128), F32),
            pltpu.VMEM((3, 7, 16, 128), F32),
            pltpu.VMEM((3, 12, 16, 128), F32),
            pltpu.VMEM((3, 12, 16, 128), F32),
        ],
        compiler_params=PARAMS,
    )(rows, *level2, *level1, *level0)


def from_peer(value, axis, step):
    peers = lax.axis_size(axis)
    return lax.ppermute(value, axis, [(i + step, i) for i in range(peers) if 0 <= i + step < peers])


def spread_all(row, axis):
    peers = lax.axis_size(axis)
    return lax.all_to_all(
        jnp.broadcast_to(row[None], (peers,) + row.shape), axis, 0, 0, tiled=True
    )


def on_device(density, solid, void, fixed, residual):
    packed = jnp.concatenate(
        [
            density[None],
            solid.astype(F32)[None],
            void.astype(F32)[None],
            1.0 - fixed.astype(F32),
            residual,
        ],
        axis=0,
    )
    own = jnp.concatenate([from_peer(packed, "gy", -1), packed, from_peer(packed, "gy", 1)], axis=2)
    first = first_call(from_peer(own, "gx", -1), own, from_peer(own, "gx", 1))
    level0, level1, piece = (first[0:5], first[5:10], first[10])
    columns = spread_all(piece, "gy")
    second = second_call(
        from_peer(columns, "gx", -1), columns, from_peer(columns, "gx", 1), from_peer(columns, "gx", 2)
    )
    rows = spread_all(second[3].reshape(-1), "gx")
    precond, image, sums = third_call(rows, second[0:3], level1, level0)
    sums = jnp.sum(spread_all(sums[0], "gx"), axis=0)
    sums = jnp.sum(spread_all(sums, "gy"), axis=0)
    alpha = sums[0] / sums[1]
    return (alpha * precond, residual - alpha * image)


def solution(mesh):
    return jax.shard_map(
        on_device,
        mesh=mesh,
        in_specs=(
            P("gx", "gy", None),
            P("gx", "gy", None),
            P("gx", "gy", None),
            P(None, "gx", "gy", None),
            P(None, "gx", "gy", None),
        ),
        out_specs=(P(None, "gx", "gy", None), P(None, "gx", "gy", None)),
        check_vma=False,
    )
```

```python
import math

import jax
import jax.numpy as jnp
import numpy as np
from jax import lax
from jax.experimental import pallas as pl
from jax.experimental.pallas import tpu as pltpu
from jax.sharding import PartitionSpec as P

COARSE_ITERS = 4
DAMPING = 0.6
VOID_MODULUS = 0.001
F32 = jnp.float32
PARAMS = pltpu.CompilerParams(vmem_limit_bytes=48 * 1024 * 1024)


def corner_list():
    return [(a, b, c) for a in (0, 1) for b in (0, 1) for c in (0, 1)]


def element_stiffness():
    poisson = 0.3
    lame_first = poisson / ((1.0 + poisson) * (1.0 - 2.0 * poisson))
    shear = 0.5 / (1.0 + poisson)
    elastic = np.zeros((6, 6))
    elastic[:3, :3] = lame_first
    for i in range(3):
        elastic[i, i] += 2.0 * shear
        elastic[i + 3, i + 3] = shear
    points = [0.5 - 0.5 / math.sqrt(3.0), 0.5 + 0.5 / math.sqrt(3.0)]
    gauss = [(u, v, w) for u in points for v in points for w in points]
    stiffness = np.zeros((24, 24))
    for coord in gauss:
        strain = np.zeros((6, 24))
        for k, corner in enumerate(corner_list()):
            values = [coord[d] if corner[d] else 1.0 - coord[d] for d in range(3)]
            slopes = [2.0 * corner[d] - 1.0 for d in range(3)]
            grad_x = slopes[0] * values[1] * values[2]
            grad_y = values[0] * slopes[1] * values[2]
            grad_z = values[0] * values[1] * slopes[2]
            strain[0, 3 * k] = grad_x
            strain[1, 3 * k + 1] = grad_y
            strain[2, 3 * k + 2] = grad_z
            strain[3, 3 * k] = grad_y
            strain[3, 3 * k + 1] = grad_x
            strain[4, 3 * k + 1] = grad_z
            strain[4, 3 * k + 2] = grad_y
            strain[5, 3 * k] = grad_z
            strain[5, 3 * k + 2] = grad_x
        stiffness += strain.T @ elastic @ strain / 8.0
    return stiffness


def mode_table():
    corners = corner_list()
    signs = np.array(
        [[math.prod(2 * c[d] - 1 if m[d] else 1 for d in range(3)) for c in corners] for m in corners],
        float,
    )
    wide = np.kron(signs, np.eye(3))
    table = wide @ element_stiffness() @ wide.T / 64.0
    rows = {}
    for i in range(24):
        row = [
            (corners[j // 3], j % 3, float(table[i, j]))
            for j in range(24)
            if abs(table[i, j]) > 1e-12
        ]
        if row:
            rows[(corners[i // 3], i % 3)] = row
    return rows


MODES = mode_table()
DIAG = float(element_stiffness()[0, 0])
PAIRS = ((0, 0), (1, 0), (0, 1), (1, 1))


def flat_modes(field, z_up, y_up):
    after = z_up(field)
    out = {}
    for k, part in ((0, field + after), (1, after - field)):
        after = y_up(part)
        out[(0, k)] = part + after
        out[(1, k)] = after - part
    return [out[p] for p in PAIRS]


def element_modes(low, high, moduli):
    values = {}
    for c in range(3):
        for q, (j, k) in enumerate(PAIRS):
            if (j, k) != (0, 0):
                values[((0, j, k), c)] = low[c][q] + high[c][q]
            values[((1, j, k), c)] = high[c][q] - low[c][q]
    forces = {}
    for key, row in MODES.items():
        total = None
        for mode, c, weight in row:
            term = weight * values[(mode, c)]
            total = term if total is None else total + term
        forces[key] = total * moduli
    to_low, to_high = [], []
    for c in range(3):
        a, b = [], []
        for j, k in PAIRS:
            slope = forces[((1, j, k), c)]
            mean = forces.get(((0, j, k), c))
            a.append(-slope if mean is None else mean - slope)
            b.append(slope if mean is None else mean + slope)
        to_low.append(a)
        to_high.append(b)
    return to_low, to_high


def node_forces(parts, z_down, y_down):
    out = []
    for k in (0, 1):
        mean, slope = (parts[PAIRS.index((0, k))], parts[PAIRS.index((1, k))])
        out.append((mean - slope) + y_down(mean + slope))
    return (out[0] - out[1]) + z_down(out[0] + out[1])


def shift_up(value, axis):
    return pltpu.roll(value, value.shape[axis] - 1, axis)


def shift_down(value, axis):
    return pltpu.roll(value, 1, axis)


def lanes_of(shape):
    return lax.broadcasted_iota(jnp.int32, shape, len(shape) - 1)


def rows_of(shape):
    return lax.broadcasted_iota(jnp.int32, shape, 0)


def z_shifts(full):
    def up(v):
        s = shift_up(v, 1)
        return jnp.where(lanes_of(v.shape) < v.shape[1] - 1, s, 0.0) if full else s

    def down(v):
        s = shift_down(v, 1)
        return jnp.where(lanes_of(v.shape) > 0, s, 0.0) if full else s

    return up, down


def y_up(v):
    return shift_up(v, 0)


def y_down(v):
    return shift_down(v, 0)


def sweep(load, moduli, first, last, full, emit, unroll=True):
    z_up, z_down = z_shifts(full)

    def modes(x):
        return [flat_modes(load(c, x), z_up, y_up) for c in range(3)]

    high = modes(first + 1)
    _, up = element_modes(modes(first), high, moduli(first))

    def body(x, carry):
        low, before = carry
        high = modes(x + 1)
        own, up = element_modes(low, high, moduli(x))
        forces = [
            node_forces([own[c][q] + before[c][q] for q in range(4)], z_down, y_down)
            for c in range(3)
        ]
        emit(x, forces)
        return (high, up)

    lax.fori_loop(first + 1, last + 1, body, (high, up), unroll=unroll)


def exact_dot(a, b):
    return jnp.dot(a, b, precision=lax.Precision.HIGHEST, preferred_element_type=F32)


def tent(shape, fine, coarse):
    gap = jnp.abs(fine - 2 * coarse)
    return jnp.where(gap == 0, 1.0, jnp.where(gap == 1, 0.5, 0.0)).astype(F32)


def square(kind, period=128):
    shape = (128, 128)
    fine, coarse = (rows_of(shape), lax.rem(lanes_of(shape), period))
    if kind == "restrict":
        return tent(shape, fine, coarse)
    if kind == "pick":
        return jnp.where(fine == 2 * coarse, 1.0, 0.0).astype(F32)
    return jnp.where((fine == 2 * coarse) | (fine == 2 * coarse + 1), 1.0, 0.0).astype(F32)


def prolong_matrix(period=128):
    shape = (128, 128)
    return tent(shape, lanes_of(shape), lax.rem(rows_of(shape), period))


def smooth_rows(v):
    return v + 0.5 * (y_up(v) + y_down(v))


def corner_sum(v, z_down):
    v = v + z_down(v)
    return v + y_down(v)


def scaled(free, inverse):
    return jnp.where(free > 0.0, inverse, DAMPING)


def first_kernel(
    lo_ref, own_ref, hi_ref,
    m_out, f_out, r_out, s_out, w_out, m1_out, f1_out, c1_out, s1_out, w1_out, pack_out,
    t_ref, b_ref, m_ref, f_ref, r_ref, s_ref, w_ref, u_ref, d_ref, v_ref, m1_ref, u1_ref, d1_ref, v2_ref, m2_ref,
):
    pieces = (lo_ref, own_ref, hi_ref)
    slab = (24, 128)
    z_up, z_down = z_shifts(True)
    gx, gy = (lax.axis_index("gx"), lax.axis_index("gy"))
    nodes_x, nodes_y = (8 * lax.axis_size("gx"), 8 * lax.axis_size("gy"))
    w0, w1, w2, w3 = [2.0 - math.sqrt(n) for n in range(4)]

    def each(first, last, body):
        for p, ref in enumerate(pieces):
            a, b = (max(first, 8 * p), min(last, 8 * p + 7))
            if a <= b:
                lax.fori_loop(a - 8 * p, b - 8 * p + 1, lambda i, _, ref=ref, p=p: body(8 * p + i, ref, i), None, unroll=True)

    def gather_flat(x, ref, i):
        own = ref[0, i]
        ring = z_up(own) + z_down(own)
        c1 = y_up(own) + y_down(own) + ring
        c2 = y_up(ring) + y_down(ring)
        b_ref[x] = w0 * own + w1 * c1 + w2 * c2
        t_ref[x] = w1 * own + w2 * c1 + w3 * c2

    each(0, 23, gather_flat)
    row_at = rows_of(slab) + (8 * gy - 8)
    lane_at = lanes_of(slab)
    inside = ((row_at >= 0) & (row_at < nodes_y)).astype(F32)
    ring_y = (row_at > 0).astype(F32) + (row_at < nodes_y - 1).astype(F32)
    ring_z = (lane_at > 0).astype(F32) + (lane_at < 127).astype(F32)
    plain = w0 + w1 * (ring_y + ring_z) + w2 * ring_y * ring_z
    beside = w1 + w2 * (ring_y + ring_z) + w3 * ring_y * ring_z
    inverse_two, inverse_one = (1.0 / (plain + 2.0 * beside), 1.0 / (plain + beside))

    def moduli_of(x, ref, i):
        at = 8 * gx - 8 + x
        edge = (at == 0) | (at == nodes_x - 1)
        inverse = jnp.where(edge, inverse_one, inverse_two)
        filtered = (b_ref[x] + (t_ref[x - 1] + t_ref[x + 1])) * inverse
        solid, void = (ref[1, i], ref[2, i])
        physical = (1.0 - void) * (solid + (1.0 - solid) * filtered)
        value = VOID_MODULUS + (1.0 - VOID_MODULUS) * (physical * physical * physical)
        mask = jnp.where((at >= 0) & (at < nodes_x), inside, 0.0)
        m_ref[x] = value * mask

    each(1, 22, moduli_of)

    def smooth_of(x, ref, i):
        total = corner_sum(m_ref[x] + m_ref[x - 1], z_down)
        inverse = (DAMPING / DIAG) / total
        for c in range(3):
            free, r = (ref[3 + c, i], ref[6 + c, i])
            w = scaled(free, inverse)
            s = w * r
            f_ref[c, x], r_ref[c, x], w_ref[c, x], s_ref[c, x] = (free, r, w, s)
            u_ref[c, x] = free * s

    each(2, 22, smooth_of)

    def defect_of(x, forces):
        for c in range(3):
            free = f_ref[c, x]
            d_ref[c, x] = r_ref[c, x] - (free * forces[c] + (1.0 - free) * s_ref[c, x])

    sweep(lambda c, x: u_ref[c, x], lambda x: m_ref[x], 2, 21, True, defect_of)

    def keep(x, _):
        m_out[x] = m_ref[x + 6, 4:20, :]
        for c in range(3):
            f_out[c, x] = f_ref[c, x + 6, 4:20, :]
            r_out[c, x] = r_ref[c, x + 6, 4:20, :]
            s_out[c, x] = s_ref[c, x + 6, 4:20, :]
            w_out[c, x] = w_ref[c, x + 6, 4:20, :]

    lax.fori_loop(0, 12, keep, None, unroll=2)

    v_ref[:, 24:32, :] = jnp.zeros((64, 8, 128), F32)

    def to_coarse(n, _):
        x = 2 * n + 4
        for c in range(3):
            v = d_ref[c, x] + 0.5 * (d_ref[c, x - 1] + d_ref[c, x + 1])
            v_ref[9 * c + n, 0:24, :] = smooth_rows(v)
            v_ref[27 + 9 * c + n, 0:24, :] = f_ref[c, x]

    lax.fori_loop(0, 9, to_coarse, None, unroll=3)

    def to_coarse_moduli(n, _):
        x = 2 * n + 2
        v = m_ref[x] + m_ref[x + 1]
        v_ref[54 + n, 0:24, :] = v + y_up(v)

    lax.fori_loop(0, 10, to_coarse_moduli, None, unroll=5)

    def half(first, count, matrix):
        v = v_ref[first : first + count, pl.ds(0, 16, stride=2), :]
        return exact_dot(v.reshape(count * 16, 128), matrix).reshape(count, 16, 128)

    restrict, pick, pair = (square("restrict"), square("pick"), square("pair"))
    m1_ref[...] = 0.25 * half(54, 10, pair)
    m1_out[...] = m1_ref[1:10]
    for c in range(3):
        f1_out[c] = half(27 + 9 * c, 9, pick)
        c1_out[c] = f1_out[c] * half(9 * c, 9, restrict)
    _, plain_down = z_shifts(False)

    def smooth1(n, _):
        inverse = (DAMPING / DIAG) / corner_sum(m1_ref[n + 1] + m1_ref[n], plain_down)
        for c in range(3):
            w = scaled(f1_out[c, n], inverse)
            s = w * c1_out[c, n]
            w1_out[c, n], s1_out[c, n] = (w, s)
            u1_ref[c, n] = f1_out[c, n] * s

    lax.fori_loop(0, 9, smooth1, None, unroll=True)

    def defect1(n, forces):
        for c in range(3):
            free = f1_out[c, n]
            d1_ref[c, n] = c1_out[c, n] - (free * forces[c] + (1.0 - free) * s1_out[c, n])

    sweep(lambda c, n: u1_ref[c, n], lambda n: m1_ref[n + 1], 0, 5, False, defect1)

    for n in range(2):
        x = 2 * n + 2
        for c in range(3):
            v2_ref[2 * c + n] = smooth_rows(d1_ref[c, x] + 0.5 * (d1_ref[c, x - 1] + d1_ref[c, x + 1]))
            v2_ref[6 + 2 * c + n] = f1_out[c, x]
    for n in range(3):
        v = m1_ref[2 * n + 1] + m1_ref[2 * n + 2]
        v2_ref[12 + n] = v + y_up(v)
    v2_ref[15] = jnp.zeros((16, 128), F32)

    def half2(first, count, matrix):
        v = v2_ref[first : first + count, pl.ds(0, 8, stride=2), :]
        return exact_dot(v.reshape(count * 8, 128), matrix).reshape(count, 8, 128)

    free2 = half2(6, 6, pick)
    rhs2 = half2(0, 6, restrict) * free2
    m2_ref[...] = 0.25 * half2(12, 4, pair)
    fields = [[m2_ref[1], m2_ref[2]]]
    fields += [[free2[2 * c], free2[2 * c + 1]] for c in range(3)]
    fields += [[rhs2[2 * c], rhs2[2 * c + 1]] for c in range(3)]
    valid = lanes_of((8, 128)) < 32
    inverse = []
    for n in range(2):
        total = corner_sum(m2_ref[n + 1] + m2_ref[n], plain_down)
        inverse.append(jnp.where(total > 0.0, (DAMPING / DIAG) / total, 0.0))
    fields.append(inverse)
    for f, pairs in enumerate(fields):
        row = None
        for n in range(2):
            v = jnp.where(valid, pairs[n], 0.0)
            for y in range(2):
                piece = v[2 + y : 3 + y]
                q = 2 * n + y
                piece = pltpu.roll(piece, 32 * q, 1) if q else piece
                row = piece if row is None else row + piece
        pack_out[f : f + 1, :] = row


def first_call(lo, own, hi):
    big = lambda *s: jax.ShapeDtypeStruct(s + (16, 128), F32)
    s24 = lambda *s: pltpu.VMEM(s + (24, 128), F32)
    return pl.pallas_call(
        first_kernel,
        out_shape=[big(12), big(3, 12), big(3, 12), big(3, 12), big(3, 12)]
        + [big(9), big(3, 9), big(3, 9), big(3, 9), big(3, 9), jax.ShapeDtypeStruct((8, 128), F32)],
        scratch_shapes=[s24(24), s24(24), s24(24)]
        + [s24(3, 24)] * 6
        + [
            pltpu.VMEM((64, 32, 128), F32),
            pltpu.VMEM((10, 16, 128), F32),
            pltpu.VMEM((3, 9, 16, 128), F32),
            pltpu.VMEM((3, 9, 16, 128), F32),
            pltpu.VMEM((16, 16, 128), F32),
            pltpu.VMEM((4, 8, 128), F32),
        ],
        compiler_params=PARAMS,
    )(lo, own, hi)


def second_kernel(lo_ref, own_ref, hi_ref, hi2_ref, l_out, s_out, w_out, pack_out, u_ref, d_ref, v_ref):
    peers = own_ref.shape[0]
    l_out[...] = jnp.zeros(l_out.shape, F32)
    valid = lanes_of((peers, 128)) < 32
    for ref, base, count in ((lo_ref, 0, 2), (own_ref, 2, 2), (hi_ref, 4, 2), (hi2_ref, 6, 1)):
        for f in range(8):
            rows = ref[:, f, :]
            for n in range(count):
                for y in range(2):
                    q = 2 * n + y
                    v = pltpu.roll(rows, 128 - 32 * q, 1) if q else rows
                    l_out[f, base + n, pl.ds(y, peers, stride=2), :] = jnp.where(valid, v, 0.0)

    def smooth(n, _):
        inverse = l_out[7, n]
        for c in range(3):
            w = scaled(l_out[1 + c, n], inverse)
            s = w * l_out[4 + c, n]
            w_out[c, n], s_out[c, n] = (w, s)
            u_ref[c, n] = l_out[1 + c, n] * s

    lax.fori_loop(0, 7, smooth, None, unroll=True)

    def defect(n, forces):
        for c in range(3):
            free = l_out[1 + c, n]
            d_ref[c, n] = l_out[4 + c, n] - (free * forces[c] + (1.0 - free) * s_out[c, n])

    sweep(lambda c, n: u_ref[c, n], lambda n: l_out[0, n], 0, 3, False, defect)
    for c in range(3):
        v_ref[c] = smooth_rows(d_ref[c, 2] + 0.5 * (d_ref[c, 1] + d_ref[c, 3]))
        v_ref[3 + c] = l_out[1 + c, 2]
    v = l_out[0, 2] + l_out[0, 3]
    v_ref[6] = v + y_up(v)

    def half(first, count, matrix):
        v = v_ref[first : first + count, pl.ds(0, 16, stride=2), :]
        return exact_dot(v.reshape(count * 16, 128), matrix).reshape(count, 16, 128)

    free = half(3, 3, square("pick", 16))
    rhs = half(0, 3, square("restrict", 16)) * free
    moduli = 0.25 * half(6, 1, square("pair", 16))
    shape = (8, 128)
    own_lane = (lanes_of(shape) // 16) == rows_of(shape)
    fields = []
    for v in (moduli[0], free[0], free[1], free[2], rhs[0], rhs[1], rhs[2]):
        fields.append(
            [
                jnp.sum(jnp.where(own_lane, v[8 * h : 8 * h + 8], 0.0), axis=0, keepdims=True)
                for h in range(2)
            ]
        )
    for t, v in enumerate(pack_rows(fields)):
        pack_out[:, 128 * t : 128 * t + 128] = v


def second_call(lo, own, hi, hi2):
    big = lambda *s: jax.ShapeDtypeStruct(s + (32, 128), F32)
    vmem = lambda *s: pltpu.VMEM(s + (32, 128), F32)
    return pl.pallas_call(
        second_kernel,
        out_shape=[big(8, 7), big(3, 7), big(3, 7), jax.ShapeDtypeStruct((1, 1408), F32)],
        scratch_shapes=[vmem(3, 7), vmem(3, 7), vmem(7)],
        compiler_params=PARAMS,
    )(lo, own, hi, hi2)


def pack_rows(fields):
    out = []
    low = lanes_of(fields[0][0].shape) < 64
    turn = lambda v: pltpu.roll(v, 64, 1)
    for k in range(0, 6, 2):
        (a0, a1), (b0, b1) = (fields[k], fields[k + 1])
        middle = turn(b0)
        out += [a0, jnp.where(low, a1, middle), jnp.where(low, middle, turn(b1))]
    return out + fields[6]


def unpack_rows(tiles):
    out = []
    low = lanes_of(tiles[0].shape) < 64
    turn = lambda v: pltpu.roll(v, 64, 1)
    for k in range(0, 9, 3):
        t0, t1, t2 = tiles[k : k + 3]
        r1, r2 = (turn(t1), turn(t2))
        out.append([t0, jnp.where(low, t1, 0.0)])
        out.append([jnp.where(low, r1, r2), jnp.where(low, r2, 0.0)])
    return out + [tiles[9:11]]


def coarse_solve(rows_ref):
    peers = rows_ref.shape[0]
    shape = (peers + 8, 256)

    fields = unpack_rows([rows_ref[:, 128 * t : 128 * t + 128] for t in range(11)])

    def field(f):
        v = jnp.concatenate(fields[f], axis=1)
        return jnp.concatenate([v, jnp.zeros((8, 256), F32)], axis=0)

    depth = lanes_of(shape) & 15
    z_up = lambda v: jnp.where(depth < 15, shift_up(v, 1), 0.0)
    z_down = lambda v: jnp.where(depth > 0, shift_down(v, 1), 0.0)
    side_up = lambda v: pltpu.roll(v, 240, 1)
    side_down = lambda v: pltpu.roll(v, 16, 1)
    moduli = field(0)
    free = [field(1 + c) for c in range(3)]
    resid = [field(4 + c) for c in range(3)]
    total = moduli + z_down(moduli)
    total = total + side_down(total)
    total = DIAG * (total + shift_down(total, 0))
    inverse = [1.0 / jnp.where(f > 0.0, total, 1.0) for f in free]

    def dot(a, b):
        return jnp.sum(a[0] * b[0] + a[1] * b[1] + a[2] * b[2], keepdims=True)

    def operator(v):
        low = [flat_modes(v[c] * free[c], z_up, side_up) for c in range(3)]
        high = [[shift_up(p, 0) for p in low[c]] for c in range(3)]
        own, up = element_modes(low, high, moduli)
        out = []
        for c in range(3):
            parts = [own[c][q] + shift_down(up[c][q], 0) for q in range(4)]
            forces = node_forces(parts, z_down, side_down)
            out.append(free[c] * forces + (1.0 - free[c]) * v[c])
        return out

    precond = [r * i for r, i in zip(resid, inverse)]
    direction = precond
    inner = dot(resid, precond)
    answer = None
    for step in range(COARSE_ITERS):
        image = operator(direction)
        alpha = inner / dot(direction, image)
        moved = [alpha * d for d in direction]
        answer = moved if answer is None else [s + m for s, m in zip(answer, moved)]
        if step + 1 < COARSE_ITERS:
            resid = [r - alpha * q for r, q in zip(resid, image)]
            precond = [r * i for r, i in zip(resid, inverse)]
            inner_new = dot(resid, precond)
            ratio = inner_new / inner
            direction = [z + ratio * d for z, d in zip(precond, direction)]
            inner = inner_new
    return answer


def third_kernel(
    rows_ref, l2_ref, s2_ref, w2_ref, m1_ref, f1_ref, c1_ref, s1_ref, w1_ref, m_ref, f_ref, r_ref, s_ref, w_ref,
    p_out, q_out, sum_out,
    a_ref, z3_ref, p2_ref, u2_ref, y2_ref, v2_ref, p1_ref, u1_ref, y1_ref, v1_ref, p0_ref, u0_ref, y0_ref,
):
    gx, gy = (lax.axis_index("gx"), lax.axis_index("gy"))
    peers = rows_ref.shape[0]
    answer = coarse_solve(rows_ref)
    for c in range(3):
        a_ref[c, 0:8, :] = jnp.zeros((8, 256), F32)
        a_ref[c, 8 : 16 + peers, :] = answer[c]

    spread3 = prolong_matrix(16)
    shape = (8, 128)
    own_lane = (lanes_of(shape) // 16) == rows_of(shape)
    for c in range(3):
        for i in range(4):
            row = a_ref[c, pl.ds(gx + 7 + i, 1), :]
            halves = [
                jnp.where(own_lane, jnp.broadcast_to(row[:, 128 * h : 128 * h + 128], shape), 0.0)
                for h in range(2)
            ]
            w = exact_dot(jnp.concatenate(halves, axis=0), spread3)
            z3_ref[i, pl.ds(0, 16, stride=2), :] = w
            z3_ref[i, pl.ds(1, 16, stride=2), :] = 0.5 * (w + y_up(w))
        for n in range(7):
            i = n // 2
            p = z3_ref[i] if n % 2 == 0 else 0.5 * (z3_ref[i] + z3_ref[i + 1])
            free = l2_ref[1 + c, n]
            s = s2_ref[c, n] + free * p
            y2_ref[c, n] = s
            u2_ref[c, n] = free * s

    v2_ref[...] = jnp.zeros(v2_ref.shape, F32)

    def level2(n, forces):
        for c in range(3):
            free, s = (l2_ref[1 + c, n], y2_ref[c, n])
            image = free * forces[c] + (1.0 - free) * s
            v2_ref[c, n - 1, 8:40, :] = s + w2_ref[c, n] * (l2_ref[4 + c, n] - image)

    sweep(lambda c, n: u2_ref[c, n], lambda n: l2_ref[0, n], 0, 5, False, level2)

    spread = prolong_matrix()
    for c in range(3):
        for i in range(5):
            w = exact_dot(v2_ref[c, i, pl.ds(2 * gy + 6, 16), :], spread)
            p1_ref[c, i, pl.ds(0, 8, stride=2), :] = w[0:8]
            p1_ref[c, i, pl.ds(1, 8, stride=2), :] = 0.5 * (w[0:8] + w[1:9])
        for n in range(9):
            i = n // 2
            p = p1_ref[c, i] if n % 2 == 0 else 0.5 * (p1_ref[c, i] + p1_ref[c, i + 1])
            free = f1_ref[c, n]
            s = s1_ref[c, n] + free * p
            y1_ref[c, n] = s
            u1_ref[c, n] = free * s

    def level1(n, forces):
        for c in range(3):
            free, s = (f1_ref[c, n], y1_ref[c, n])
            image = free * forces[c] + (1.0 - free) * s
            v1_ref[c, n - 1] = s + w1_ref[c, n] * (c1_ref[c, n] - image)

    sweep(lambda c, n: u1_ref[c, n], lambda n: m1_ref[n], 0, 7, False, level1)

    for c in range(3):
        w = exact_dot(v1_ref[c].reshape(7 * 16, 128), spread).reshape(7, 16, 128)
        for i in range(7):
            p0_ref[c, i, pl.ds(0, 8, stride=2), :] = w[i, 2:10]
            p0_ref[c, i, pl.ds(1, 8, stride=2), :] = 0.5 * (w[i, 2:10] + w[i, 3:11])
        for n in range(12):
            i = n // 2
            p = p0_ref[c, i] if n % 2 == 0 else 0.5 * (p0_ref[c, i] + p0_ref[c, i + 1])
            free = f_ref[c, n]
            s = s_ref[c, n] + free * p
            y0_ref[c, n] = s
            u0_ref[c, n] = free * s

    def level0(n, forces):
        for c in range(3):
            free, s = (f_ref[c, n], y0_ref[c, n])
            image = free * forces[c] + (1.0 - free) * s
            y0_ref[c, n] = s + w_ref[c, n] * (r_ref[c, n] - image)

    sweep(lambda c, n: u0_ref[c, n], lambda n: m_ref[n], 0, 10, True, level0)
    sum_out[...] = jnp.zeros((8, 128), F32)

    def last(n, forces):
        one = two = None
        for c in range(3):
            free, v = (f_ref[c, n], y0_ref[c, n])
            image = (free * forces[c] + (1.0 - free) * v)[4:12]
            v = v[4:12]
            p_out[c, n - 2] = v
            q_out[c, n - 2] = image
            a, b = (r_ref[c, n, 4:12, :] * v, v * image)
            one, two = ((a, b) if one is None else (one + a, two + b))
        sum_out[0:1, :] = sum_out[0:1, :] + jnp.sum(one, axis=0, keepdims=True)
        sum_out[1:2, :] = sum_out[1:2, :] + jnp.sum(two, axis=0, keepdims=True)

    sweep(lambda c, n: f_ref[c, n] * y0_ref[c, n], lambda n: m_ref[n], 1, 9, True, last)
    lane = lanes_of((1, 128))
    one = jnp.sum(sum_out[0:1, :], keepdims=True)
    two = jnp.sum(sum_out[1:2, :], keepdims=True)
    sum_out[0:1, :] = jnp.where(lane == 0, one, jnp.where(lane == 1, two, 0.0))


def third_call(rows, level2, level1, level0):
    own = jax.ShapeDtypeStruct((3, 8, 8, 128), F32)
    peers = rows.shape[0]
    return pl.pallas_call(
        third_kernel,
        out_shape=[own, own, jax.ShapeDtypeStruct((8, 128), F32)],
        scratch_shapes=[
            pltpu.VMEM((3, peers + 16, 256), F32),
            pltpu.VMEM((4, 32, 128), F32),
            pltpu.VMEM((1, 8, 128), F32),
            pltpu.VMEM((3, 7, 32, 128), F32),
            pltpu.VMEM((3, 7, 32, 128), F32),
            pltpu.VMEM((3, 5, 48, 128), F32),
            pltpu.VMEM((3, 5, 16, 128), F32),
            pltpu.VMEM((3, 9, 16, 128), F32),
            pltpu.VMEM((3, 9, 16, 128), F32),
            pltpu.VMEM((3, 7, 16, 128), F32),
            pltpu.VMEM((3, 7, 16, 128), F32),
            pltpu.VMEM((3, 12, 16, 128), F32),
            pltpu.VMEM((3, 12, 16, 128), F32),
        ],
        compiler_params=PARAMS,
    )(rows, *level2, *level1, *level0)


def pack_kernel(density_ref, solid_ref, void_ref, fixed_ref, residual_ref, out_ref):
    out_ref[0] = density_ref[...]
    out_ref[1] = solid_ref[...].astype(F32)
    out_ref[2] = void_ref[...].astype(F32)
    out_ref[3:6] = 1.0 - fixed_ref[...].astype(F32)
    out_ref[6:9] = residual_ref[...]


def last_kernel(sums_ref, precond_ref, image_ref, residual_ref, update_ref, next_ref):
    total = jnp.sum(sums_ref[...], axis=0, keepdims=True)
    alpha = total[:, 0:1] / total[:, 1:2]
    for c in range(3):
        update_ref[c] = alpha * precond_ref[c]
        next_ref[c] = residual_ref[c] - alpha * image_ref[c]


def from_peer(value, axis, step):
    peers = lax.axis_size(axis)
    return lax.ppermute(value, axis, [(i + step, i) for i in range(peers) if 0 <= i + step < peers])


def spread_all(row, axis):
    peers = lax.axis_size(axis)
    return lax.all_to_all(
        jnp.broadcast_to(row[None], (peers,) + row.shape), axis, 0, 0, tiled=True
    )


def on_device(density, solid, void, fixed, residual):
    packed = pl.pallas_call(
        pack_kernel,
        out_shape=jax.ShapeDtypeStruct((9,) + density.shape, F32),
        compiler_params=PARAMS,
    )(density, solid, void, fixed, residual)
    own = jnp.concatenate([from_peer(packed, "gy", -1), packed, from_peer(packed, "gy", 1)], axis=2)
    first = first_call(from_peer(own, "gx", -1), own, from_peer(own, "gx", 1))
    level0, level1, piece = (first[0:5], first[5:10], first[10])
    columns = spread_all(piece, "gy")
    second = second_call(
        from_peer(columns, "gx", -1), columns, from_peer(columns, "gx", 1), from_peer(columns, "gx", 2)
    )
    rows = spread_all(second[3].reshape(-1), "gx")
    precond, image, sums = third_call(rows, second[0:3], level1, level0)
    sums = jnp.sum(spread_all(sums[0], "gx"), axis=0)
    block = jax.ShapeDtypeStruct(residual.shape, F32)
    return tuple(
        pl.pallas_call(last_kernel, out_shape=[block, block], compiler_params=PARAMS)(
            spread_all(sums, "gy"), precond, image, residual
        )
    )


def solution(mesh):
    return jax.shard_map(
        on_device,
        mesh=mesh,
        in_specs=(
            P("gx", "gy", None),
            P("gx", "gy", None),
            P("gx", "gy", None),
            P(None, "gx", "gy", None),
            P(None, "gx", "gy", None),
        ),
        out_specs=(P(None, "gx", "gy", None), P(None, "gx", "gy", None)),
        check_vma=False,
    )
```

```python
import math

import jax
import jax.numpy as jnp
import numpy as np
from jax import lax
from jax.experimental import pallas as pl
from jax.experimental.pallas import tpu as pltpu
from jax.sharding import PartitionSpec as P

COARSE_ITERS = 4
DAMPING = 0.6
VOID_MODULUS = 0.001
F32 = jnp.float32
PARAMS = pltpu.CompilerParams(vmem_limit_bytes=16 * 1024 * 1024)


def corner_list():
    return [(a, b, c) for a in (0, 1) for b in (0, 1) for c in (0, 1)]


def element_stiffness():
    poisson = 0.3
    lame_first = poisson / ((1.0 + poisson) * (1.0 - 2.0 * poisson))
    shear = 0.5 / (1.0 + poisson)
    elastic = np.zeros((6, 6))
    elastic[:3, :3] = lame_first
    for i in range(3):
        elastic[i, i] += 2.0 * shear
        elastic[i + 3, i + 3] = shear
    points = [0.5 - 0.5 / math.sqrt(3.0), 0.5 + 0.5 / math.sqrt(3.0)]
    gauss = [(u, v, w) for u in points for v in points for w in points]
    stiffness = np.zeros((24, 24))
    for coord in gauss:
        strain = np.zeros((6, 24))
        for k, corner in enumerate(corner_list()):
            values = [coord[d] if corner[d] else 1.0 - coord[d] for d in range(3)]
            slopes = [2.0 * corner[d] - 1.0 for d in range(3)]
            grad_x = slopes[0] * values[1] * values[2]
            grad_y = values[0] * slopes[1] * values[2]
            grad_z = values[0] * values[1] * slopes[2]
            strain[0, 3 * k] = grad_x
            strain[1, 3 * k + 1] = grad_y
            strain[2, 3 * k + 2] = grad_z
            strain[3, 3 * k] = grad_y
            strain[3, 3 * k + 1] = grad_x
            strain[4, 3 * k + 1] = grad_z
            strain[4, 3 * k + 2] = grad_y
            strain[5, 3 * k] = grad_z
            strain[5, 3 * k + 2] = grad_x
        stiffness += strain.T @ elastic @ strain / 8.0
    return stiffness


def mode_table():
    corners = corner_list()
    signs = np.array(
        [[math.prod(2 * c[d] - 1 if m[d] else 1 for d in range(3)) for c in corners] for m in corners],
        float,
    )
    wide = np.kron(signs, np.eye(3))
    table = wide @ element_stiffness() @ wide.T / 64.0
    rows = {}
    for i in range(24):
        row = [
            (corners[j // 3], j % 3, float(table[i, j]))
            for j in range(24)
            if abs(table[i, j]) > 1e-12
        ]
        if row:
            rows[(corners[i // 3], i % 3)] = row
    return rows


MODES = mode_table()
DIAG = float(element_stiffness()[0, 0])
PAIRS = ((0, 0), (1, 0), (0, 1), (1, 1))


def flat_modes(field, z_up, y_up):
    after = z_up(field)
    out = {}
    for k, part in ((0, field + after), (1, after - field)):
        after = y_up(part)
        out[(0, k)] = part + after
        out[(1, k)] = after - part
    return [out[p] for p in PAIRS]


def element_modes(low, high, moduli):
    values = {}
    for c in range(3):
        for q, (j, k) in enumerate(PAIRS):
            if (j, k) != (0, 0):
                values[((0, j, k), c)] = low[c][q] + high[c][q]
            values[((1, j, k), c)] = high[c][q] - low[c][q]
    forces = {}
    for key, row in MODES.items():
        total = None
        for mode, c, weight in row:
            term = weight * values[(mode, c)]
            total = term if total is None else total + term
        forces[key] = total * moduli
    to_low, to_high = [], []
    for c in range(3):
        a, b = [], []
        for j, k in PAIRS:
            slope = forces[((1, j, k), c)]
            mean = forces.get(((0, j, k), c))
            a.append(-slope if mean is None else mean - slope)
            b.append(slope if mean is None else mean + slope)
        to_low.append(a)
        to_high.append(b)
    return to_low, to_high


def node_forces(parts, z_down, y_down):
    out = []
    for k in (0, 1):
        mean, slope = (parts[PAIRS.index((0, k))], parts[PAIRS.index((1, k))])
        out.append((mean - slope) + y_down(mean + slope))
    return (out[0] - out[1]) + z_down(out[0] + out[1])


def shift_up(value, axis):
    return pltpu.roll(value, value.shape[axis] - 1, axis)


def shift_down(value, axis):
    return pltpu.roll(value, 1, axis)


def lanes_of(shape):
    return lax.broadcasted_iota(jnp.int32, shape, len(shape) - 1)


def rows_of(shape):
    return lax.broadcasted_iota(jnp.int32, shape, 0)


def z_shifts(full):
    def up(v):
        s = shift_up(v, 1)
        return jnp.where(lanes_of(v.shape) < v.shape[1] - 1, s, 0.0) if full else s

    def down(v):
        s = shift_down(v, 1)
        return jnp.where(lanes_of(v.shape) > 0, s, 0.0) if full else s

    return up, down


def y_up(v):
    return shift_up(v, 0)


def y_down(v):
    return shift_down(v, 0)


def sweep(load, moduli, first, last, full, emit, unroll=True):
    z_up, z_down = z_shifts(full)

    def modes(x):
        return [flat_modes(load(c, x), z_up, y_up) for c in range(3)]

    high = modes(first + 1)
    _, up = element_modes(modes(first), high, moduli(first))

    def body(x, carry):
        low, before = carry
        high = modes(x + 1)
        own, up = element_modes(low, high, moduli(x))
        forces = [
            node_forces([own[c][q] + before[c][q] for q in range(4)], z_down, y_down)
            for c in range(3)
        ]
        emit(x, forces)
        return (high, up)

    lax.fori_loop(first + 1, last + 1, body, (high, up), unroll=unroll)


def exact_dot(a, b):
    return jnp.dot(a, b, precision=lax.Precision.HIGHEST, preferred_element_type=F32)


def tent(shape, fine, coarse):
    gap = jnp.abs(fine - 2 * coarse)
    return jnp.where(gap == 0, 1.0, jnp.where(gap == 1, 0.5, 0.0)).astype(F32)


def square(kind, period=128):
    shape = (128, 128)
    fine, coarse = (rows_of(shape), lax.rem(lanes_of(shape), period))
    if kind == "restrict":
        return tent(shape, fine, coarse)
    if kind == "pick":
        return jnp.where(fine == 2 * coarse, 1.0, 0.0).astype(F32)
    return jnp.where((fine == 2 * coarse) | (fine == 2 * coarse + 1), 1.0, 0.0).astype(F32)


def prolong_matrix(period=128):
    shape = (128, 128)
    return tent(shape, lanes_of(shape), lax.rem(rows_of(shape), period))


def smooth_rows(v):
    return v + 0.5 * (y_up(v) + y_down(v))


def corner_sum(v, z_down):
    v = v + z_down(v)
    return v + y_down(v)


def scaled(free, inverse):
    return jnp.where(free > 0.0, inverse, DAMPING)


def first_kernel(
    lo_ref, own_ref, hi_ref,
    m_out, i_out, f_out, r_out, m1_out, i1_out, f1_out, c1_out, pack_out,
    t_ref, b_ref, m_ref, i_ref, f_ref, r_ref, s_ref, u_ref, d_ref, v_ref, m1_ref, s1_ref, u1_ref, d1_ref, v2_ref,
):
    pieces = (lo_ref, own_ref, hi_ref)
    slab = (24, 128)
    z_up, z_down = z_shifts(True)
    gx, gy = (lax.axis_index("gx"), lax.axis_index("gy"))
    nodes_x, nodes_y = (8 * lax.axis_size("gx"), 8 * lax.axis_size("gy"))
    w0, w1, w2, w3 = [2.0 - math.sqrt(n) for n in range(4)]

    def each(first, last, body):
        for p, ref in enumerate(pieces):
            a, b = (max(first, 8 * p), min(last, 8 * p + 7))
            if a <= b:
                lax.fori_loop(a - 8 * p, b - 8 * p + 1, lambda i, _, ref=ref, p=p: body(8 * p + i, ref, i), None, unroll=True)

    def gather_flat(x, ref, i):
        own = ref[0, i]
        ring = z_up(own) + z_down(own)
        c1 = y_up(own) + y_down(own) + ring
        c2 = y_up(ring) + y_down(ring)
        b_ref[x] = w0 * own + w1 * c1 + w2 * c2
        t_ref[x] = w1 * own + w2 * c1 + w3 * c2

    each(0, 23, gather_flat)
    row_at = rows_of(slab) + (8 * gy - 8)
    lane_at = lanes_of(slab)
    inside = ((row_at >= 0) & (row_at < nodes_y)).astype(F32)
    ring_y = (row_at > 0).astype(F32) + (row_at < nodes_y - 1).astype(F32)
    ring_z = (lane_at > 0).astype(F32) + (lane_at < 127).astype(F32)
    plain = w0 + w1 * (ring_y + ring_z) + w2 * ring_y * ring_z
    beside = w1 + w2 * (ring_y + ring_z) + w3 * ring_y * ring_z
    inverse_two, inverse_one = (1.0 / (plain + 2.0 * beside), 1.0 / (plain + beside))

    def moduli_of(x, ref, i):
        at = 8 * gx - 8 + x
        edge = (at == 0) | (at == nodes_x - 1)
        inverse = jnp.where(edge, inverse_one, inverse_two)
        filtered = (b_ref[x] + (t_ref[x - 1] + t_ref[x + 1])) * inverse
        solid, void = (ref[1, i], ref[2, i])
        physical = (1.0 - void) * (solid + (1.0 - solid) * filtered)
        value = VOID_MODULUS + (1.0 - VOID_MODULUS) * (physical * physical * physical)
        mask = jnp.where((at >= 0) & (at < nodes_x), inside, 0.0)
        m_ref[x] = value * mask

    each(1, 22, moduli_of)

    def smooth_of(x, ref, i):
        total = corner_sum(m_ref[x] + m_ref[x - 1], z_down)
        inverse = (DAMPING / DIAG) / total
        i_ref[x] = inverse
        for c in range(3):
            free, r = (ref[3 + c, i], ref[6 + c, i])
            s = scaled(free, inverse) * r
            f_ref[c, x], r_ref[c, x], s_ref[c, x] = (free, r, s)
            u_ref[c, x] = free * s

    each(2, 22, smooth_of)

    def defect_of(x, forces):
        for c in range(3):
            free = f_ref[c, x]
            d_ref[c, x] = r_ref[c, x] - (free * forces[c] + (1.0 - free) * s_ref[c, x])

    sweep(lambda c, x: u_ref[c, x], lambda x: m_ref[x], 2, 21, True, defect_of)

    def keep(x, _):
        m_out[x] = m_ref[x + 6, 4:20, :]
        i_out[x] = i_ref[x + 6, 4:20, :]
        for c in range(3):
            f_out[c, x] = f_ref[c, x + 6, 4:20, :]
            r_out[c, x] = r_ref[c, x + 6, 4:20, :]

    lax.fori_loop(0, 12, keep, None, unroll=2)

    v_ref[:, 24:32, :] = jnp.zeros((64, 8, 128), F32)

    def to_coarse(n, _):
        x = 2 * n + 4
        for c in range(3):
            v = d_ref[c, x] + 0.5 * (d_ref[c, x - 1] + d_ref[c, x + 1])
            v_ref[9 * c + n, 0:24, :] = smooth_rows(v)
            v_ref[27 + 9 * c + n, 0:24, :] = f_ref[c, x]

    lax.fori_loop(0, 9, to_coarse, None, unroll=3)

    def to_coarse_moduli(n, _):
        x = 2 * n + 2
        v = m_ref[x] + m_ref[x + 1]
        v_ref[54 + n, 0:24, :] = v + y_up(v)

    lax.fori_loop(0, 10, to_coarse_moduli, None, unroll=5)

    def half(first, count, matrix):
        v = v_ref[first : first + count, pl.ds(0, 16, stride=2), :]
        return exact_dot(v.reshape(count * 16, 128), matrix).reshape(count, 16, 128)

    restrict, pick, pair = (square("restrict"), square("pick"), square("pair"))
    m1_ref[...] = 0.25 * half(54, 10, pair)
    m1_out[...] = m1_ref[1:10]
    for c in range(3):
        f1_out[c] = half(27 + 9 * c, 9, pick)
        c1_out[c] = f1_out[c] * half(9 * c, 9, restrict)
    _, plain_down = z_shifts(False)

    def smooth1(n, _):
        inverse = (DAMPING / DIAG) / corner_sum(m1_ref[n + 1] + m1_ref[n], plain_down)
        i1_out[n] = inverse
        for c in range(3):
            s = scaled(f1_out[c, n], inverse) * c1_out[c, n]
            s1_ref[c, n] = s
            u1_ref[c, n] = f1_out[c, n] * s

    lax.fori_loop(0, 9, smooth1, None, unroll=True)

    def defect1(n, forces):
        for c in range(3):
            free = f1_out[c, n]
            d1_ref[c, n] = c1_out[c, n] - (free * forces[c] + (1.0 - free) * s1_ref[c, n])

    sweep(lambda c, n: u1_ref[c, n], lambda n: m1_ref[n + 1], 0, 7, False, defect1)

    for n in range(3):
        x = 2 * n + 2
        for c in range(3):
            v2_ref[3 * c + n] = smooth_rows(d1_ref[c, x] + 0.5 * (d1_ref[c, x - 1] + d1_ref[c, x + 1]))
            v2_ref[9 + 3 * c + n] = f1_out[c, x]
    for n in range(4):
        v = m1_ref[2 * n + 1] + m1_ref[2 * n + 2]
        v2_ref[18 + n] = v + y_up(v)

    def half2(first, count, matrix):
        v = v2_ref[first : first + count, pl.ds(0, 8, stride=2), :]
        return exact_dot(v.reshape(count * 8, 128), matrix).reshape(count, 8, 128)

    free2 = half2(9, 9, pick)
    rhs2 = half2(0, 9, restrict) * free2
    moduli2 = 0.25 * half2(18, 4, pair)
    fields = [[moduli2[1 + n] for n in range(3)]]
    fields += [[free2[3 * c + n] for n in range(3)] for c in range(3)]
    fields += [[rhs2[3 * c + n] for n in range(3)] for c in range(3)]
    valid = lanes_of((8, 128)) < 32
    inverse = []
    for n in range(3):
        total = corner_sum(moduli2[n + 1] + moduli2[n], plain_down)
        inverse.append(jnp.where(total > 0.0, (DAMPING / DIAG) / total, 0.0))
    fields.append(inverse)
    for f, slabs in enumerate(fields):
        rows = [None, None]
        for n in range(3):
            v = jnp.where(valid, slabs[n], 0.0)
            for y in range(2):
                piece = v[2 + y : 3 + y]
                q = 2 * (n % 2) + y
                piece = pltpu.roll(piece, 32 * q, 1) if q else piece
                rows[n // 2] = piece if rows[n // 2] is None else rows[n // 2] + piece
        pack_out[f : f + 1, 0:128] = rows[0]
        pack_out[f : f + 1, 128:256] = rows[1]


def first_call(lo, own, hi):
    big = lambda *s: jax.ShapeDtypeStruct(s + (16, 128), F32)
    s24 = lambda *s: pltpu.VMEM(s + (24, 128), F32)
    return pl.pallas_call(
        first_kernel,
        out_shape=[big(12), big(12), big(3, 12), big(3, 12)]
        + [big(9), big(9), big(3, 9), big(3, 9), jax.ShapeDtypeStruct((8, 256), F32)],
        scratch_shapes=[s24(24)] * 4
        + [s24(3, 24)] * 5
        + [
            pltpu.VMEM((64, 32, 128), F32),
            pltpu.VMEM((10, 16, 128), F32),
            pltpu.VMEM((3, 9, 16, 128), F32),
            pltpu.VMEM((3, 9, 16, 128), F32),
            pltpu.VMEM((3, 9, 16, 128), F32),
            pltpu.VMEM((22, 16, 128), F32),
        ],
        compiler_params=PARAMS,
    )(lo, own, hi)


def second_kernel(lo_ref, own_ref, hi_ref, l_out, pack_out, s_ref, u_ref, d_ref, v_ref):
    peers = own_ref.shape[0]
    l_out[...] = jnp.zeros(l_out.shape, F32)
    valid = lanes_of((peers, 128)) < 32
    for ref, base, count in ((lo_ref, 0, 2), (own_ref, 2, 2), (hi_ref, 4, 3)):
        for f in range(8):
            for h in range((count + 1) // 2):
                rows = ref[:, f, 128 * h : 128 * h + 128]
                for n in range(2 * h, min(2 * h + 2, count)):
                    for y in range(2):
                        q = 2 * (n % 2) + y
                        v = pltpu.roll(rows, 128 - 32 * q, 1) if q else rows
                        l_out[f, base + n, pl.ds(y, peers, stride=2), :] = jnp.where(valid, v, 0.0)

    def smooth(n, _):
        inverse = l_out[7, n]
        for c in range(3):
            s = scaled(l_out[1 + c, n], inverse) * l_out[4 + c, n]
            s_ref[c, n] = s
            u_ref[c, n] = l_out[1 + c, n] * s

    lax.fori_loop(0, 5, smooth, None, unroll=True)

    def defect(n, forces):
        for c in range(3):
            free = l_out[1 + c, n]
            d_ref[c, n] = l_out[4 + c, n] - (free * forces[c] + (1.0 - free) * s_ref[c, n])

    sweep(lambda c, n: u_ref[c, n], lambda n: l_out[0, n], 0, 3, False, defect)
    for c in range(3):
        v_ref[c] = smooth_rows(d_ref[c, 2] + 0.5 * (d_ref[c, 1] + d_ref[c, 3]))
        v_ref[3 + c] = l_out[1 + c, 2]
    v = l_out[0, 2] + l_out[0, 3]
    v_ref[6] = v + y_up(v)

    def half(first, count, matrix):
        v = v_ref[first : first + count, pl.ds(0, 16, stride=2), :]
        return exact_dot(v.reshape(count * 16, 128), matrix).reshape(count, 16, 128)

    free = half(3, 3, square("pick", 16))
    rhs = half(0, 3, square("restrict", 16)) * free
    moduli = 0.25 * half(6, 1, square("pair", 16))
    shape = (8, 128)
    own_lane = (lanes_of(shape) // 16) == rows_of(shape)
    fields = []
    for v in (moduli[0], free[0], free[1], free[2], rhs[0], rhs[1], rhs[2]):
        fields.append(
            [
                jnp.sum(jnp.where(own_lane, v[8 * h : 8 * h + 8], 0.0), axis=0, keepdims=True)
                for h in range(2)
            ]
        )
    for t, v in enumerate(pack_rows(fields)):
        pack_out[:, 128 * t : 128 * t + 128] = v


def second_call(lo, own, hi):
    big = lambda *s: jax.ShapeDtypeStruct(s + (32, 128), F32)
    vmem = lambda *s: pltpu.VMEM(s + (32, 128), F32)
    return pl.pallas_call(
        second_kernel,
        out_shape=[big(8, 7), jax.ShapeDtypeStruct((1, 1408), F32)],
        scratch_shapes=[vmem(3, 5), vmem(3, 5), vmem(3, 4), vmem(7)],
        compiler_params=PARAMS,
    )(lo, own, hi)


def pack_rows(fields):
    out = []
    low = lanes_of(fields[0][0].shape) < 64
    turn = lambda v: pltpu.roll(v, 64, 1)
    for k in range(0, 6, 2):
        (a0, a1), (b0, b1) = (fields[k], fields[k + 1])
        middle = turn(b0)
        out += [a0, jnp.where(low, a1, middle), jnp.where(low, middle, turn(b1))]
    return out + fields[6]


def unpack_rows(tiles):
    out = []
    low = lanes_of(tiles[0].shape) < 64
    turn = lambda v: pltpu.roll(v, 64, 1)
    for k in range(0, 9, 3):
        t0, t1, t2 = tiles[k : k + 3]
        r1, r2 = (turn(t1), turn(t2))
        out.append([t0, jnp.where(low, t1, 0.0)])
        out.append([jnp.where(low, r1, r2), jnp.where(low, r2, 0.0)])
    return out + [tiles[9:11]]


def coarse_solve(rows_ref):
    peers = rows_ref.shape[0]
    shape = (peers + 8, 256)

    fields = unpack_rows([rows_ref[:, 128 * t : 128 * t + 128] for t in range(11)])

    def field(f):
        v = jnp.concatenate(fields[f], axis=1)
        return jnp.concatenate([v, jnp.zeros((8, 256), F32)], axis=0)

    depth = lanes_of(shape) & 15
    z_up = lambda v: jnp.where(depth < 15, shift_up(v, 1), 0.0)
    z_down = lambda v: jnp.where(depth > 0, shift_down(v, 1), 0.0)
    side_up = lambda v: pltpu.roll(v, 240, 1)
    side_down = lambda v: pltpu.roll(v, 16, 1)
    moduli = field(0)
    free = [field(1 + c) for c in range(3)]
    resid = [field(4 + c) for c in range(3)]
    total = moduli + z_down(moduli)
    total = total + side_down(total)
    total = DIAG * (total + shift_down(total, 0))
    inverse = [1.0 / jnp.where(f > 0.0, total, 1.0) for f in free]

    def dot(a, b):
        return jnp.sum(a[0] * b[0] + a[1] * b[1] + a[2] * b[2], keepdims=True)

    def operator(v):
        low = [flat_modes(v[c] * free[c], z_up, side_up) for c in range(3)]
        high = [[shift_up(p, 0) for p in low[c]] for c in range(3)]
        own, up = element_modes(low, high, moduli)
        out = []
        for c in range(3):
            parts = [own[c][q] + shift_down(up[c][q], 0) for q in range(4)]
            forces = node_forces(parts, z_down, side_down)
            out.append(free[c] * forces + (1.0 - free[c]) * v[c])
        return out

    precond = [r * i for r, i in zip(resid, inverse)]
    direction = precond
    inner = dot(resid, precond)
    answer = None
    for step in range(COARSE_ITERS):
        image = operator(direction)
        alpha = inner / dot(direction, image)
        moved = [alpha * d for d in direction]
        answer = moved if answer is None else [s + m for s, m in zip(answer, moved)]
        if step + 1 < COARSE_ITERS:
            resid = [r - alpha * q for r, q in zip(resid, image)]
            precond = [r * i for r, i in zip(resid, inverse)]
            inner_new = dot(resid, precond)
            ratio = inner_new / inner
            direction = [z + ratio * d for z, d in zip(precond, direction)]
            inner = inner_new
    return answer


def third_kernel(
    rows_ref, l2_ref, m1_ref, i1_ref, f1_ref, c1_ref, m_ref, i_ref, f_ref, r_ref,
    p_out, q_out, sum_out,
    a_ref, z3_ref, u2_ref, y2_ref, v2_ref, p1_ref, u1_ref, y1_ref, v1_ref, p0_ref, u0_ref, y0_ref,
):
    gx, gy = (lax.axis_index("gx"), lax.axis_index("gy"))
    peers = rows_ref.shape[0]
    answer = coarse_solve(rows_ref)
    for c in range(3):
        a_ref[c, 0:8, :] = jnp.zeros((8, 256), F32)
        a_ref[c, 8 : 16 + peers, :] = answer[c]

    spread3 = prolong_matrix(16)
    shape = (8, 128)
    own_lane = (lanes_of(shape) // 16) == rows_of(shape)
    for c in range(3):
        for i in range(4):
            row = a_ref[c, pl.ds(gx + 7 + i, 1), :]
            halves = [
                jnp.where(own_lane, jnp.broadcast_to(row[:, 128 * h : 128 * h + 128], shape), 0.0)
                for h in range(2)
            ]
            w = exact_dot(jnp.concatenate(halves, axis=0), spread3)
            z3_ref[i, pl.ds(0, 16, stride=2), :] = w
            z3_ref[i, pl.ds(1, 16, stride=2), :] = 0.5 * (w + y_up(w))
        for n in range(7):
            i = n // 2
            p = z3_ref[i] if n % 2 == 0 else 0.5 * (z3_ref[i] + z3_ref[i + 1])
            free = l2_ref[1 + c, n]
            s = scaled(free, l2_ref[7, n]) * l2_ref[4 + c, n] + free * p
            y2_ref[c, n] = s
            u2_ref[c, n] = free * s

    v2_ref[...] = jnp.zeros(v2_ref.shape, F32)

    def level2(n, forces):
        for c in range(3):
            free, s = (l2_ref[1 + c, n], y2_ref[c, n])
            image = free * forces[c] + (1.0 - free) * s
            v2_ref[c, n - 1, 8:40, :] = s + scaled(free, l2_ref[7, n]) * (l2_ref[4 + c, n] - image)

    sweep(lambda c, n: u2_ref[c, n], lambda n: l2_ref[0, n], 0, 5, False, level2)

    spread = prolong_matrix()
    for c in range(3):
        for i in range(5):
            w = exact_dot(v2_ref[c, i, pl.ds(2 * gy + 6, 16), :], spread)
            p1_ref[c, i, pl.ds(0, 8, stride=2), :] = w[0:8]
            p1_ref[c, i, pl.ds(1, 8, stride=2), :] = 0.5 * (w[0:8] + w[1:9])
        for n in range(9):
            i = n // 2
            p = p1_ref[c, i] if n % 2 == 0 else 0.5 * (p1_ref[c, i] + p1_ref[c, i + 1])
            free = f1_ref[c, n]
            s = scaled(free, i1_ref[n]) * c1_ref[c, n] + free * p
            y1_ref[c, n] = s
            u1_ref[c, n] = free * s

    def level1(n, forces):
        for c in range(3):
            free, s = (f1_ref[c, n], y1_ref[c, n])
            image = free * forces[c] + (1.0 - free) * s
            v1_ref[c, n - 1] = s + scaled(free, i1_ref[n]) * (c1_ref[c, n] - image)

    sweep(lambda c, n: u1_ref[c, n], lambda n: m1_ref[n], 0, 7, False, level1)

    for c in range(3):
        w = exact_dot(v1_ref[c].reshape(7 * 16, 128), spread).reshape(7, 16, 128)
        for i in range(7):
            p0_ref[c, i, pl.ds(0, 8, stride=2), :] = w[i, 2:10]
            p0_ref[c, i, pl.ds(1, 8, stride=2), :] = 0.5 * (w[i, 2:10] + w[i, 3:11])
        for n in range(12):
            i = n // 2
            p = p0_ref[c, i] if n % 2 == 0 else 0.5 * (p0_ref[c, i] + p0_ref[c, i + 1])
            free = f_ref[c, n]
            s = scaled(free, i_ref[n]) * r_ref[c, n] + free * p
            y0_ref[c, n] = s
            u0_ref[c, n] = free * s

    def level0(n, forces):
        for c in range(3):
            free, s = (f_ref[c, n], y0_ref[c, n])
            image = free * forces[c] + (1.0 - free) * s
            y0_ref[c, n] = s + scaled(free, i_ref[n]) * (r_ref[c, n] - image)

    sweep(lambda c, n: u0_ref[c, n], lambda n: m_ref[n], 0, 10, True, level0)
    sum_out[...] = jnp.zeros((8, 128), F32)

    def last(n, forces):
        one = two = None
        for c in range(3):
            free, v = (f_ref[c, n], y0_ref[c, n])
            image = (free * forces[c] + (1.0 - free) * v)[4:12]
            v = v[4:12]
            p_out[c, n - 2] = v
            q_out[c, n - 2] = image
            a, b = (r_ref[c, n, 4:12, :] * v, v * image)
            one, two = ((a, b) if one is None else (one + a, two + b))
        sum_out[0:1, :] = sum_out[0:1, :] + jnp.sum(one, axis=0, keepdims=True)
        sum_out[1:2, :] = sum_out[1:2, :] + jnp.sum(two, axis=0, keepdims=True)

    sweep(lambda c, n: f_ref[c, n] * y0_ref[c, n], lambda n: m_ref[n], 1, 9, True, last)
    lane = lanes_of((1, 128))
    one = jnp.sum(sum_out[0:1, :], keepdims=True)
    two = jnp.sum(sum_out[1:2, :], keepdims=True)
    sum_out[0:1, :] = jnp.where(lane == 0, one, jnp.where(lane == 1, two, 0.0))


def third_call(rows, level2, level1, level0):
    own = jax.ShapeDtypeStruct((3, 8, 8, 128), F32)
    peers = rows.shape[0]
    return pl.pallas_call(
        third_kernel,
        out_shape=[own, own, jax.ShapeDtypeStruct((8, 128), F32)],
        scratch_shapes=[
            pltpu.VMEM((3, peers + 16, 256), F32),
            pltpu.VMEM((4, 32, 128), F32),
            pltpu.VMEM((3, 7, 32, 128), F32),
            pltpu.VMEM((3, 7, 32, 128), F32),
            pltpu.VMEM((3, 5, 48, 128), F32),
            pltpu.VMEM((3, 5, 16, 128), F32),
            pltpu.VMEM((3, 9, 16, 128), F32),
            pltpu.VMEM((3, 9, 16, 128), F32),
            pltpu.VMEM((3, 7, 16, 128), F32),
            pltpu.VMEM((3, 7, 16, 128), F32),
            pltpu.VMEM((3, 12, 16, 128), F32),
            pltpu.VMEM((3, 12, 16, 128), F32),
        ],
        compiler_params=PARAMS,
    )(rows, level2, *level1, *level0)


def pack_kernel(density_ref, solid_ref, void_ref, fixed_ref, residual_ref, out_ref, flags_ref, fixed_to, sems):
    copies = [
        pltpu.make_async_copy(solid_ref, flags_ref.at[0], sems.at[0]),
        pltpu.make_async_copy(void_ref, flags_ref.at[1], sems.at[1]),
        pltpu.make_async_copy(fixed_ref, fixed_to, sems.at[2]),
        pltpu.make_async_copy(density_ref, out_ref.at[0], sems.at[3]),
        pltpu.make_async_copy(residual_ref, out_ref.at[pl.ds(6, 3)], sems.at[4]),
    ]
    for copy in copies:
        copy.start()
    copies[0].wait()
    out_ref[1] = flags_ref[0].astype(F32)
    copies[1].wait()
    out_ref[2] = flags_ref[1].astype(F32)
    copies[2].wait()
    out_ref[3:6] = 1.0 - fixed_to[...].astype(F32)
    copies[3].wait()
    copies[4].wait()


def last_kernel(sums_ref, precond_ref, image_ref, packed_ref, update_ref, next_ref):
    total = jnp.sum(sums_ref[...], axis=0, keepdims=True)
    alpha = total[:, 0:1] / total[:, 1:2]
    for c in range(3):
        update_ref[c] = alpha * precond_ref[c]
        next_ref[c] = packed_ref[6 + c] - alpha * image_ref[c]


def from_peer(value, axis, step):
    peers = lax.axis_size(axis)
    return lax.ppermute(value, axis, [(i + step, i) for i in range(peers) if 0 <= i + step < peers])


def spread_all(row, axis):
    peers = lax.axis_size(axis)
    return lax.all_to_all(
        jnp.broadcast_to(row[None], (peers,) + row.shape), axis, 0, 0, tiled=True
    )


def on_device(density, solid, void, fixed, residual):
    packed = pl.pallas_call(
        pack_kernel,
        out_shape=jax.ShapeDtypeStruct((9,) + density.shape, F32),
        in_specs=[pl.BlockSpec(memory_space=pltpu.HBM)] * 5,
        scratch_shapes=[
            pltpu.VMEM((2,) + solid.shape, jnp.int32),
            pltpu.VMEM(fixed.shape, jnp.int32),
            pltpu.SemaphoreType.DMA((5,)),
        ],
        compiler_params=pltpu.CompilerParams(vmem_limit_bytes=60 * 1024 * 1024),
    )(density, solid, void, fixed, residual)
    own = jnp.concatenate([from_peer(packed, "gy", -1), packed, from_peer(packed, "gy", 1)], axis=2)
    first = first_call(from_peer(own, "gx", -1), own, from_peer(own, "gx", 1))
    level0, level1, piece = (first[0:4], first[4:8], first[8])
    columns = spread_all(piece, "gy")
    second = second_call(
        from_peer(columns, "gx", -1), columns, from_peer(columns, "gx", 1)
    )
    rows = spread_all(second[1].reshape(-1), "gx")
    precond, image, sums = third_call(rows, second[0], level1, level0)
    sums = jnp.sum(spread_all(sums[0], "gx"), axis=0)
    block = jax.ShapeDtypeStruct(residual.shape, F32)
    return tuple(
        pl.pallas_call(last_kernel, out_shape=[block, block], compiler_params=PARAMS)(
            spread_all(sums, "gy"), precond, image, packed
        )
    )


def solution(mesh):
    return jax.shard_map(
        on_device,
        mesh=mesh,
        in_specs=(
            P("gx", "gy", None),
            P("gx", "gy", None),
            P("gx", "gy", None),
            P(None, "gx", "gy", None),
            P(None, "gx", "gy", None),
        ),
        out_specs=(P(None, "gx", "gy", None), P(None, "gx", "gy", None)),
        check_vma=False,
    )
```

```python
import math

import jax
import jax.numpy as jnp
import numpy as np
from jax import lax
from jax.experimental import pallas as pl
from jax.experimental.pallas import tpu as pltpu
from jax.sharding import PartitionSpec as P

COARSE_ITERS = 4
DAMPING = 0.6
VOID_MODULUS = 0.001
F32 = jnp.float32
GX = ("chip", "core")
PARAMS = pltpu.CompilerParams(vmem_limit_bytes=16 * 1024 * 1024)


def corner_list():
    return [(a, b, c) for a in (0, 1) for b in (0, 1) for c in (0, 1)]


def element_stiffness():
    poisson = 0.3
    lame_first = poisson / ((1.0 + poisson) * (1.0 - 2.0 * poisson))
    shear = 0.5 / (1.0 + poisson)
    elastic = np.zeros((6, 6))
    elastic[:3, :3] = lame_first
    for i in range(3):
        elastic[i, i] += 2.0 * shear
        elastic[i + 3, i + 3] = shear
    points = [0.5 - 0.5 / math.sqrt(3.0), 0.5 + 0.5 / math.sqrt(3.0)]
    gauss = [(u, v, w) for u in points for v in points for w in points]
    stiffness = np.zeros((24, 24))
    for coord in gauss:
        strain = np.zeros((6, 24))
        for k, corner in enumerate(corner_list()):
            values = [coord[d] if corner[d] else 1.0 - coord[d] for d in range(3)]
            slopes = [2.0 * corner[d] - 1.0 for d in range(3)]
            grad_x = slopes[0] * values[1] * values[2]
            grad_y = values[0] * slopes[1] * values[2]
            grad_z = values[0] * values[1] * slopes[2]
            strain[0, 3 * k] = grad_x
            strain[1, 3 * k + 1] = grad_y
            strain[2, 3 * k + 2] = grad_z
            strain[3, 3 * k] = grad_y
            strain[3, 3 * k + 1] = grad_x
            strain[4, 3 * k + 1] = grad_z
            strain[4, 3 * k + 2] = grad_y
            strain[5, 3 * k] = grad_z
            strain[5, 3 * k + 2] = grad_x
        stiffness += strain.T @ elastic @ strain / 8.0
    return stiffness


def mode_table():
    corners = corner_list()
    signs = np.array(
        [[math.prod(2 * c[d] - 1 if m[d] else 1 for d in range(3)) for c in corners] for m in corners],
        float,
    )
    wide = np.kron(signs, np.eye(3))
    table = wide @ element_stiffness() @ wide.T / 64.0
    rows = {}
    for i in range(24):
        row = [
            (corners[j // 3], j % 3, float(table[i, j]))
            for j in range(24)
            if abs(table[i, j]) > 1e-12
        ]
        if row:
            rows[(corners[i // 3], i % 3)] = row
    return rows


MODES = mode_table()
DIAG = float(element_stiffness()[0, 0])
PAIRS = ((0, 0), (1, 0), (0, 1), (1, 1))


def flat_modes(field, z_up, y_up):
    after = z_up(field)
    out = {}
    for k, part in ((0, field + after), (1, after - field)):
        after = y_up(part)
        out[(0, k)] = part + after
        out[(1, k)] = after - part
    return [out[p] for p in PAIRS]


def element_modes(low, high, moduli):
    values = {}
    for c in range(3):
        for q, (j, k) in enumerate(PAIRS):
            if (j, k) != (0, 0):
                values[((0, j, k), c)] = low[c][q] + high[c][q]
            values[((1, j, k), c)] = high[c][q] - low[c][q]
    forces = {}
    for key, row in MODES.items():
        total = None
        for mode, c, weight in row:
            term = weight * values[(mode, c)]
            total = term if total is None else total + term
        forces[key] = total * moduli
    to_low, to_high = [], []
    for c in range(3):
        a, b = [], []
        for j, k in PAIRS:
            slope = forces[((1, j, k), c)]
            mean = forces.get(((0, j, k), c))
            a.append(-slope if mean is None else mean - slope)
            b.append(slope if mean is None else mean + slope)
        to_low.append(a)
        to_high.append(b)
    return to_low, to_high


def node_forces(parts, z_down, y_down):
    out = []
    for k in (0, 1):
        mean, slope = (parts[PAIRS.index((0, k))], parts[PAIRS.index((1, k))])
        out.append((mean - slope) + y_down(mean + slope))
    return (out[0] - out[1]) + z_down(out[0] + out[1])


def shift_up(value, axis):
    return pltpu.roll(value, value.shape[axis] - 1, axis)


def shift_down(value, axis):
    return pltpu.roll(value, 1, axis)


def lanes_of(shape):
    return lax.broadcasted_iota(jnp.int32, shape, len(shape) - 1)


def rows_of(shape):
    return lax.broadcasted_iota(jnp.int32, shape, 0)


def z_shifts(full):
    def up(v):
        s = shift_up(v, 1)
        return jnp.where(lanes_of(v.shape) < v.shape[1] - 1, s, 0.0) if full else s

    def down(v):
        s = shift_down(v, 1)
        return jnp.where(lanes_of(v.shape) > 0, s, 0.0) if full else s

    return up, down


def y_up(v):
    return shift_up(v, 0)


def y_down(v):
    return shift_down(v, 0)


def sweep(load, moduli, first, last, full, emit, unroll=True):
    z_up, z_down = z_shifts(full)

    def modes(x):
        return [flat_modes(load(c, x), z_up, y_up) for c in range(3)]

    high = modes(first + 1)
    _, up = element_modes(modes(first), high, moduli(first))

    def body(x, carry):
        low, before = carry
        high = modes(x + 1)
        own, up = element_modes(low, high, moduli(x))
        forces = [
            node_forces([own[c][q] + before[c][q] for q in range(4)], z_down, y_down)
            for c in range(3)
        ]
        emit(x, forces)
        return (high, up)

    lax.fori_loop(first + 1, last + 1, body, (high, up), unroll=unroll)


def exact_dot(a, b):
    return jnp.dot(a, b, precision=lax.Precision.HIGHEST, preferred_element_type=F32)


def tent(shape, fine, coarse):
    gap = jnp.abs(fine - 2 * coarse)
    return jnp.where(gap == 0, 1.0, jnp.where(gap == 1, 0.5, 0.0)).astype(F32)


def square(kind, period=128):
    shape = (128, 128)
    fine, coarse = (rows_of(shape), lax.rem(lanes_of(shape), period))
    if kind == "restrict":
        return tent(shape, fine, coarse)
    if kind == "pick":
        return jnp.where(fine == 2 * coarse, 1.0, 0.0).astype(F32)
    return jnp.where((fine == 2 * coarse) | (fine == 2 * coarse + 1), 1.0, 0.0).astype(F32)


def prolong_matrix(period=128):
    shape = (128, 128)
    return tent(shape, lanes_of(shape), lax.rem(rows_of(shape), period))


def smooth_rows(v):
    return v + 0.5 * (y_up(v) + y_down(v))


def corner_sum(v, z_down):
    v = v + z_down(v)
    return v + y_down(v)


def scaled(free, inverse):
    return jnp.where(free > 0.0, inverse, DAMPING)


def first_kernel(
    lo_ref, own_ref, hi_ref,
    m_out, i_out, f_out, r_out, m1_out, i1_out, f1_out, c1_out, pack_out,
    t_ref, b_ref, m_ref, i_ref, f_ref, r_ref, s_ref, u_ref, d_ref, v_ref, m1_ref, s1_ref, u1_ref, d1_ref, v2_ref,
):
    pieces = (lo_ref, own_ref, hi_ref)
    slab = (24, 128)
    z_up, z_down = z_shifts(True)
    gx, gy = (lax.axis_index(GX), lax.axis_index("gy"))
    nodes_x, nodes_y = (8 * lax.axis_size(GX), 8 * lax.axis_size("gy"))
    w0, w1, w2, w3 = [2.0 - math.sqrt(n) for n in range(4)]

    def each(first, last, body):
        for p, ref in enumerate(pieces):
            a, b = (max(first, 8 * p), min(last, 8 * p + 7))
            if a <= b:
                lax.fori_loop(a - 8 * p, b - 8 * p + 1, lambda i, _, ref=ref, p=p: body(8 * p + i, ref, i), None, unroll=True)

    def gather_flat(x, ref, i):
        own = ref[0, i]
        ring = z_up(own) + z_down(own)
        c1 = y_up(own) + y_down(own) + ring
        c2 = y_up(ring) + y_down(ring)
        b_ref[x] = w0 * own + w1 * c1 + w2 * c2
        t_ref[x] = w1 * own + w2 * c1 + w3 * c2

    each(0, 23, gather_flat)
    row_at = rows_of(slab) + (8 * gy - 8)
    lane_at = lanes_of(slab)
    inside = ((row_at >= 0) & (row_at < nodes_y)).astype(F32)
    ring_y = (row_at > 0).astype(F32) + (row_at < nodes_y - 1).astype(F32)
    ring_z = (lane_at > 0).astype(F32) + (lane_at < 127).astype(F32)
    plain = w0 + w1 * (ring_y + ring_z) + w2 * ring_y * ring_z
    beside = w1 + w2 * (ring_y + ring_z) + w3 * ring_y * ring_z
    inverse_two, inverse_one = (1.0 / (plain + 2.0 * beside), 1.0 / (plain + beside))

    def moduli_of(x, ref, i):
        at = 8 * gx - 8 + x
        edge = (at == 0) | (at == nodes_x - 1)
        inverse = jnp.where(edge, inverse_one, inverse_two)
        filtered = (b_ref[x] + (t_ref[x - 1] + t_ref[x + 1])) * inverse
        solid, void = (ref[1, i], ref[2, i])
        physical = (1.0 - void) * (solid + (1.0 - solid) * filtered)
        value = VOID_MODULUS + (1.0 - VOID_MODULUS) * (physical * physical * physical)
        mask = jnp.where((at >= 0) & (at < nodes_x), inside, 0.0)
        m_ref[x] = value * mask

    each(1, 22, moduli_of)

    def smooth_of(x, ref, i):
        total = corner_sum(m_ref[x] + m_ref[x - 1], z_down)
        inverse = (DAMPING / DIAG) / total
        i_ref[x] = inverse
        for c in range(3):
            free, r = (ref[3 + c, i], ref[6 + c, i])
            s = scaled(free, inverse) * r
            f_ref[c, x], r_ref[c, x], s_ref[c, x] = (free, r, s)
            u_ref[c, x] = free * s

    each(2, 22, smooth_of)

    def defect_of(x, forces):
        for c in range(3):
            free = f_ref[c, x]
            d_ref[c, x] = r_ref[c, x] - (free * forces[c] + (1.0 - free) * s_ref[c, x])

    sweep(lambda c, x: u_ref[c, x], lambda x: m_ref[x], 2, 21, True, defect_of)

    def keep(x, _):
        m_out[x] = m_ref[x + 6, 4:20, :]
        i_out[x] = i_ref[x + 6, 4:20, :]
        for c in range(3):
            f_out[c, x] = f_ref[c, x + 6, 4:20, :]
            r_out[c, x] = r_ref[c, x + 6, 4:20, :]

    lax.fori_loop(0, 12, keep, None, unroll=2)

    v_ref[:, 24:32, :] = jnp.zeros((64, 8, 128), F32)

    def to_coarse(n, _):
        x = 2 * n + 4
        for c in range(3):
            v = d_ref[c, x] + 0.5 * (d_ref[c, x - 1] + d_ref[c, x + 1])
            v_ref[9 * c + n, 0:24, :] = smooth_rows(v)
            v_ref[27 + 9 * c + n, 0:24, :] = f_ref[c, x]

    lax.fori_loop(0, 9, to_coarse, None, unroll=3)

    def to_coarse_moduli(n, _):
        x = 2 * n + 2
        v = m_ref[x] + m_ref[x + 1]
        v_ref[54 + n, 0:24, :] = v + y_up(v)

    lax.fori_loop(0, 10, to_coarse_moduli, None, unroll=5)

    def half(first, count, matrix):
        v = v_ref[first : first + count, pl.ds(0, 16, stride=2), :]
        return exact_dot(v.reshape(count * 16, 128), matrix).reshape(count, 16, 128)

    restrict, pick, pair = (square("restrict"), square("pick"), square("pair"))
    m1_ref[...] = 0.25 * half(54, 10, pair)
    m1_out[...] = m1_ref[1:10]
    for c in range(3):
        f1_out[c] = half(27 + 9 * c, 9, pick)
        c1_out[c] = f1_out[c] * half(9 * c, 9, restrict)
    _, plain_down = z_shifts(False)

    def smooth1(n, _):
        inverse = (DAMPING / DIAG) / corner_sum(m1_ref[n + 1] + m1_ref[n], plain_down)
        i1_out[n] = inverse
        for c in range(3):
            s = scaled(f1_out[c, n], inverse) * c1_out[c, n]
            s1_ref[c, n] = s
            u1_ref[c, n] = f1_out[c, n] * s

    lax.fori_loop(0, 9, smooth1, None, unroll=True)

    def defect1(n, forces):
        for c in range(3):
            free = f1_out[c, n]
            d1_ref[c, n] = c1_out[c, n] - (free * forces[c] + (1.0 - free) * s1_ref[c, n])

    sweep(lambda c, n: u1_ref[c, n], lambda n: m1_ref[n + 1], 0, 7, False, defect1)

    for n in range(3):
        x = 2 * n + 2
        for c in range(3):
            v2_ref[3 * c + n] = smooth_rows(d1_ref[c, x] + 0.5 * (d1_ref[c, x - 1] + d1_ref[c, x + 1]))
            v2_ref[9 + 3 * c + n] = f1_out[c, x]
    for n in range(4):
        v = m1_ref[2 * n + 1] + m1_ref[2 * n + 2]
        v2_ref[18 + n] = v + y_up(v)

    def half2(first, count, matrix):
        v = v2_ref[first : first + count, pl.ds(0, 8, stride=2), :]
        return exact_dot(v.reshape(count * 8, 128), matrix).reshape(count, 8, 128)

    free2 = half2(9, 9, pick)
    rhs2 = half2(0, 9, restrict) * free2
    moduli2 = 0.25 * half2(18, 4, pair)
    fields = [[moduli2[1 + n] for n in range(3)]]
    fields += [[free2[3 * c + n] for n in range(3)] for c in range(3)]
    fields += [[rhs2[3 * c + n] for n in range(3)] for c in range(3)]
    valid = lanes_of((8, 128)) < 32
    inverse = []
    for n in range(3):
        total = corner_sum(moduli2[n + 1] + moduli2[n], plain_down)
        inverse.append(jnp.where(total > 0.0, (DAMPING / DIAG) / total, 0.0))
    fields.append(inverse)
    for f, slabs in enumerate(fields):
        rows = [None, None]
        for n in range(3):
            v = jnp.where(valid, slabs[n], 0.0)
            for y in range(2):
                piece = v[2 + y : 3 + y]
                q = 2 * (n % 2) + y
                piece = pltpu.roll(piece, 32 * q, 1) if q else piece
                rows[n // 2] = piece if rows[n // 2] is None else rows[n // 2] + piece
        pack_out[f : f + 1, 0:128] = rows[0]
        pack_out[f : f + 1, 128:256] = rows[1]


def first_call(lo, own, hi):
    big = lambda *s: jax.ShapeDtypeStruct(s + (16, 128), F32)
    s24 = lambda *s: pltpu.VMEM(s + (24, 128), F32)
    return pl.pallas_call(
        first_kernel,
        out_shape=[big(12), big(12), big(3, 12), big(3, 12)]
        + [big(9), big(9), big(3, 9), big(3, 9), jax.ShapeDtypeStruct((8, 256), F32)],
        scratch_shapes=[s24(24)] * 4
        + [s24(3, 24)] * 5
        + [
            pltpu.VMEM((64, 32, 128), F32),
            pltpu.VMEM((10, 16, 128), F32),
            pltpu.VMEM((3, 9, 16, 128), F32),
            pltpu.VMEM((3, 9, 16, 128), F32),
            pltpu.VMEM((3, 9, 16, 128), F32),
            pltpu.VMEM((22, 16, 128), F32),
        ],
        compiler_params=PARAMS,
    )(lo, own, hi)


def second_kernel(pair_ref, far_ref, l_out, pack_out, s_ref, u_ref, d_ref, v_ref):
    peers = far_ref.shape[0]
    first = lax.axis_index("core") == 0
    l_out[...] = jnp.zeros(l_out.shape, F32)
    valid = lanes_of((peers, 128)) < 32
    for piece, (base, count) in enumerate(((0, 2), (2, 2), (4, 3))):
        for f in range(8):
            for h in range((count + 1) // 2):
                lanes = slice(128 * h, 128 * h + 128)
                sides = [
                    far_ref[:, f, lanes],
                    pair_ref[0:peers, f, lanes],
                    pair_ref[peers : 2 * peers, f, lanes],
                ]
                rows = jnp.where(first, sides[piece], sides[(piece + 1) % 3])
                for n in range(2 * h, min(2 * h + 2, count)):
                    for y in range(2):
                        q = 2 * (n % 2) + y
                        v = pltpu.roll(rows, 128 - 32 * q, 1) if q else rows
                        l_out[f, base + n, pl.ds(y, peers, stride=2), :] = jnp.where(valid, v, 0.0)

    def smooth(n, _):
        inverse = l_out[7, n]
        for c in range(3):
            s = scaled(l_out[1 + c, n], inverse) * l_out[4 + c, n]
            s_ref[c, n] = s
            u_ref[c, n] = l_out[1 + c, n] * s

    lax.fori_loop(0, 5, smooth, None, unroll=True)

    def defect(n, forces):
        for c in range(3):
            free = l_out[1 + c, n]
            d_ref[c, n] = l_out[4 + c, n] - (free * forces[c] + (1.0 - free) * s_ref[c, n])

    sweep(lambda c, n: u_ref[c, n], lambda n: l_out[0, n], 0, 3, False, defect)
    for c in range(3):
        v_ref[c] = smooth_rows(d_ref[c, 2] + 0.5 * (d_ref[c, 1] + d_ref[c, 3]))
        v_ref[3 + c] = l_out[1 + c, 2]
    v = l_out[0, 2] + l_out[0, 3]
    v_ref[6] = v + y_up(v)

    def half(first, count, matrix):
        v = v_ref[first : first + count, pl.ds(0, 16, stride=2), :]
        return exact_dot(v.reshape(count * 16, 128), matrix).reshape(count, 16, 128)

    free = half(3, 3, square("pick", 16))
    rhs = half(0, 3, square("restrict", 16)) * free
    moduli = 0.25 * half(6, 1, square("pair", 16))
    shape = (8, 128)
    own_lane = (lanes_of(shape) // 16) == rows_of(shape)
    fields = []
    for v in (moduli[0], free[0], free[1], free[2], rhs[0], rhs[1], rhs[2]):
        fields.append(
            [
                jnp.sum(jnp.where(own_lane, v[8 * h : 8 * h + 8], 0.0), axis=0, keepdims=True)
                for h in range(2)
            ]
        )
    for t, v in enumerate(pack_rows(fields)):
        pack_out[:, 128 * t : 128 * t + 128] = v


def second_call(pair, far):
    big = lambda *s: jax.ShapeDtypeStruct(s + (32, 128), F32)
    vmem = lambda *s: pltpu.VMEM(s + (32, 128), F32)
    return pl.pallas_call(
        second_kernel,
        out_shape=[big(8, 7), jax.ShapeDtypeStruct((1, 1408), F32)],
        scratch_shapes=[vmem(3, 5), vmem(3, 5), vmem(3, 4), vmem(7)],
        compiler_params=PARAMS,
    )(pair, far)


def pack_rows(fields):
    out = []
    low = lanes_of(fields[0][0].shape) < 64
    turn = lambda v: pltpu.roll(v, 64, 1)
    for k in range(0, 6, 2):
        (a0, a1), (b0, b1) = (fields[k], fields[k + 1])
        middle = turn(b0)
        out += [a0, jnp.where(low, a1, middle), jnp.where(low, middle, turn(b1))]
    return out + fields[6]


def unpack_rows(tiles):
    out = []
    low = lanes_of(tiles[0].shape) < 64
    turn = lambda v: pltpu.roll(v, 64, 1)
    for k in range(0, 9, 3):
        t0, t1, t2 = tiles[k : k + 3]
        r1, r2 = (turn(t1), turn(t2))
        out.append([t0, jnp.where(low, t1, 0.0)])
        out.append([jnp.where(low, r1, r2), jnp.where(low, r2, 0.0)])
    return out + [tiles[9:11]]


def coarse_solve(rows_ref):
    peers = rows_ref.shape[0]
    shape = (peers + 8, 256)

    fields = unpack_rows([rows_ref[:, 128 * t : 128 * t + 128] for t in range(11)])

    def field(f):
        v = jnp.concatenate(fields[f], axis=1)
        return jnp.concatenate([v, jnp.zeros((8, 256), F32)], axis=0)

    depth = lanes_of(shape) & 15
    z_up = lambda v: jnp.where(depth < 15, shift_up(v, 1), 0.0)
    z_down = lambda v: jnp.where(depth > 0, shift_down(v, 1), 0.0)
    side_up = lambda v: pltpu.roll(v, 240, 1)
    side_down = lambda v: pltpu.roll(v, 16, 1)
    moduli = field(0)
    free = [field(1 + c) for c in range(3)]
    resid = [field(4 + c) for c in range(3)]
    total = moduli + z_down(moduli)
    total = total + side_down(total)
    total = DIAG * (total + shift_down(total, 0))
    inverse = [1.0 / jnp.where(f > 0.0, total, 1.0) for f in free]

    def dot(a, b):
        return jnp.sum(a[0] * b[0] + a[1] * b[1] + a[2] * b[2], keepdims=True)

    def operator(v):
        low = [flat_modes(v[c] * free[c], z_up, side_up) for c in range(3)]
        high = [[shift_up(p, 0) for p in low[c]] for c in range(3)]
        own, up = element_modes(low, high, moduli)
        out = []
        for c in range(3):
            parts = [own[c][q] + shift_down(up[c][q], 0) for q in range(4)]
            forces = node_forces(parts, z_down, side_down)
            out.append(free[c] * forces + (1.0 - free[c]) * v[c])
        return out

    precond = [r * i for r, i in zip(resid, inverse)]
    direction = precond
    inner = dot(resid, precond)
    answer = None
    for step in range(COARSE_ITERS):
        image = operator(direction)
        alpha = inner / dot(direction, image)
        moved = [alpha * d for d in direction]
        answer = moved if answer is None else [s + m for s, m in zip(answer, moved)]
        if step + 1 < COARSE_ITERS:
            resid = [r - alpha * q for r, q in zip(resid, image)]
            precond = [r * i for r, i in zip(resid, inverse)]
            inner_new = dot(resid, precond)
            ratio = inner_new / inner
            direction = [z + ratio * d for z, d in zip(precond, direction)]
            inner = inner_new
    return answer


def third_kernel(
    rows_ref, l2_ref, m1_ref, i1_ref, f1_ref, c1_ref, m_ref, i_ref, f_ref, r_ref,
    p_out, q_out, sum_out,
    a_ref, z3_ref, u2_ref, y2_ref, v2_ref, p1_ref, u1_ref, y1_ref, v1_ref, p0_ref, u0_ref, y0_ref,
):
    gx, gy = (lax.axis_index(GX), lax.axis_index("gy"))
    peers = rows_ref.shape[0]
    answer = coarse_solve(rows_ref)
    for c in range(3):
        a_ref[c, 0:8, :] = jnp.zeros((8, 256), F32)
        a_ref[c, 8 : 16 + peers, :] = answer[c]

    spread3 = prolong_matrix(16)
    shape = (8, 128)
    own_lane = (lanes_of(shape) // 16) == rows_of(shape)
    for c in range(3):
        for i in range(4):
            row = a_ref[c, pl.ds(gx + 7 + i, 1), :]
            halves = [
                jnp.where(own_lane, jnp.broadcast_to(row[:, 128 * h : 128 * h + 128], shape), 0.0)
                for h in range(2)
            ]
            w = exact_dot(jnp.concatenate(halves, axis=0), spread3)
            z3_ref[i, pl.ds(0, 16, stride=2), :] = w
            z3_ref[i, pl.ds(1, 16, stride=2), :] = 0.5 * (w + y_up(w))
        for n in range(7):
            i = n // 2
            p = z3_ref[i] if n % 2 == 0 else 0.5 * (z3_ref[i] + z3_ref[i + 1])
            free = l2_ref[1 + c, n]
            s = scaled(free, l2_ref[7, n]) * l2_ref[4 + c, n] + free * p
            y2_ref[c, n] = s
            u2_ref[c, n] = free * s

    v2_ref[...] = jnp.zeros(v2_ref.shape, F32)

    def level2(n, forces):
        for c in range(3):
            free, s = (l2_ref[1 + c, n], y2_ref[c, n])
            image = free * forces[c] + (1.0 - free) * s
            v2_ref[c, n - 1, 8:40, :] = s + scaled(free, l2_ref[7, n]) * (l2_ref[4 + c, n] - image)

    sweep(lambda c, n: u2_ref[c, n], lambda n: l2_ref[0, n], 0, 5, False, level2)

    spread = prolong_matrix()
    for c in range(3):
        for i in range(5):
            w = exact_dot(v2_ref[c, i, pl.ds(2 * gy + 6, 16), :], spread)
            p1_ref[c, i, pl.ds(0, 8, stride=2), :] = w[0:8]
            p1_ref[c, i, pl.ds(1, 8, stride=2), :] = 0.5 * (w[0:8] + w[1:9])
        for n in range(9):
            i = n // 2
            p = p1_ref[c, i] if n % 2 == 0 else 0.5 * (p1_ref[c, i] + p1_ref[c, i + 1])
            free = f1_ref[c, n]
            s = scaled(free, i1_ref[n]) * c1_ref[c, n] + free * p
            y1_ref[c, n] = s
            u1_ref[c, n] = free * s

    def level1(n, forces):
        for c in range(3):
            free, s = (f1_ref[c, n], y1_ref[c, n])
            image = free * forces[c] + (1.0 - free) * s
            v1_ref[c, n - 1] = s + scaled(free, i1_ref[n]) * (c1_ref[c, n] - image)

    sweep(lambda c, n: u1_ref[c, n], lambda n: m1_ref[n], 0, 7, False, level1)

    for c in range(3):
        w = exact_dot(v1_ref[c].reshape(7 * 16, 128), spread).reshape(7, 16, 128)
        for i in range(7):
            p0_ref[c, i, pl.ds(0, 8, stride=2), :] = w[i, 2:10]
            p0_ref[c, i, pl.ds(1, 8, stride=2), :] = 0.5 * (w[i, 2:10] + w[i, 3:11])
        for n in range(12):
            i = n // 2
            p = p0_ref[c, i] if n % 2 == 0 else 0.5 * (p0_ref[c, i] + p0_ref[c, i + 1])
            free = f_ref[c, n]
            s = scaled(free, i_ref[n]) * r_ref[c, n] + free * p
            y0_ref[c, n] = s
            u0_ref[c, n] = free * s

    def level0(n, forces):
        for c in range(3):
            free, s = (f_ref[c, n], y0_ref[c, n])
            image = free * forces[c] + (1.0 - free) * s
            y0_ref[c, n] = s + scaled(free, i_ref[n]) * (r_ref[c, n] - image)

    sweep(lambda c, n: u0_ref[c, n], lambda n: m_ref[n], 0, 10, True, level0)
    sum_out[...] = jnp.zeros((8, 128), F32)

    def last(n, forces):
        one = two = None
        for c in range(3):
            free, v = (f_ref[c, n], y0_ref[c, n])
            image = (free * forces[c] + (1.0 - free) * v)[4:12]
            v = v[4:12]
            p_out[c, n - 2] = v
            q_out[c, n - 2] = image
            a, b = (r_ref[c, n, 4:12, :] * v, v * image)
            one, two = ((a, b) if one is None else (one + a, two + b))
        sum_out[0:1, :] = sum_out[0:1, :] + jnp.sum(one, axis=0, keepdims=True)
        sum_out[1:2, :] = sum_out[1:2, :] + jnp.sum(two, axis=0, keepdims=True)

    sweep(lambda c, n: f_ref[c, n] * y0_ref[c, n], lambda n: m_ref[n], 1, 9, True, last)
    lane = lanes_of((1, 128))
    one = jnp.sum(sum_out[0:1, :], keepdims=True)
    two = jnp.sum(sum_out[1:2, :], keepdims=True)
    sum_out[0:1, :] = jnp.where(lane == 0, one, jnp.where(lane == 1, two, 0.0))


def third_call(rows, level2, level1, level0):
    own = jax.ShapeDtypeStruct((3, 8, 8, 128), F32)
    peers = rows.shape[0]
    return pl.pallas_call(
        third_kernel,
        out_shape=[own, own, jax.ShapeDtypeStruct((8, 128), F32)],
        scratch_shapes=[
            pltpu.VMEM((3, peers + 16, 256), F32),
            pltpu.VMEM((4, 32, 128), F32),
            pltpu.VMEM((3, 7, 32, 128), F32),
            pltpu.VMEM((3, 7, 32, 128), F32),
            pltpu.VMEM((3, 5, 48, 128), F32),
            pltpu.VMEM((3, 5, 16, 128), F32),
            pltpu.VMEM((3, 9, 16, 128), F32),
            pltpu.VMEM((3, 9, 16, 128), F32),
            pltpu.VMEM((3, 7, 16, 128), F32),
            pltpu.VMEM((3, 7, 16, 128), F32),
            pltpu.VMEM((3, 12, 16, 128), F32),
            pltpu.VMEM((3, 12, 16, 128), F32),
        ],
        compiler_params=PARAMS,
    )(rows, level2, *level1, *level0)


def pack_kernel(density_ref, solid_ref, void_ref, fixed_ref, residual_ref, out_ref, flags_ref, fixed_to, sems):
    copies = [
        pltpu.make_async_copy(solid_ref, flags_ref.at[0], sems.at[0]),
        pltpu.make_async_copy(void_ref, flags_ref.at[1], sems.at[1]),
        pltpu.make_async_copy(fixed_ref, fixed_to, sems.at[2]),
        pltpu.make_async_copy(density_ref, out_ref.at[0], sems.at[3]),
        pltpu.make_async_copy(residual_ref, out_ref.at[pl.ds(6, 3)], sems.at[4]),
    ]
    for copy in copies:
        copy.start()
    copies[0].wait()
    out_ref[1] = flags_ref[0].astype(F32)
    copies[1].wait()
    out_ref[2] = flags_ref[1].astype(F32)
    copies[2].wait()
    out_ref[3:6] = 1.0 - fixed_to[...].astype(F32)
    copies[3].wait()
    copies[4].wait()


def last_kernel(sums_ref, precond_ref, image_ref, packed_ref, update_ref, next_ref):
    total = jnp.sum(sums_ref[...], axis=0, keepdims=True)
    alpha = total[:, 0:1] / total[:, 1:2]
    for c in range(3):
        update_ref[c] = alpha * precond_ref[c]
        next_ref[c] = packed_ref[6 + c] - alpha * image_ref[c]


def from_peer(value, axis, step):
    peers = lax.axis_size(axis)
    return lax.ppermute(value, axis, [(i + step, i) for i in range(peers) if 0 <= i + step < peers])


def spread_all(row, axis):
    peers = lax.axis_size(axis)
    return lax.all_to_all(
        jnp.broadcast_to(row[None], (peers,) + row.shape), axis, 0, 0, tiled=True
    )


def on_device(density, solid, void, fixed, residual):
    packed = pl.pallas_call(
        pack_kernel,
        out_shape=jax.ShapeDtypeStruct((9,) + density.shape, F32),
        in_specs=[pl.BlockSpec(memory_space=pltpu.HBM)] * 5,
        scratch_shapes=[
            pltpu.VMEM((2,) + solid.shape, jnp.int32),
            pltpu.VMEM(fixed.shape, jnp.int32),
            pltpu.SemaphoreType.DMA((5,)),
        ],
        compiler_params=PARAMS,
    )(*[pltpu.with_memory_space_constraint(v, pltpu.HBM) for v in (density, solid, void, fixed, residual)])
    own = jnp.concatenate([from_peer(packed, "gy", -1), packed, from_peer(packed, "gy", 1)], axis=2)
    first = first_call(from_peer(own, GX, -1), own, from_peer(own, GX, 1))
    level0, level1, piece = (first[0:4], first[4:8], first[8])
    columns = spread_all(piece, ("core", "gy"))
    count = lax.axis_size("gy")
    own = jnp.where(lax.axis_index("core") == 0, columns[:count], columns[count:])
    devices = lax.axis_size(GX)
    meet = [(i, i + 1) for i in range(1, devices - 1, 2)]
    second = second_call(columns, lax.ppermute(own, GX, meet + [(j, i) for i, j in meet]))
    rows = spread_all(second[1].reshape(-1), GX)
    precond, image, sums = third_call(rows, second[0], level1, level0)
    sums = jnp.sum(spread_all(sums[0], GX), axis=0)
    block = jax.ShapeDtypeStruct(residual.shape, F32)
    return tuple(
        pl.pallas_call(last_kernel, out_shape=[block, block], compiler_params=PARAMS)(
            spread_all(sums, "gy"), precond, image, packed
        )
    )


def solution(mesh):
    chips, side = (mesh.devices.shape[0] // 2, mesh.devices.shape[1])
    split = jax.sharding.Mesh(mesh.devices.reshape(chips, 2, side), ("chip", "core", "gy"))
    return jax.shard_map(
        on_device,
        mesh=split,
        in_specs=(
            P(("chip", "core"), "gy", None),
            P(("chip", "core"), "gy", None),
            P(("chip", "core"), "gy", None),
            P(None, ("chip", "core"), "gy", None),
            P(None, ("chip", "core"), "gy", None),
        ),
        out_specs=(P(None, ("chip", "core"), "gy", None), P(None, ("chip", "core"), "gy", None)),
        check_vma=False,
    )
```

```python
import math

import jax
import jax.numpy as jnp
import numpy as np
from jax import lax
from jax.experimental import pallas as pl
from jax.experimental.pallas import tpu as pltpu
from jax.sharding import PartitionSpec as P

COARSE_ITERS = 4
DAMPING = 0.6
VOID_MODULUS = 0.001
F32 = jnp.float32
GX = ("chip", "core")
PARAMS = pltpu.CompilerParams(vmem_limit_bytes=16 * 1024 * 1024)


def corner_list():
    return [(a, b, c) for a in (0, 1) for b in (0, 1) for c in (0, 1)]


def element_stiffness():
    poisson = 0.3
    lame_first = poisson / ((1.0 + poisson) * (1.0 - 2.0 * poisson))
    shear = 0.5 / (1.0 + poisson)
    elastic = np.zeros((6, 6))
    elastic[:3, :3] = lame_first
    for i in range(3):
        elastic[i, i] += 2.0 * shear
        elastic[i + 3, i + 3] = shear
    points = [0.5 - 0.5 / math.sqrt(3.0), 0.5 + 0.5 / math.sqrt(3.0)]
    gauss = [(u, v, w) for u in points for v in points for w in points]
    stiffness = np.zeros((24, 24))
    for coord in gauss:
        strain = np.zeros((6, 24))
        for k, corner in enumerate(corner_list()):
            values = [coord[d] if corner[d] else 1.0 - coord[d] for d in range(3)]
            slopes = [2.0 * corner[d] - 1.0 for d in range(3)]
            grad_x = slopes[0] * values[1] * values[2]
            grad_y = values[0] * slopes[1] * values[2]
            grad_z = values[0] * values[1] * slopes[2]
            strain[0, 3 * k] = grad_x
            strain[1, 3 * k + 1] = grad_y
            strain[2, 3 * k + 2] = grad_z
            strain[3, 3 * k] = grad_y
            strain[3, 3 * k + 1] = grad_x
            strain[4, 3 * k + 1] = grad_z
            strain[4, 3 * k + 2] = grad_y
            strain[5, 3 * k] = grad_z
            strain[5, 3 * k + 2] = grad_x
        stiffness += strain.T @ elastic @ strain / 8.0
    return stiffness


def mode_table():
    corners = corner_list()
    signs = np.array(
        [[math.prod(2 * c[d] - 1 if m[d] else 1 for d in range(3)) for c in corners] for m in corners],
        float,
    )
    wide = np.kron(signs, np.eye(3))
    table = wide @ element_stiffness() @ wide.T / 64.0
    rows = {}
    for i in range(24):
        row = [
            (corners[j // 3], j % 3, float(table[i, j]))
            for j in range(24)
            if abs(table[i, j]) > 1e-12
        ]
        if row:
            rows[(corners[i // 3], i % 3)] = row
    return rows


MODES = mode_table()
DIAG = float(element_stiffness()[0, 0])
PAIRS = ((0, 0), (1, 0), (0, 1), (1, 1))


def flat_modes(field, z_up, y_up):
    after = z_up(field)
    out = {}
    for k, part in ((0, field + after), (1, after - field)):
        after = y_up(part)
        out[(0, k)] = part + after
        out[(1, k)] = after - part
    return [out[p] for p in PAIRS]


def element_modes(low, high, moduli):
    values = {}
    for c in range(3):
        for q, (j, k) in enumerate(PAIRS):
            if (j, k) != (0, 0):
                values[((0, j, k), c)] = low[c][q] + high[c][q]
            values[((1, j, k), c)] = high[c][q] - low[c][q]
    forces = {}
    for key, row in MODES.items():
        total = None
        for mode, c, weight in row:
            term = weight * values[(mode, c)]
            total = term if total is None else total + term
        forces[key] = total * moduli
    to_low, to_high = [], []
    for c in range(3):
        a, b = [], []
        for j, k in PAIRS:
            slope = forces[((1, j, k), c)]
            mean = forces.get(((0, j, k), c))
            a.append(-slope if mean is None else mean - slope)
            b.append(slope if mean is None else mean + slope)
        to_low.append(a)
        to_high.append(b)
    return to_low, to_high


def node_forces(parts, z_down, y_down):
    out = []
    for k in (0, 1):
        mean, slope = (parts[PAIRS.index((0, k))], parts[PAIRS.index((1, k))])
        out.append((mean - slope) + y_down(mean + slope))
    return (out[0] - out[1]) + z_down(out[0] + out[1])


def shift_up(value, axis):
    return pltpu.roll(value, value.shape[axis] - 1, axis)


def shift_down(value, axis):
    return pltpu.roll(value, 1, axis)


def lanes_of(shape):
    return lax.broadcasted_iota(jnp.int32, shape, len(shape) - 1)


def rows_of(shape):
    return lax.broadcasted_iota(jnp.int32, shape, 0)


def z_shifts(full):
    def up(v):
        s = shift_up(v, 1)
        return jnp.where(lanes_of(v.shape) < v.shape[1] - 1, s, 0.0) if full else s

    def down(v):
        s = shift_down(v, 1)
        return jnp.where(lanes_of(v.shape) > 0, s, 0.0) if full else s

    return up, down


def y_up(v):
    return shift_up(v, 0)


def y_down(v):
    return shift_down(v, 0)


def sweep(load, moduli, first, last, full, emit, unroll=True):
    z_up, z_down = z_shifts(full)

    def modes(x):
        return [flat_modes(load(c, x), z_up, y_up) for c in range(3)]

    high = modes(first + 1)
    _, up = element_modes(modes(first), high, moduli(first))

    def body(x, carry):
        low, before = carry
        high = modes(x + 1)
        own, up = element_modes(low, high, moduli(x))
        forces = [
            node_forces([own[c][q] + before[c][q] for q in range(4)], z_down, y_down)
            for c in range(3)
        ]
        emit(x, forces)
        return (high, up)

    lax.fori_loop(first + 1, last + 1, body, (high, up), unroll=unroll)


def exact_dot(a, b):
    return jnp.dot(a, b, precision=lax.Precision.HIGHEST, preferred_element_type=F32)


def tent(shape, fine, coarse):
    gap = jnp.abs(fine - 2 * coarse)
    return jnp.where(gap == 0, 1.0, jnp.where(gap == 1, 0.5, 0.0)).astype(F32)


def square(kind, period=128):
    shape = (128, 128)
    fine, coarse = (rows_of(shape), lax.rem(lanes_of(shape), period))
    if kind == "restrict":
        return tent(shape, fine, coarse)
    if kind == "pick":
        return jnp.where(fine == 2 * coarse, 1.0, 0.0).astype(F32)
    return jnp.where((fine == 2 * coarse) | (fine == 2 * coarse + 1), 1.0, 0.0).astype(F32)


def prolong_matrix(period=128):
    shape = (128, 128)
    return tent(shape, lanes_of(shape), lax.rem(rows_of(shape), period))


def smooth_rows(v):
    return v + 0.5 * (y_up(v) + y_down(v))


def corner_sum(v, z_down):
    v = v + z_down(v)
    return v + y_down(v)


def scaled(free, inverse):
    return jnp.where(free > 0.0, inverse, DAMPING)


def first_kernel(
    lo_ref, own_ref, hi_ref,
    m_out, i_out, f_out, r_out, m1_out, i1_out, f1_out, c1_out, pack_out,
    t_ref, b_ref, m_ref, i_ref, f_ref, r_ref, s_ref, u_ref, d_ref, v_ref, m1_ref, s1_ref, u1_ref, d1_ref, v2_ref,
):
    pieces = (lo_ref, own_ref, hi_ref)
    slab = (24, 128)
    z_up, z_down = z_shifts(True)
    gx, gy = (lax.axis_index(GX), lax.axis_index("gy"))
    nodes_x, nodes_y = (8 * lax.axis_size(GX), 8 * lax.axis_size("gy"))
    w0, w1, w2, w3 = [2.0 - math.sqrt(n) for n in range(4)]

    def each(first, last, body):
        for p, ref in enumerate(pieces):
            a, b = (max(first, 8 * p), min(last, 8 * p + 7))
            if a <= b:
                lax.fori_loop(a - 8 * p, b - 8 * p + 1, lambda i, _, ref=ref, p=p: body(8 * p + i, ref, i), None, unroll=True)

    def gather_flat(x, ref, i):
        own = ref[0, i]
        ring = z_up(own) + z_down(own)
        c1 = y_up(own) + y_down(own) + ring
        c2 = y_up(ring) + y_down(ring)
        b_ref[x] = w0 * own + w1 * c1 + w2 * c2
        t_ref[x] = w1 * own + w2 * c1 + w3 * c2

    each(0, 23, gather_flat)
    row_at = rows_of(slab) + (8 * gy - 8)
    lane_at = lanes_of(slab)
    inside = ((row_at >= 0) & (row_at < nodes_y)).astype(F32)
    ring_y = (row_at > 0).astype(F32) + (row_at < nodes_y - 1).astype(F32)
    ring_z = (lane_at > 0).astype(F32) + (lane_at < 127).astype(F32)
    plain = w0 + w1 * (ring_y + ring_z) + w2 * ring_y * ring_z
    beside = w1 + w2 * (ring_y + ring_z) + w3 * ring_y * ring_z
    inverse_two, inverse_one = (1.0 / (plain + 2.0 * beside), 1.0 / (plain + beside))

    def moduli_of(x, ref, i):
        at = 8 * gx - 8 + x
        edge = (at == 0) | (at == nodes_x - 1)
        inverse = jnp.where(edge, inverse_one, inverse_two)
        filtered = (b_ref[x] + (t_ref[x - 1] + t_ref[x + 1])) * inverse
        solid, void = (ref[1, i], ref[2, i])
        physical = (1.0 - void) * (solid + (1.0 - solid) * filtered)
        value = VOID_MODULUS + (1.0 - VOID_MODULUS) * (physical * physical * physical)
        mask = jnp.where((at >= 0) & (at < nodes_x), inside, 0.0)
        m_ref[x] = value * mask

    each(1, 22, moduli_of)

    def smooth_of(x, ref, i):
        total = corner_sum(m_ref[x] + m_ref[x - 1], z_down)
        inverse = (DAMPING / DIAG) / total
        i_ref[x] = inverse
        for c in range(3):
            free, r = (ref[3 + c, i], ref[6 + c, i])
            s = scaled(free, inverse) * r
            f_ref[c, x], r_ref[c, x], s_ref[c, x] = (free, r, s)
            u_ref[c, x] = free * s

    each(2, 22, smooth_of)

    def defect_of(x, forces):
        for c in range(3):
            free = f_ref[c, x]
            d_ref[c, x] = r_ref[c, x] - (free * forces[c] + (1.0 - free) * s_ref[c, x])

    sweep(lambda c, x: u_ref[c, x], lambda x: m_ref[x], 2, 21, True, defect_of)

    def keep(x, _):
        m_out[x] = m_ref[x + 6, 4:20, :]
        i_out[x] = i_ref[x + 6, 4:20, :]
        for c in range(3):
            f_out[c, x] = f_ref[c, x + 6, 4:20, :]
            r_out[c, x] = r_ref[c, x + 6, 4:20, :]

    lax.fori_loop(0, 12, keep, None, unroll=2)

    v_ref[:, 24:32, :] = jnp.zeros((64, 8, 128), F32)

    def to_coarse(n, _):
        x = 2 * n + 4
        for c in range(3):
            v = d_ref[c, x] + 0.5 * (d_ref[c, x - 1] + d_ref[c, x + 1])
            v_ref[9 * c + n, 0:24, :] = smooth_rows(v)
            v_ref[27 + 9 * c + n, 0:24, :] = f_ref[c, x]

    lax.fori_loop(0, 9, to_coarse, None, unroll=3)

    def to_coarse_moduli(n, _):
        x = 2 * n + 2
        v = m_ref[x] + m_ref[x + 1]
        v_ref[54 + n, 0:24, :] = v + y_up(v)

    lax.fori_loop(0, 10, to_coarse_moduli, None, unroll=5)

    def half(first, count, matrix):
        v = v_ref[first : first + count, pl.ds(0, 16, stride=2), :]
        return exact_dot(v.reshape(count * 16, 128), matrix).reshape(count, 16, 128)

    restrict, pick, pair = (square("restrict"), square("pick"), square("pair"))
    m1_ref[...] = 0.25 * half(54, 10, pair)
    m1_out[...] = m1_ref[1:10]
    for c in range(3):
        f1_out[c] = half(27 + 9 * c, 9, pick)
        c1_out[c] = f1_out[c] * half(9 * c, 9, restrict)
    _, plain_down = z_shifts(False)

    def smooth1(n, _):
        inverse = (DAMPING / DIAG) / corner_sum(m1_ref[n + 1] + m1_ref[n], plain_down)
        i1_out[n] = inverse
        for c in range(3):
            s = scaled(f1_out[c, n], inverse) * c1_out[c, n]
            s1_ref[c, n] = s
            u1_ref[c, n] = f1_out[c, n] * s

    lax.fori_loop(0, 9, smooth1, None, unroll=True)

    def defect1(n, forces):
        for c in range(3):
            free = f1_out[c, n]
            d1_ref[c, n] = c1_out[c, n] - (free * forces[c] + (1.0 - free) * s1_ref[c, n])

    sweep(lambda c, n: u1_ref[c, n], lambda n: m1_ref[n + 1], 0, 7, False, defect1)

    for n in range(3):
        x = 2 * n + 2
        for c in range(3):
            v2_ref[3 * c + n] = smooth_rows(d1_ref[c, x] + 0.5 * (d1_ref[c, x - 1] + d1_ref[c, x + 1]))
            v2_ref[9 + 3 * c + n] = f1_out[c, x]
    for n in range(4):
        v = m1_ref[2 * n + 1] + m1_ref[2 * n + 2]
        v2_ref[18 + n] = v + y_up(v)

    def half2(first, count, matrix):
        v = v2_ref[first : first + count, pl.ds(0, 8, stride=2), :]
        return exact_dot(v.reshape(count * 8, 128), matrix).reshape(count, 8, 128)

    free2 = half2(9, 9, pick)
    rhs2 = half2(0, 9, restrict) * free2
    moduli2 = 0.25 * half2(18, 4, pair)
    fields = [[moduli2[1 + n] for n in range(3)]]
    fields += [[free2[3 * c + n] for n in range(3)] for c in range(3)]
    fields += [[rhs2[3 * c + n] for n in range(3)] for c in range(3)]
    valid = lanes_of((8, 128)) < 32
    inverse = []
    for n in range(3):
        total = corner_sum(moduli2[n + 1] + moduli2[n], plain_down)
        inverse.append(jnp.where(total > 0.0, (DAMPING / DIAG) / total, 0.0))
    fields.append(inverse)
    for f, slabs in enumerate(fields):
        rows = [None, None]
        for n in range(3):
            v = jnp.where(valid, slabs[n], 0.0)
            for y in range(2):
                piece = v[2 + y : 3 + y]
                q = 2 * (n % 2) + y
                piece = pltpu.roll(piece, 32 * q, 1) if q else piece
                rows[n // 2] = piece if rows[n // 2] is None else rows[n // 2] + piece
        pack_out[f : f + 1, 0:128] = rows[0]
        pack_out[f : f + 1, 128:256] = rows[1]


def first_call(lo, own, hi):
    big = lambda *s: jax.ShapeDtypeStruct(s + (16, 128), F32)
    s24 = lambda *s: pltpu.VMEM(s + (24, 128), F32)
    return pl.pallas_call(
        first_kernel,
        out_shape=[big(12), big(12), big(3, 12), big(3, 12)]
        + [big(9), big(9), big(3, 9), big(3, 9), jax.ShapeDtypeStruct((8, 256), F32)],
        scratch_shapes=[s24(24)] * 4
        + [s24(3, 24)] * 5
        + [
            pltpu.VMEM((64, 32, 128), F32),
            pltpu.VMEM((10, 16, 128), F32),
            pltpu.VMEM((3, 9, 16, 128), F32),
            pltpu.VMEM((3, 9, 16, 128), F32),
            pltpu.VMEM((3, 9, 16, 128), F32),
            pltpu.VMEM((22, 16, 128), F32),
        ],
        compiler_params=PARAMS,
    )(lo, own, hi)


def second_kernel(pair_ref, far_ref, l_out, pack_out, s_ref, u_ref, d_ref, v_ref):
    peers = far_ref.shape[0]
    first = lax.axis_index("core") == 0
    l_out[...] = jnp.zeros(l_out.shape, F32)
    valid = lanes_of((peers, 128)) < 32
    for piece, (base, count) in enumerate(((0, 2), (2, 2), (4, 3))):
        for f in range(8):
            for h in range((count + 1) // 2):
                lanes = slice(128 * h, 128 * h + 128)
                sides = [
                    far_ref[:, f, lanes],
                    pair_ref[0:peers, f, lanes],
                    pair_ref[peers : 2 * peers, f, lanes],
                ]
                rows = jnp.where(first, sides[piece], sides[(piece + 1) % 3])
                for n in range(2 * h, min(2 * h + 2, count)):
                    for y in range(2):
                        q = 2 * (n % 2) + y
                        v = pltpu.roll(rows, 128 - 32 * q, 1) if q else rows
                        l_out[f, base + n, pl.ds(y, peers, stride=2), :] = jnp.where(valid, v, 0.0)

    def smooth(n, _):
        inverse = l_out[7, n]
        for c in range(3):
            s = scaled(l_out[1 + c, n], inverse) * l_out[4 + c, n]
            s_ref[c, n] = s
            u_ref[c, n] = l_out[1 + c, n] * s

    lax.fori_loop(0, 5, smooth, None, unroll=True)

    def defect(n, forces):
        for c in range(3):
            free = l_out[1 + c, n]
            d_ref[c, n] = l_out[4 + c, n] - (free * forces[c] + (1.0 - free) * s_ref[c, n])

    sweep(lambda c, n: u_ref[c, n], lambda n: l_out[0, n], 0, 3, False, defect)
    for c in range(3):
        v_ref[c] = smooth_rows(d_ref[c, 2] + 0.5 * (d_ref[c, 1] + d_ref[c, 3]))
        v_ref[3 + c] = l_out[1 + c, 2]
    v = l_out[0, 2] + l_out[0, 3]
    v_ref[6] = v + y_up(v)

    def half(first, count, matrix):
        v = v_ref[first : first + count, pl.ds(0, 16, stride=2), :]
        return exact_dot(v.reshape(count * 16, 128), matrix).reshape(count, 16, 128)

    free = half(3, 3, square("pick", 16))
    rhs = half(0, 3, square("restrict", 16)) * free
    moduli = 0.25 * half(6, 1, square("pair", 16))
    shape = (8, 128)
    own_lane = (lanes_of(shape) // 16) == rows_of(shape)
    fields = []
    for v in (moduli[0], free[0], free[1], free[2], rhs[0], rhs[1], rhs[2]):
        fields.append(
            [
                jnp.sum(jnp.where(own_lane, v[8 * h : 8 * h + 8], 0.0), axis=0, keepdims=True)
                for h in range(2)
            ]
        )
    for t, v in enumerate(pack_rows(fields)):
        pack_out[:, 128 * t : 128 * t + 128] = v


def second_call(pair, far):
    big = lambda *s: jax.ShapeDtypeStruct(s + (32, 128), F32)
    vmem = lambda *s: pltpu.VMEM(s + (32, 128), F32)
    return pl.pallas_call(
        second_kernel,
        out_shape=[big(8, 7), jax.ShapeDtypeStruct((1, 1408), F32)],
        scratch_shapes=[vmem(3, 5), vmem(3, 5), vmem(3, 4), vmem(7)],
        compiler_params=PARAMS,
    )(pair, far)


def pack_rows(fields):
    out = []
    low = lanes_of(fields[0][0].shape) < 64
    turn = lambda v: pltpu.roll(v, 64, 1)
    for k in range(0, 6, 2):
        (a0, a1), (b0, b1) = (fields[k], fields[k + 1])
        middle = turn(b0)
        out += [a0, jnp.where(low, a1, middle), jnp.where(low, middle, turn(b1))]
    return out + fields[6]


def unpack_rows(tiles):
    out = []
    low = lanes_of(tiles[0].shape) < 64
    turn = lambda v: pltpu.roll(v, 64, 1)
    for k in range(0, 9, 3):
        t0, t1, t2 = tiles[k : k + 3]
        r1, r2 = (turn(t1), turn(t2))
        out.append([t0, jnp.where(low, t1, 0.0)])
        out.append([jnp.where(low, r1, r2), jnp.where(low, r2, 0.0)])
    return out + [tiles[9:11]]


def coarse_solve(rows_ref):
    peers = rows_ref.shape[0]
    shape = (peers + 8, 256)

    fields = unpack_rows([rows_ref[:, 128 * t : 128 * t + 128] for t in range(11)])

    def field(f):
        v = jnp.concatenate(fields[f], axis=1)
        return jnp.concatenate([v, jnp.zeros((8, 256), F32)], axis=0)

    depth = lanes_of(shape) & 15
    z_up = lambda v: jnp.where(depth < 15, shift_up(v, 1), 0.0)
    z_down = lambda v: jnp.where(depth > 0, shift_down(v, 1), 0.0)
    side_up = lambda v: pltpu.roll(v, 240, 1)
    side_down = lambda v: pltpu.roll(v, 16, 1)
    moduli = field(0)
    free = [field(1 + c) for c in range(3)]
    resid = [field(4 + c) for c in range(3)]
    total = moduli + z_down(moduli)
    total = total + side_down(total)
    total = DIAG * (total + shift_down(total, 0))
    inverse = [1.0 / jnp.where(f > 0.0, total, 1.0) for f in free]

    def dot(a, b):
        return jnp.sum(a[0] * b[0] + a[1] * b[1] + a[2] * b[2], keepdims=True)

    def operator(v):
        low = [flat_modes(v[c] * free[c], z_up, side_up) for c in range(3)]
        high = [[shift_up(p, 0) for p in low[c]] for c in range(3)]
        own, up = element_modes(low, high, moduli)
        out = []
        for c in range(3):
            parts = [own[c][q] + shift_down(up[c][q], 0) for q in range(4)]
            forces = node_forces(parts, z_down, side_down)
            out.append(free[c] * forces + (1.0 - free[c]) * v[c])
        return out

    precond = [r * i for r, i in zip(resid, inverse)]
    direction = precond
    inner = dot(resid, precond)
    answer = None
    for step in range(COARSE_ITERS):
        image = operator(direction)
        alpha = inner / dot(direction, image)
        moved = [alpha * d for d in direction]
        answer = moved if answer is None else [s + m for s, m in zip(answer, moved)]
        if step + 1 < COARSE_ITERS:
            resid = [r - alpha * q for r, q in zip(resid, image)]
            precond = [r * i for r, i in zip(resid, inverse)]
            inner_new = dot(resid, precond)
            ratio = inner_new / inner
            direction = [z + ratio * d for z, d in zip(precond, direction)]
            inner = inner_new
    return answer


def third_kernel(
    rows_ref, l2_ref, m1_ref, i1_ref, f1_ref, c1_ref, m_ref, i_ref, f_ref, r_ref,
    p_out, q_out, sum_out,
    a_ref, z3_ref, u2_ref, y2_ref, v2_ref, p1_ref, u1_ref, y1_ref, v1_ref, p0_ref, u0_ref, y0_ref,
):
    gx, gy = (lax.axis_index(GX), lax.axis_index("gy"))
    peers = rows_ref.shape[0]
    answer = coarse_solve(rows_ref)
    for c in range(3):
        a_ref[c, 0:8, :] = jnp.zeros((8, 256), F32)
        a_ref[c, 8 : 16 + peers, :] = answer[c]

    spread3 = prolong_matrix(16)
    shape = (8, 128)
    own_lane = (lanes_of(shape) // 16) == rows_of(shape)
    for c in range(3):
        for i in range(4):
            row = a_ref[c, pl.ds(gx + 7 + i, 1), :]
            halves = [
                jnp.where(own_lane, jnp.broadcast_to(row[:, 128 * h : 128 * h + 128], shape), 0.0)
                for h in range(2)
            ]
            w = exact_dot(jnp.concatenate(halves, axis=0), spread3)
            z3_ref[i, pl.ds(0, 16, stride=2), :] = w
            z3_ref[i, pl.ds(1, 16, stride=2), :] = 0.5 * (w + y_up(w))
        for n in range(7):
            i = n // 2
            p = z3_ref[i] if n % 2 == 0 else 0.5 * (z3_ref[i] + z3_ref[i + 1])
            free = l2_ref[1 + c, n]
            s = scaled(free, l2_ref[7, n]) * l2_ref[4 + c, n] + free * p
            y2_ref[c, n] = s
            u2_ref[c, n] = free * s

    v2_ref[...] = jnp.zeros(v2_ref.shape, F32)

    def level2(n, forces):
        for c in range(3):
            free, s = (l2_ref[1 + c, n], y2_ref[c, n])
            image = free * forces[c] + (1.0 - free) * s
            v2_ref[c, n - 1, 8:40, :] = s + scaled(free, l2_ref[7, n]) * (l2_ref[4 + c, n] - image)

    sweep(lambda c, n: u2_ref[c, n], lambda n: l2_ref[0, n], 0, 5, False, level2)

    spread = prolong_matrix()
    for c in range(3):
        for i in range(5):
            w = exact_dot(v2_ref[c, i, pl.ds(2 * gy + 6, 16), :], spread)
            p1_ref[c, i, pl.ds(0, 8, stride=2), :] = w[0:8]
            p1_ref[c, i, pl.ds(1, 8, stride=2), :] = 0.5 * (w[0:8] + w[1:9])
        for n in range(9):
            i = n // 2
            p = p1_ref[c, i] if n % 2 == 0 else 0.5 * (p1_ref[c, i] + p1_ref[c, i + 1])
            free = f1_ref[c, n]
            s = scaled(free, i1_ref[n]) * c1_ref[c, n] + free * p
            y1_ref[c, n] = s
            u1_ref[c, n] = free * s

    def level1(n, forces):
        for c in range(3):
            free, s = (f1_ref[c, n], y1_ref[c, n])
            image = free * forces[c] + (1.0 - free) * s
            v1_ref[c, n - 1] = s + scaled(free, i1_ref[n]) * (c1_ref[c, n] - image)

    sweep(lambda c, n: u1_ref[c, n], lambda n: m1_ref[n], 0, 7, False, level1)

    for c in range(3):
        w = exact_dot(v1_ref[c].reshape(7 * 16, 128), spread).reshape(7, 16, 128)
        for i in range(7):
            p0_ref[c, i, pl.ds(0, 8, stride=2), :] = w[i, 2:10]
            p0_ref[c, i, pl.ds(1, 8, stride=2), :] = 0.5 * (w[i, 2:10] + w[i, 3:11])
        for n in range(12):
            i = n // 2
            p = p0_ref[c, i] if n % 2 == 0 else 0.5 * (p0_ref[c, i] + p0_ref[c, i + 1])
            free = f_ref[c, n]
            s = scaled(free, i_ref[n]) * r_ref[c, n] + free * p
            y0_ref[c, n] = s
            u0_ref[c, n] = free * s

    def level0(n, forces):
        for c in range(3):
            free, s = (f_ref[c, n], y0_ref[c, n])
            image = free * forces[c] + (1.0 - free) * s
            y0_ref[c, n] = s + scaled(free, i_ref[n]) * (r_ref[c, n] - image)

    sweep(lambda c, n: u0_ref[c, n], lambda n: m_ref[n], 0, 10, True, level0)
    sum_out[...] = jnp.zeros((8, 128), F32)

    def last(n, forces):
        one = two = None
        for c in range(3):
            free, v = (f_ref[c, n], y0_ref[c, n])
            image = (free * forces[c] + (1.0 - free) * v)[4:12]
            v = v[4:12]
            p_out[c, n - 2] = v
            q_out[c, n - 2] = image
            a, b = (r_ref[c, n, 4:12, :] * v, v * image)
            one, two = ((a, b) if one is None else (one + a, two + b))
        sum_out[0:1, :] = sum_out[0:1, :] + jnp.sum(one, axis=0, keepdims=True)
        sum_out[1:2, :] = sum_out[1:2, :] + jnp.sum(two, axis=0, keepdims=True)

    sweep(lambda c, n: f_ref[c, n] * y0_ref[c, n], lambda n: m_ref[n], 1, 9, True, last)
    lane = lanes_of((1, 128))
    one = jnp.sum(sum_out[0:1, :], keepdims=True)
    two = jnp.sum(sum_out[1:2, :], keepdims=True)
    sum_out[0:1, :] = jnp.where(lane == 0, one, jnp.where(lane == 1, two, 0.0))


def third_call(rows, level2, level1, level0):
    own = jax.ShapeDtypeStruct((3, 8, 8, 128), F32)
    peers = rows.shape[0]
    return pl.pallas_call(
        third_kernel,
        out_shape=[own, own, jax.ShapeDtypeStruct((8, 128), F32)],
        scratch_shapes=[
            pltpu.VMEM((3, peers + 16, 256), F32),
            pltpu.VMEM((4, 32, 128), F32),
            pltpu.VMEM((3, 7, 32, 128), F32),
            pltpu.VMEM((3, 7, 32, 128), F32),
            pltpu.VMEM((3, 5, 48, 128), F32),
            pltpu.VMEM((3, 5, 16, 128), F32),
            pltpu.VMEM((3, 9, 16, 128), F32),
            pltpu.VMEM((3, 9, 16, 128), F32),
            pltpu.VMEM((3, 7, 16, 128), F32),
            pltpu.VMEM((3, 7, 16, 128), F32),
            pltpu.VMEM((3, 12, 16, 128), F32),
            pltpu.VMEM((3, 12, 16, 128), F32),
        ],
        compiler_params=PARAMS,
    )(rows, level2, *level1, *level0)


def pack_kernel(density_ref, solid_ref, void_ref, fixed_ref, residual_ref, out_ref, flags_ref, fixed_to, sems):
    copies = [
        pltpu.make_async_copy(solid_ref, flags_ref.at[0], sems.at[0]),
        pltpu.make_async_copy(void_ref, flags_ref.at[1], sems.at[1]),
        pltpu.make_async_copy(fixed_ref, fixed_to, sems.at[2]),
        pltpu.make_async_copy(density_ref, out_ref.at[0], sems.at[3]),
        pltpu.make_async_copy(residual_ref, out_ref.at[pl.ds(6, 3)], sems.at[4]),
    ]
    for copy in copies:
        copy.start()
    copies[0].wait()
    out_ref[1] = flags_ref[0].astype(F32)
    copies[1].wait()
    out_ref[2] = flags_ref[1].astype(F32)
    copies[2].wait()
    out_ref[3:6] = 1.0 - fixed_to[...].astype(F32)
    copies[3].wait()
    copies[4].wait()


def own_kernel(pair_ref, out_ref):
    count = out_ref.shape[0]
    out_ref[...] = jnp.where(lax.axis_index("core") == 0, pair_ref[:count], pair_ref[count:])


def last_kernel(sums_ref, precond_ref, image_ref, packed_ref, update_ref, next_ref):
    total = jnp.sum(sums_ref[...], axis=0, keepdims=True)
    alpha = total[:, 0:1] / total[:, 1:2]
    for c in range(3):
        update_ref[c] = alpha * precond_ref[c]
        next_ref[c] = packed_ref[6 + c] - alpha * image_ref[c]


def from_peer(value, axis, step):
    peers = lax.axis_size(axis)
    return lax.ppermute(value, axis, [(i + step, i) for i in range(peers) if 0 <= i + step < peers])


def spread_all(row, axis):
    peers = lax.axis_size(axis)
    return lax.all_to_all(
        jnp.broadcast_to(row[None], (peers,) + row.shape), axis, 0, 0, tiled=True
    )


def on_device(density, solid, void, fixed, residual):
    packed = pl.pallas_call(
        pack_kernel,
        out_shape=jax.ShapeDtypeStruct((9,) + density.shape, F32),
        in_specs=[pl.BlockSpec(memory_space=pltpu.HBM)] * 5,
        scratch_shapes=[
            pltpu.VMEM((2,) + solid.shape, jnp.int32),
            pltpu.VMEM(fixed.shape, jnp.int32),
            pltpu.SemaphoreType.DMA((5,)),
        ],
        compiler_params=PARAMS,
    )(*[pltpu.with_memory_space_constraint(v, pltpu.HBM) for v in (density, solid, void, fixed, residual)])
    own = jnp.concatenate([from_peer(packed, "gy", -1), packed, from_peer(packed, "gy", 1)], axis=2)
    first = first_call(from_peer(own, GX, -1), own, from_peer(own, GX, 1))
    level0, level1, piece = (first[0:4], first[4:8], first[8])
    columns = spread_all(piece, ("core", "gy"))
    half = jax.ShapeDtypeStruct((lax.axis_size("gy"),) + piece.shape, F32)
    columns_own = pl.pallas_call(own_kernel, out_shape=half, compiler_params=PARAMS)(columns)
    devices = lax.axis_size(GX)
    meet = [(i, i + 1) for i in range(1, devices - 1, 2)]
    second = second_call(columns, lax.ppermute(columns_own, GX, meet + [(j, i) for i, j in meet]))
    rows = spread_all(second[1].reshape(-1), GX)
    precond, image, sums = third_call(rows, second[0], level1, level0)
    sums = jnp.sum(spread_all(sums[0], GX), axis=0)
    block = jax.ShapeDtypeStruct(residual.shape, F32)
    return tuple(
        pl.pallas_call(last_kernel, out_shape=[block, block], compiler_params=PARAMS)(
            spread_all(sums, "gy"), precond, image, packed
        )
    )


def solution(mesh):
    chips, side = (mesh.devices.shape[0] // 2, mesh.devices.shape[1])
    split = jax.sharding.Mesh(mesh.devices.reshape(chips, 2, side), ("chip", "core", "gy"))
    return jax.shard_map(
        on_device,
        mesh=split,
        in_specs=(
            P(("chip", "core"), "gy", None),
            P(("chip", "core"), "gy", None),
            P(("chip", "core"), "gy", None),
            P(None, ("chip", "core"), "gy", None),
            P(None, ("chip", "core"), "gy", None),
        ),
        out_specs=(P(None, ("chip", "core"), "gy", None), P(None, ("chip", "core"), "gy", None)),
        check_vma=False,
    )
```

```python
import math

import jax
import jax.numpy as jnp
import numpy as np
from jax import lax
from jax.experimental import pallas as pl
from jax.experimental.pallas import tpu as pltpu
from jax.sharding import PartitionSpec as P

COARSE_ITERS = 4
DAMPING = 0.6
VOID_MODULUS = 0.001
F32 = jnp.float32
PARAMS = pltpu.CompilerParams(vmem_limit_bytes=16 * 1024 * 1024)


def corner_list():
    return [(a, b, c) for a in (0, 1) for b in (0, 1) for c in (0, 1)]


def element_stiffness():
    poisson = 0.3
    lame_first = poisson / ((1.0 + poisson) * (1.0 - 2.0 * poisson))
    shear = 0.5 / (1.0 + poisson)
    elastic = np.zeros((6, 6))
    elastic[:3, :3] = lame_first
    for i in range(3):
        elastic[i, i] += 2.0 * shear
        elastic[i + 3, i + 3] = shear
    points = [0.5 - 0.5 / math.sqrt(3.0), 0.5 + 0.5 / math.sqrt(3.0)]
    gauss = [(u, v, w) for u in points for v in points for w in points]
    stiffness = np.zeros((24, 24))
    for coord in gauss:
        strain = np.zeros((6, 24))
        for k, corner in enumerate(corner_list()):
            values = [coord[d] if corner[d] else 1.0 - coord[d] for d in range(3)]
            slopes = [2.0 * corner[d] - 1.0 for d in range(3)]
            grad_x = slopes[0] * values[1] * values[2]
            grad_y = values[0] * slopes[1] * values[2]
            grad_z = values[0] * values[1] * slopes[2]
            strain[0, 3 * k] = grad_x
            strain[1, 3 * k + 1] = grad_y
            strain[2, 3 * k + 2] = grad_z
            strain[3, 3 * k] = grad_y
            strain[3, 3 * k + 1] = grad_x
            strain[4, 3 * k + 1] = grad_z
            strain[4, 3 * k + 2] = grad_y
            strain[5, 3 * k] = grad_z
            strain[5, 3 * k + 2] = grad_x
        stiffness += strain.T @ elastic @ strain / 8.0
    return stiffness


def mode_table():
    corners = corner_list()
    signs = np.array(
        [[math.prod(2 * c[d] - 1 if m[d] else 1 for d in range(3)) for c in corners] for m in corners],
        float,
    )
    wide = np.kron(signs, np.eye(3))
    table = wide @ element_stiffness() @ wide.T / 64.0
    rows = {}
    for i in range(24):
        row = [
            (corners[j // 3], j % 3, float(table[i, j]))
            for j in range(24)
            if abs(table[i, j]) > 1e-12
        ]
        if row:
            rows[(corners[i // 3], i % 3)] = row
    return rows


MODES = mode_table()
DIAG = float(element_stiffness()[0, 0])
PAIRS = ((0, 0), (1, 0), (0, 1), (1, 1))


def flat_modes(field, z_up, y_up):
    after = z_up(field)
    out = {}
    for k, part in ((0, field + after), (1, after - field)):
        after = y_up(part)
        out[(0, k)] = part + after
        out[(1, k)] = after - part
    return [out[p] for p in PAIRS]


def element_modes(low, high, moduli):
    values = {}
    for c in range(3):
        for q, (j, k) in enumerate(PAIRS):
            if (j, k) != (0, 0):
                values[((0, j, k), c)] = low[c][q] + high[c][q]
            values[((1, j, k), c)] = high[c][q] - low[c][q]
    forces = {}
    for key, row in MODES.items():
        total = None
        for mode, c, weight in row:
            term = weight * values[(mode, c)]
            total = term if total is None else total + term
        forces[key] = total * moduli
    to_low, to_high = [], []
    for c in range(3):
        a, b = [], []
        for j, k in PAIRS:
            slope = forces[((1, j, k), c)]
            mean = forces.get(((0, j, k), c))
            a.append(-slope if mean is None else mean - slope)
            b.append(slope if mean is None else mean + slope)
        to_low.append(a)
        to_high.append(b)
    return to_low, to_high


def node_forces(parts, z_down, y_down):
    out = []
    for k in (0, 1):
        mean, slope = (parts[PAIRS.index((0, k))], parts[PAIRS.index((1, k))])
        out.append((mean - slope) + y_down(mean + slope))
    return (out[0] - out[1]) + z_down(out[0] + out[1])


def shift_up(value, axis):
    return pltpu.roll(value, value.shape[axis] - 1, axis)


def shift_down(value, axis):
    return pltpu.roll(value, 1, axis)


def lanes_of(shape):
    return lax.broadcasted_iota(jnp.int32, shape, len(shape) - 1)


def rows_of(shape):
    return lax.broadcasted_iota(jnp.int32, shape, 0)


def z_shifts(full):
    def up(v):
        s = shift_up(v, 1)
        return jnp.where(lanes_of(v.shape) < v.shape[1] - 1, s, 0.0) if full else s

    def down(v):
        s = shift_down(v, 1)
        return jnp.where(lanes_of(v.shape) > 0, s, 0.0) if full else s

    return up, down


def y_up(v):
    return shift_up(v, 0)


def y_down(v):
    return shift_down(v, 0)


def sweep(load, moduli, first, last, full, emit, unroll=True):
    z_up, z_down = z_shifts(full)

    def modes(x):
        return [flat_modes(load(c, x), z_up, y_up) for c in range(3)]

    high = modes(first + 1)
    _, up = element_modes(modes(first), high, moduli(first))

    def body(x, carry):
        low, before = carry
        high = modes(x + 1)
        own, up = element_modes(low, high, moduli(x))
        forces = [
            node_forces([own[c][q] + before[c][q] for q in range(4)], z_down, y_down)
            for c in range(3)
        ]
        emit(x, forces)
        return (high, up)

    lax.fori_loop(first + 1, last + 1, body, (high, up), unroll=unroll)


def exact_dot(a, b):
    return jnp.dot(a, b, precision=lax.Precision.HIGHEST, preferred_element_type=F32)


def tent(shape, fine, coarse):
    gap = jnp.abs(fine - 2 * coarse)
    return jnp.where(gap == 0, 1.0, jnp.where(gap == 1, 0.5, 0.0)).astype(F32)


def square(kind, period=128):
    shape = (128, 128)
    fine, coarse = (rows_of(shape), lax.rem(lanes_of(shape), period))
    if kind == "restrict":
        return tent(shape, fine, coarse)
    if kind == "pick":
        return jnp.where(fine == 2 * coarse, 1.0, 0.0).astype(F32)
    return jnp.where((fine == 2 * coarse) | (fine == 2 * coarse + 1), 1.0, 0.0).astype(F32)


def prolong_matrix(period=128):
    shape = (128, 128)
    return tent(shape, lanes_of(shape), lax.rem(rows_of(shape), period))


def smooth_rows(v):
    return v + 0.5 * (y_up(v) + y_down(v))


def corner_sum(v, z_down):
    v = v + z_down(v)
    return v + y_down(v)


def scaled(free, inverse):
    return jnp.where(free > 0.0, inverse, DAMPING)


def first_kernel(
    lo_ref, own_ref, hi_ref,
    m_out, i_out, f_out, r_out, m1_out, i1_out, f1_out, c1_out, pack_out,
    t_ref, b_ref, m_ref, i_ref, f_ref, r_ref, s_ref, u_ref, d_ref, v_ref, m1_ref, s1_ref, u1_ref, d1_ref, v2_ref,
):
    pieces = (lo_ref, own_ref, hi_ref)
    slab = (24, 128)
    z_up, z_down = z_shifts(True)
    gx, gy = (lax.axis_index("gx"), lax.axis_index("gy"))
    nodes_x, nodes_y = (8 * lax.axis_size("gx"), 8 * lax.axis_size("gy"))
    w0, w1, w2, w3 = [2.0 - math.sqrt(n) for n in range(4)]

    def each(first, last, body):
        for p, ref in enumerate(pieces):
            a, b = (max(first, 8 * p), min(last, 8 * p + 7))
            if a <= b:
                lax.fori_loop(a - 8 * p, b - 8 * p + 1, lambda i, _, ref=ref, p=p: body(8 * p + i, ref, i), None, unroll=True)

    def gather_flat(x, ref, i):
        own = ref[0, i]
        ring = z_up(own) + z_down(own)
        c1 = y_up(own) + y_down(own) + ring
        c2 = y_up(ring) + y_down(ring)
        b_ref[x] = w0 * own + w1 * c1 + w2 * c2
        t_ref[x] = w1 * own + w2 * c1 + w3 * c2

    each(0, 23, gather_flat)
    row_at = rows_of(slab) + (8 * gy - 8)
    lane_at = lanes_of(slab)
    inside = ((row_at >= 0) & (row_at < nodes_y)).astype(F32)
    ring_y = (row_at > 0).astype(F32) + (row_at < nodes_y - 1).astype(F32)
    ring_z = (lane_at > 0).astype(F32) + (lane_at < 127).astype(F32)
    plain = w0 + w1 * (ring_y + ring_z) + w2 * ring_y * ring_z
    beside = w1 + w2 * (ring_y + ring_z) + w3 * ring_y * ring_z
    inverse_two, inverse_one = (1.0 / (plain + 2.0 * beside), 1.0 / (plain + beside))

    def moduli_of(x, ref, i):
        at = 8 * gx - 8 + x
        edge = (at == 0) | (at == nodes_x - 1)
        inverse = jnp.where(edge, inverse_one, inverse_two)
        filtered = (b_ref[x] + (t_ref[x - 1] + t_ref[x + 1])) * inverse
        solid, void = (ref[1, i], ref[2, i])
        physical = (1.0 - void) * (solid + (1.0 - solid) * filtered)
        value = VOID_MODULUS + (1.0 - VOID_MODULUS) * (physical * physical * physical)
        mask = jnp.where((at >= 0) & (at < nodes_x), inside, 0.0)
        m_ref[x] = value * mask

    each(1, 22, moduli_of)

    def smooth_of(x, ref, i):
        total = corner_sum(m_ref[x] + m_ref[x - 1], z_down)
        inverse = (DAMPING / DIAG) / total
        i_ref[x] = inverse
        for c in range(3):
            free, r = (ref[3 + c, i], ref[6 + c, i])
            s = scaled(free, inverse) * r
            f_ref[c, x], r_ref[c, x], s_ref[c, x] = (free, r, s)
            u_ref[c, x] = free * s

    each(2, 22, smooth_of)

    def defect_of(x, forces):
        for c in range(3):
            free = f_ref[c, x]
            d_ref[c, x] = r_ref[c, x] - (free * forces[c] + (1.0 - free) * s_ref[c, x])

    sweep(lambda c, x: u_ref[c, x], lambda x: m_ref[x], 2, 21, True, defect_of)

    def keep(x, _):
        m_out[x] = m_ref[x + 6, 4:20, :]
        i_out[x] = i_ref[x + 6, 4:20, :]
        for c in range(3):
            f_out[c, x] = f_ref[c, x + 6, 4:20, :]
            r_out[c, x] = r_ref[c, x + 6, 4:20, :]

    lax.fori_loop(0, 12, keep, None, unroll=2)

    v_ref[:, 24:32, :] = jnp.zeros((64, 8, 128), F32)

    def to_coarse(n, _):
        x = 2 * n + 4
        for c in range(3):
            v = d_ref[c, x] + 0.5 * (d_ref[c, x - 1] + d_ref[c, x + 1])
            v_ref[9 * c + n, 0:24, :] = smooth_rows(v)
            v_ref[27 + 9 * c + n, 0:24, :] = f_ref[c, x]

    lax.fori_loop(0, 9, to_coarse, None, unroll=3)

    def to_coarse_moduli(n, _):
        x = 2 * n + 2
        v = m_ref[x] + m_ref[x + 1]
        v_ref[54 + n, 0:24, :] = v + y_up(v)

    lax.fori_loop(0, 10, to_coarse_moduli, None, unroll=5)

    def half(first, count, matrix):
        v = v_ref[first : first + count, pl.ds(0, 16, stride=2), :]
        return exact_dot(v.reshape(count * 16, 128), matrix).reshape(count, 16, 128)

    restrict, pick, pair = (square("restrict"), square("pick"), square("pair"))
    m1_ref[...] = 0.25 * half(54, 10, pair)
    m1_out[...] = m1_ref[1:10]
    for c in range(3):
        f1_out[c] = half(27 + 9 * c, 9, pick)
        c1_out[c] = f1_out[c] * half(9 * c, 9, restrict)
    _, plain_down = z_shifts(False)

    def smooth1(n, _):
        inverse = (DAMPING / DIAG) / corner_sum(m1_ref[n + 1] + m1_ref[n], plain_down)
        i1_out[n] = inverse
        for c in range(3):
            s = scaled(f1_out[c, n], inverse) * c1_out[c, n]
            s1_ref[c, n] = s
            u1_ref[c, n] = f1_out[c, n] * s

    lax.fori_loop(0, 9, smooth1, None, unroll=True)

    def defect1(n, forces):
        for c in range(3):
            free = f1_out[c, n]
            d1_ref[c, n] = c1_out[c, n] - (free * forces[c] + (1.0 - free) * s1_ref[c, n])

    sweep(lambda c, n: u1_ref[c, n], lambda n: m1_ref[n + 1], 0, 7, False, defect1)

    for n in range(3):
        x = 2 * n + 2
        for c in range(3):
            v2_ref[3 * c + n] = smooth_rows(d1_ref[c, x] + 0.5 * (d1_ref[c, x - 1] + d1_ref[c, x + 1]))
            v2_ref[9 + 3 * c + n] = f1_out[c, x]
    for n in range(4):
        v = m1_ref[2 * n + 1] + m1_ref[2 * n + 2]
        v2_ref[18 + n] = v + y_up(v)

    def half2(first, count, matrix):
        v = v2_ref[first : first + count, pl.ds(0, 8, stride=2), :]
        return exact_dot(v.reshape(count * 8, 128), matrix).reshape(count, 8, 128)

    free2 = half2(9, 9, pick)
    rhs2 = half2(0, 9, restrict) * free2
    moduli2 = 0.25 * half2(18, 4, pair)
    fields = [[moduli2[1 + n] for n in range(3)]]
    fields += [[free2[3 * c + n] for n in range(3)] for c in range(3)]
    fields += [[rhs2[3 * c + n] for n in range(3)] for c in range(3)]
    valid = lanes_of((8, 128)) < 32
    inverse = []
    for n in range(3):
        total = corner_sum(moduli2[n + 1] + moduli2[n], plain_down)
        inverse.append(jnp.where(total > 0.0, (DAMPING / DIAG) / total, 0.0))
    fields.append(inverse)
    for f, slabs in enumerate(fields):
        rows = [None, None]
        for n in range(3):
            v = jnp.where(valid, slabs[n], 0.0)
            for y in range(2):
                piece = v[2 + y : 3 + y]
                q = 2 * (n % 2) + y
                piece = pltpu.roll(piece, 32 * q, 1) if q else piece
                rows[n // 2] = piece if rows[n // 2] is None else rows[n // 2] + piece
        pack_out[f : f + 1, 0:128] = rows[0]
        pack_out[f : f + 1, 128:256] = rows[1]


def first_call(lo, own, hi):
    big = lambda *s: jax.ShapeDtypeStruct(s + (16, 128), F32)
    s24 = lambda *s: pltpu.VMEM(s + (24, 128), F32)
    return pl.pallas_call(
        first_kernel,
        out_shape=[big(12), big(12), big(3, 12), big(3, 12)]
        + [big(9), big(9), big(3, 9), big(3, 9), jax.ShapeDtypeStruct((8, 256), F32)],
        scratch_shapes=[s24(24)] * 4
        + [s24(3, 24)] * 5
        + [
            pltpu.VMEM((64, 32, 128), F32),
            pltpu.VMEM((10, 16, 128), F32),
            pltpu.VMEM((3, 9, 16, 128), F32),
            pltpu.VMEM((3, 9, 16, 128), F32),
            pltpu.VMEM((3, 9, 16, 128), F32),
            pltpu.VMEM((22, 16, 128), F32),
        ],
        compiler_params=PARAMS,
    )(lo, own, hi)


def second_kernel(lo_ref, own_ref, hi_ref, l_out, pack_out, s_ref, u_ref, d_ref, v_ref):
    peers = own_ref.shape[0]
    l_out[...] = jnp.zeros(l_out.shape, F32)
    valid = lanes_of((peers, 128)) < 32
    for ref, base, count in ((lo_ref, 0, 2), (own_ref, 2, 2), (hi_ref, 4, 3)):
        for f in range(8):
            for h in range((count + 1) // 2):
                rows = ref[:, f, 128 * h : 128 * h + 128]
                for n in range(2 * h, min(2 * h + 2, count)):
                    for y in range(2):
                        q = 2 * (n % 2) + y
                        v = pltpu.roll(rows, 128 - 32 * q, 1) if q else rows
                        l_out[f, base + n, pl.ds(y, peers, stride=2), :] = jnp.where(valid, v, 0.0)

    def smooth(n, _):
        inverse = l_out[7, n]
        for c in range(3):
            s = scaled(l_out[1 + c, n], inverse) * l_out[4 + c, n]
            s_ref[c, n] = s
            u_ref[c, n] = l_out[1 + c, n] * s

    lax.fori_loop(0, 5, smooth, None, unroll=True)

    def defect(n, forces):
        for c in range(3):
            free = l_out[1 + c, n]
            d_ref[c, n] = l_out[4 + c, n] - (free * forces[c] + (1.0 - free) * s_ref[c, n])

    sweep(lambda c, n: u_ref[c, n], lambda n: l_out[0, n], 0, 3, False, defect)
    for c in range(3):
        v_ref[c] = smooth_rows(d_ref[c, 2] + 0.5 * (d_ref[c, 1] + d_ref[c, 3]))
        v_ref[3 + c] = l_out[1 + c, 2]
    v = l_out[0, 2] + l_out[0, 3]
    v_ref[6] = v + y_up(v)

    def half(first, count, matrix):
        v = v_ref[first : first + count, pl.ds(0, 16, stride=2), :]
        return exact_dot(v.reshape(count * 16, 128), matrix).reshape(count, 16, 128)

    free = half(3, 3, square("pick", 16))
    rhs = half(0, 3, square("restrict", 16)) * free
    moduli = 0.25 * half(6, 1, square("pair", 16))
    shape = (8, 128)
    own_lane = (lanes_of(shape) // 16) == rows_of(shape)
    fields = []
    for v in (moduli[0], free[0], free[1], free[2], rhs[0], rhs[1], rhs[2]):
        fields.append(
            [
                jnp.sum(jnp.where(own_lane, v[8 * h : 8 * h + 8], 0.0), axis=0, keepdims=True)
                for h in range(2)
            ]
        )
    for t, v in enumerate(pack_rows(fields)):
        pack_out[:, 128 * t : 128 * t + 128] = v


def second_call(lo, own, hi):
    big = lambda *s: jax.ShapeDtypeStruct(s + (32, 128), F32)
    vmem = lambda *s: pltpu.VMEM(s + (32, 128), F32)
    return pl.pallas_call(
        second_kernel,
        out_shape=[big(8, 7), jax.ShapeDtypeStruct((1, 1408), F32)],
        scratch_shapes=[vmem(3, 5), vmem(3, 5), vmem(3, 4), vmem(7)],
        compiler_params=PARAMS,
    )(lo, own, hi)


def pack_rows(fields):
    out = []
    low = lanes_of(fields[0][0].shape) < 64
    turn = lambda v: pltpu.roll(v, 64, 1)
    for k in range(0, 6, 2):
        (a0, a1), (b0, b1) = (fields[k], fields[k + 1])
        middle = turn(b0)
        out += [a0, jnp.where(low, a1, middle), jnp.where(low, middle, turn(b1))]
    return out + fields[6]


def unpack_rows(tiles):
    out = []
    low = lanes_of(tiles[0].shape) < 64
    turn = lambda v: pltpu.roll(v, 64, 1)
    for k in range(0, 9, 3):
        t0, t1, t2 = tiles[k : k + 3]
        r1, r2 = (turn(t1), turn(t2))
        out.append([t0, jnp.where(low, t1, 0.0)])
        out.append([jnp.where(low, r1, r2), jnp.where(low, r2, 0.0)])
    return out + [tiles[9:11]]


def coarse_solve(rows_ref):
    peers = rows_ref.shape[0]
    shape = (peers + 8, 256)

    fields = unpack_rows([rows_ref[:, 128 * t : 128 * t + 128] for t in range(11)])

    def field(f):
        v = jnp.concatenate(fields[f], axis=1)
        return jnp.concatenate([v, jnp.zeros((8, 256), F32)], axis=0)

    depth = lanes_of(shape) & 15
    z_up = lambda v: jnp.where(depth < 15, shift_up(v, 1), 0.0)
    z_down = lambda v: jnp.where(depth > 0, shift_down(v, 1), 0.0)
    side_up = lambda v: pltpu.roll(v, 240, 1)
    side_down = lambda v: pltpu.roll(v, 16, 1)
    moduli = field(0)
    free = [field(1 + c) for c in range(3)]
    resid = [field(4 + c) for c in range(3)]
    total = moduli + z_down(moduli)
    total = total + side_down(total)
    total = DIAG * (total + shift_down(total, 0))
    inverse = [1.0 / jnp.where(f > 0.0, total, 1.0) for f in free]

    def dot(a, b):
        return jnp.sum(a[0] * b[0] + a[1] * b[1] + a[2] * b[2], keepdims=True)

    def operator(v):
        low = [flat_modes(v[c] * free[c], z_up, side_up) for c in range(3)]
        high = [[shift_up(p, 0) for p in low[c]] for c in range(3)]
        own, up = element_modes(low, high, moduli)
        out = []
        for c in range(3):
            parts = [own[c][q] + shift_down(up[c][q], 0) for q in range(4)]
            forces = node_forces(parts, z_down, side_down)
            out.append(free[c] * forces + (1.0 - free[c]) * v[c])
        return out

    precond = [r * i for r, i in zip(resid, inverse)]
    direction = precond
    inner = dot(resid, precond)
    answer = None
    for step in range(COARSE_ITERS):
        image = operator(direction)
        alpha = inner / dot(direction, image)
        moved = [alpha * d for d in direction]
        answer = moved if answer is None else [s + m for s, m in zip(answer, moved)]
        if step + 1 < COARSE_ITERS:
            resid = [r - alpha * q for r, q in zip(resid, image)]
            precond = [r * i for r, i in zip(resid, inverse)]
            inner_new = dot(resid, precond)
            ratio = inner_new / inner
            direction = [z + ratio * d for z, d in zip(precond, direction)]
            inner = inner_new
    return answer


def third_kernel(
    rows_ref, l2_ref, m1_ref, i1_ref, f1_ref, c1_ref, m_ref, i_ref, f_ref, r_ref,
    p_out, q_out, sum_out,
    a_ref, z3_ref, u2_ref, y2_ref, v2_ref, p1_ref, u1_ref, y1_ref, v1_ref, p0_ref, u0_ref, y0_ref,
):
    gx, gy = (lax.axis_index("gx"), lax.axis_index("gy"))
    peers = rows_ref.shape[0]
    answer = coarse_solve(rows_ref)
    for c in range(3):
        a_ref[c, 0:8, :] = jnp.zeros((8, 256), F32)
        a_ref[c, 8 : 16 + peers, :] = answer[c]

    spread3 = prolong_matrix(16)
    shape = (8, 128)
    own_lane = (lanes_of(shape) // 16) == rows_of(shape)
    for c in range(3):
        for i in range(4):
            row = a_ref[c, pl.ds(gx + 7 + i, 1), :]
            halves = [
                jnp.where(own_lane, jnp.broadcast_to(row[:, 128 * h : 128 * h + 128], shape), 0.0)
                for h in range(2)
            ]
            w = exact_dot(jnp.concatenate(halves, axis=0), spread3)
            z3_ref[i, pl.ds(0, 16, stride=2), :] = w
            z3_ref[i, pl.ds(1, 16, stride=2), :] = 0.5 * (w + y_up(w))
        for n in range(7):
            i = n // 2
            p = z3_ref[i] if n % 2 == 0 else 0.5 * (z3_ref[i] + z3_ref[i + 1])
            free = l2_ref[1 + c, n]
            s = scaled(free, l2_ref[7, n]) * l2_ref[4 + c, n] + free * p
            y2_ref[c, n] = s
            u2_ref[c, n] = free * s

    v2_ref[...] = jnp.zeros(v2_ref.shape, F32)

    def level2(n, forces):
        for c in range(3):
            free, s = (l2_ref[1 + c, n], y2_ref[c, n])
            image = free * forces[c] + (1.0 - free) * s
            v2_ref[c, n - 1, 8:40, :] = s + scaled(free, l2_ref[7, n]) * (l2_ref[4 + c, n] - image)

    sweep(lambda c, n: u2_ref[c, n], lambda n: l2_ref[0, n], 0, 5, False, level2)

    spread = prolong_matrix()
    for c in range(3):
        for i in range(5):
            w = exact_dot(v2_ref[c, i, pl.ds(2 * gy + 6, 16), :], spread)
            p1_ref[c, i, pl.ds(0, 8, stride=2), :] = w[0:8]
            p1_ref[c, i, pl.ds(1, 8, stride=2), :] = 0.5 * (w[0:8] + w[1:9])
        for n in range(9):
            i = n // 2
            p = p1_ref[c, i] if n % 2 == 0 else 0.5 * (p1_ref[c, i] + p1_ref[c, i + 1])
            free = f1_ref[c, n]
            s = scaled(free, i1_ref[n]) * c1_ref[c, n] + free * p
            y1_ref[c, n] = s
            u1_ref[c, n] = free * s

    def level1(n, forces):
        for c in range(3):
            free, s = (f1_ref[c, n], y1_ref[c, n])
            image = free * forces[c] + (1.0 - free) * s
            v1_ref[c, n - 1] = s + scaled(free, i1_ref[n]) * (c1_ref[c, n] - image)

    sweep(lambda c, n: u1_ref[c, n], lambda n: m1_ref[n], 0, 7, False, level1)

    for c in range(3):
        w = exact_dot(v1_ref[c].reshape(7 * 16, 128), spread).reshape(7, 16, 128)
        for i in range(7):
            p0_ref[c, i, pl.ds(0, 8, stride=2), :] = w[i, 2:10]
            p0_ref[c, i, pl.ds(1, 8, stride=2), :] = 0.5 * (w[i, 2:10] + w[i, 3:11])
        for n in range(12):
            i = n // 2
            p = p0_ref[c, i] if n % 2 == 0 else 0.5 * (p0_ref[c, i] + p0_ref[c, i + 1])
            free = f_ref[c, n]
            s = scaled(free, i_ref[n]) * r_ref[c, n] + free * p
            y0_ref[c, n] = s
            u0_ref[c, n] = free * s

    def level0(n, forces):
        for c in range(3):
            free, s = (f_ref[c, n], y0_ref[c, n])
            image = free * forces[c] + (1.0 - free) * s
            y0_ref[c, n] = s + scaled(free, i_ref[n]) * (r_ref[c, n] - image)

    sweep(lambda c, n: u0_ref[c, n], lambda n: m_ref[n], 0, 10, True, level0)
    sum_out[...] = jnp.zeros((8, 128), F32)

    def last(n, forces):
        one = two = None
        for c in range(3):
            free, v = (f_ref[c, n], y0_ref[c, n])
            image = (free * forces[c] + (1.0 - free) * v)[4:12]
            v = v[4:12]
            p_out[c, n - 2] = v
            q_out[c, n - 2] = image
            a, b = (r_ref[c, n, 4:12, :] * v, v * image)
            one, two = ((a, b) if one is None else (one + a, two + b))
        sum_out[0:1, :] = sum_out[0:1, :] + jnp.sum(one, axis=0, keepdims=True)
        sum_out[1:2, :] = sum_out[1:2, :] + jnp.sum(two, axis=0, keepdims=True)

    sweep(lambda c, n: f_ref[c, n] * y0_ref[c, n], lambda n: m_ref[n], 1, 9, True, last)
    lane = lanes_of((1, 128))
    one = jnp.sum(sum_out[0:1, :], keepdims=True)
    two = jnp.sum(sum_out[1:2, :], keepdims=True)
    sum_out[0:1, :] = jnp.where(lane == 0, one, jnp.where(lane == 1, two, 0.0))


def third_call(rows, level2, level1, level0):
    own = jax.ShapeDtypeStruct((3, 8, 8, 128), F32)
    peers = rows.shape[0]
    return pl.pallas_call(
        third_kernel,
        out_shape=[own, own, jax.ShapeDtypeStruct((8, 128), F32)],
        scratch_shapes=[
            pltpu.VMEM((3, peers + 16, 256), F32),
            pltpu.VMEM((4, 32, 128), F32),
            pltpu.VMEM((3, 7, 32, 128), F32),
            pltpu.VMEM((3, 7, 32, 128), F32),
            pltpu.VMEM((3, 5, 48, 128), F32),
            pltpu.VMEM((3, 5, 16, 128), F32),
            pltpu.VMEM((3, 9, 16, 128), F32),
            pltpu.VMEM((3, 9, 16, 128), F32),
            pltpu.VMEM((3, 7, 16, 128), F32),
            pltpu.VMEM((3, 7, 16, 128), F32),
            pltpu.VMEM((3, 12, 16, 128), F32),
            pltpu.VMEM((3, 12, 16, 128), F32),
        ],
        compiler_params=PARAMS,
    )(rows, level2, *level1, *level0)


def pack_kernel(density_ref, solid_ref, void_ref, fixed_ref, residual_ref, out_ref, flags_ref, fixed_to, sems):
    copies = [
        pltpu.make_async_copy(solid_ref, flags_ref.at[0], sems.at[0]),
        pltpu.make_async_copy(void_ref, flags_ref.at[1], sems.at[1]),
        pltpu.make_async_copy(fixed_ref, fixed_to, sems.at[2]),
        pltpu.make_async_copy(density_ref, out_ref.at[0], sems.at[3]),
        pltpu.make_async_copy(residual_ref, out_ref.at[pl.ds(6, 3)], sems.at[4]),
    ]
    for copy in copies:
        copy.start()
    copies[0].wait()
    out_ref[1] = flags_ref[0].astype(F32)
    copies[1].wait()
    out_ref[2] = flags_ref[1].astype(F32)
    copies[2].wait()
    out_ref[3:6] = 1.0 - fixed_to[...].astype(F32)
    copies[3].wait()
    copies[4].wait()


def last_kernel(sums_ref, precond_ref, image_ref, packed_ref, update_ref, next_ref):
    total = jnp.sum(sums_ref[...], axis=0, keepdims=True)
    alpha = total[:, 0:1] / total[:, 1:2]
    for c in range(3):
        update_ref[c] = alpha * precond_ref[c]
        next_ref[c] = packed_ref[6 + c] - alpha * image_ref[c]


def from_peer(value, axis, step):
    peers = lax.axis_size(axis)
    return lax.ppermute(value, axis, [(i + step, i) for i in range(peers) if 0 <= i + step < peers])


def spread_all(row, axis):
    peers = lax.axis_size(axis)
    return lax.all_to_all(
        jnp.broadcast_to(row[None], (peers,) + row.shape), axis, 0, 0, tiled=True
    )


def on_device(density, solid, void, fixed, residual):
    packed = pl.pallas_call(
        pack_kernel,
        out_shape=jax.ShapeDtypeStruct((9,) + density.shape, F32),
        in_specs=[pl.BlockSpec(memory_space=pltpu.HBM)] * 5,
        scratch_shapes=[
            pltpu.VMEM((2,) + solid.shape, jnp.int32),
            pltpu.VMEM(fixed.shape, jnp.int32),
            pltpu.SemaphoreType.DMA((5,)),
        ],
        compiler_params=PARAMS,
    )(*[pltpu.with_memory_space_constraint(v, pltpu.HBM) for v in (density, solid, void, fixed, residual)])
    own = jnp.concatenate([from_peer(packed, "gy", -1), packed, from_peer(packed, "gy", 1)], axis=2)
    first = first_call(from_peer(own, "gx", -1), own, from_peer(own, "gx", 1))
    level0, level1, piece = (first[0:4], first[4:8], first[8])
    columns = spread_all(piece, "gy")
    second = second_call(
        from_peer(columns, "gx", -1), columns, from_peer(columns, "gx", 1)
    )
    rows = spread_all(second[1].reshape(-1), "gx")
    precond, image, sums = third_call(rows, second[0], level1, level0)
    sums = jnp.sum(spread_all(sums[0], "gx"), axis=0)
    block = jax.ShapeDtypeStruct(residual.shape, F32)
    return tuple(
        pl.pallas_call(last_kernel, out_shape=[block, block], compiler_params=PARAMS)(
            spread_all(sums, "gy"), precond, image, packed
        )
    )


def solution(mesh):
    return jax.shard_map(
        on_device,
        mesh=mesh,
        in_specs=(
            P("gx", "gy", None),
            P("gx", "gy", None),
            P("gx", "gy", None),
            P(None, "gx", "gy", None),
            P(None, "gx", "gy", None),
        ),
        out_specs=(P(None, "gx", "gy", None), P(None, "gx", "gy", None)),
        check_vma=False,
    )
```

```python
import math

import jax
import jax.numpy as jnp
import numpy as np
from jax import lax
from jax.experimental import pallas as pl
from jax.experimental.pallas import tpu as pltpu
from jax.sharding import PartitionSpec as P

COARSE_ITERS = 4
DAMPING = 0.6
VOID_MODULUS = 0.001
F32 = jnp.float32
PARAMS = pltpu.CompilerParams(vmem_limit_bytes=16 * 1024 * 1024)


def corner_list():
    return [(a, b, c) for a in (0, 1) for b in (0, 1) for c in (0, 1)]


def element_stiffness():
    poisson = 0.3
    lame_first = poisson / ((1.0 + poisson) * (1.0 - 2.0 * poisson))
    shear = 0.5 / (1.0 + poisson)
    elastic = np.zeros((6, 6))
    elastic[:3, :3] = lame_first
    for i in range(3):
        elastic[i, i] += 2.0 * shear
        elastic[i + 3, i + 3] = shear
    points = [0.5 - 0.5 / math.sqrt(3.0), 0.5 + 0.5 / math.sqrt(3.0)]
    gauss = [(u, v, w) for u in points for v in points for w in points]
    stiffness = np.zeros((24, 24))
    for coord in gauss:
        strain = np.zeros((6, 24))
        for k, corner in enumerate(corner_list()):
            values = [coord[d] if corner[d] else 1.0 - coord[d] for d in range(3)]
            slopes = [2.0 * corner[d] - 1.0 for d in range(3)]
            grad_x = slopes[0] * values[1] * values[2]
            grad_y = values[0] * slopes[1] * values[2]
            grad_z = values[0] * values[1] * slopes[2]
            strain[0, 3 * k] = grad_x
            strain[1, 3 * k + 1] = grad_y
            strain[2, 3 * k + 2] = grad_z
            strain[3, 3 * k] = grad_y
            strain[3, 3 * k + 1] = grad_x
            strain[4, 3 * k + 1] = grad_z
            strain[4, 3 * k + 2] = grad_y
            strain[5, 3 * k] = grad_z
            strain[5, 3 * k + 2] = grad_x
        stiffness += strain.T @ elastic @ strain / 8.0
    return stiffness


def mode_table():
    corners = corner_list()
    signs = np.array(
        [[math.prod(2 * c[d] - 1 if m[d] else 1 for d in range(3)) for c in corners] for m in corners],
        float,
    )
    wide = np.kron(signs, np.eye(3))
    table = wide @ element_stiffness() @ wide.T / 64.0
    rows = {}
    for i in range(24):
        row = [
            (corners[j // 3], j % 3, float(table[i, j]))
            for j in range(24)
            if abs(table[i, j]) > 1e-12
        ]
        if row:
            rows[(corners[i // 3], i % 3)] = row
    return rows


MODES = mode_table()
DIAG = float(element_stiffness()[0, 0])
PAIRS = ((0, 0), (1, 0), (0, 1), (1, 1))


def flat_modes(field, z_up, y_up):
    after = z_up(field)
    out = {}
    for k, part in ((0, field + after), (1, after - field)):
        after = y_up(part)
        out[(0, k)] = part + after
        out[(1, k)] = after - part
    return [out[p] for p in PAIRS]


def element_modes(low, high, moduli):
    values = {}
    for c in range(3):
        for q, (j, k) in enumerate(PAIRS):
            if (j, k) != (0, 0):
                values[((0, j, k), c)] = low[c][q] + high[c][q]
            values[((1, j, k), c)] = high[c][q] - low[c][q]
    forces = {}
    for key, row in MODES.items():
        total = None
        for mode, c, weight in row:
            term = weight * values[(mode, c)]
            total = term if total is None else total + term
        forces[key] = total * moduli
    to_low, to_high = [], []
    for c in range(3):
        a, b = [], []
        for j, k in PAIRS:
            slope = forces[((1, j, k), c)]
            mean = forces.get(((0, j, k), c))
            a.append(-slope if mean is None else mean - slope)
            b.append(slope if mean is None else mean + slope)
        to_low.append(a)
        to_high.append(b)
    return to_low, to_high


def node_forces(parts, z_down, y_down):
    out = []
    for k in (0, 1):
        mean, slope = (parts[PAIRS.index((0, k))], parts[PAIRS.index((1, k))])
        out.append((mean - slope) + y_down(mean + slope))
    return (out[0] - out[1]) + z_down(out[0] + out[1])


def shift_up(value, axis):
    return pltpu.roll(value, value.shape[axis] - 1, axis)


def shift_down(value, axis):
    return pltpu.roll(value, 1, axis)


def lanes_of(shape):
    return lax.broadcasted_iota(jnp.int32, shape, len(shape) - 1)


def rows_of(shape):
    return lax.broadcasted_iota(jnp.int32, shape, 0)


def z_shifts(full):
    def up(v):
        s = shift_up(v, 1)
        return jnp.where(lanes_of(v.shape) < v.shape[1] - 1, s, 0.0) if full else s

    def down(v):
        s = shift_down(v, 1)
        return jnp.where(lanes_of(v.shape) > 0, s, 0.0) if full else s

    return up, down


def y_up(v):
    return shift_up(v, 0)


def y_down(v):
    return shift_down(v, 0)


def sweep(load, moduli, first, last, full, emit, unroll=True):
    z_up, z_down = z_shifts(full)

    def modes(x):
        return [flat_modes(load(c, x), z_up, y_up) for c in range(3)]

    high = modes(first + 1)
    _, up = element_modes(modes(first), high, moduli(first))

    def body(x, carry):
        low, before = carry
        high = modes(x + 1)
        own, up = element_modes(low, high, moduli(x))
        forces = [
            node_forces([own[c][q] + before[c][q] for q in range(4)], z_down, y_down)
            for c in range(3)
        ]
        emit(x, forces)
        return (high, up)

    lax.fori_loop(first + 1, last + 1, body, (high, up), unroll=unroll)


def exact_dot(a, b):
    return jnp.dot(a, b, precision=lax.Precision.HIGHEST, preferred_element_type=F32)


def tent(shape, fine, coarse):
    gap = jnp.abs(fine - 2 * coarse)
    return jnp.where(gap == 0, 1.0, jnp.where(gap == 1, 0.5, 0.0)).astype(F32)


def square(kind, period=128):
    shape = (128, 128)
    fine, coarse = (rows_of(shape), lax.rem(lanes_of(shape), period))
    if kind == "restrict":
        return tent(shape, fine, coarse)
    if kind == "pick":
        return jnp.where(fine == 2 * coarse, 1.0, 0.0).astype(F32)
    return jnp.where((fine == 2 * coarse) | (fine == 2 * coarse + 1), 1.0, 0.0).astype(F32)


def prolong_matrix(period=128):
    shape = (128, 128)
    return tent(shape, lanes_of(shape), lax.rem(rows_of(shape), period))


def smooth_rows(v):
    return v + 0.5 * (y_up(v) + y_down(v))


def corner_sum(v, z_down):
    v = v + z_down(v)
    return v + y_down(v)


def scaled(free, inverse):
    return jnp.where(free > 0.0, inverse, DAMPING)


def low_slab(f):
    return (0, 7, 14)[f] if f < 3 else 20 + 6 * (f - 3)


def high_slab(f):
    return 0 if f == 0 else 8 + 7 * (f - 1)


def join_kernel(lo_ref, mid_ref, hi_ref, own_ref, up_ref, down_ref):
    for r, ref in enumerate((lo_ref, mid_ref, hi_ref)):
        rows = slice(8 * r, 8 * r + 8)
        for f in range(9):
            v = ref[f]
            own_ref[f, :, rows, :] = v
            first = min(f, 1) if f < 3 else 2
            up_ref[low_slab(f) + first : low_slab(f) + 8, rows, :] = v[first:]
            last = 8 if f == 0 else 7
            down_ref[high_slab(f) : high_slab(f) + last, rows, :] = v[:last]


def join_call(lo, mid, hi):
    shapes = [(9, 8, 24, 128), (58, 24, 128), (64, 24, 128)]
    return pl.pallas_call(
        join_kernel,
        out_shape=[jax.ShapeDtypeStruct(shape, F32) for shape in shapes],
        compiler_params=PARAMS,
    )(lo, mid, hi)


def first_kernel(
    lo_ref, own_ref, hi_ref,
    m_out, i_out, f_out, r_out, m1_out, i1_out, f1_out, c1_out, pack_out,
    t_ref, b_ref, m_ref, i_ref, f_ref, r_ref, s_ref, u_ref, d_ref, v_ref, m1_ref, s1_ref, u1_ref, d1_ref, v2_ref,
):
    pieces = (
        lambda f, i: lo_ref[low_slab(f) + i],
        lambda f, i: own_ref[f, i],
        lambda f, i: hi_ref[high_slab(f) + i],
    )
    slab = (24, 128)
    z_up, z_down = z_shifts(True)
    gx, gy = (lax.axis_index("gx"), lax.axis_index("gy"))
    nodes_x, nodes_y = (8 * lax.axis_size("gx"), 8 * lax.axis_size("gy"))
    w0, w1, w2, w3 = [2.0 - math.sqrt(n) for n in range(4)]

    def each(first, last, body):
        for p, get in enumerate(pieces):
            a, b = (max(first, 8 * p), min(last, 8 * p + 7))
            if a <= b:
                lax.fori_loop(a - 8 * p, b - 8 * p + 1, lambda i, _, get=get, p=p: body(8 * p + i, get, i), None, unroll=True)

    def gather_flat(x, get, i):
        own = get(0, i)
        ring = z_up(own) + z_down(own)
        c1 = y_up(own) + y_down(own) + ring
        c2 = y_up(ring) + y_down(ring)
        b_ref[x] = w0 * own + w1 * c1 + w2 * c2
        t_ref[x] = w1 * own + w2 * c1 + w3 * c2

    each(0, 23, gather_flat)
    row_at = rows_of(slab) + (8 * gy - 8)
    lane_at = lanes_of(slab)
    inside = ((row_at >= 0) & (row_at < nodes_y)).astype(F32)
    ring_y = (row_at > 0).astype(F32) + (row_at < nodes_y - 1).astype(F32)
    ring_z = (lane_at > 0).astype(F32) + (lane_at < 127).astype(F32)
    plain = w0 + w1 * (ring_y + ring_z) + w2 * ring_y * ring_z
    beside = w1 + w2 * (ring_y + ring_z) + w3 * ring_y * ring_z
    inverse_two, inverse_one = (1.0 / (plain + 2.0 * beside), 1.0 / (plain + beside))

    def moduli_of(x, get, i):
        at = 8 * gx - 8 + x
        edge = (at == 0) | (at == nodes_x - 1)
        inverse = jnp.where(edge, inverse_one, inverse_two)
        filtered = (b_ref[x] + (t_ref[x - 1] + t_ref[x + 1])) * inverse
        solid, void = (get(1, i), get(2, i))
        physical = (1.0 - void) * (solid + (1.0 - solid) * filtered)
        value = VOID_MODULUS + (1.0 - VOID_MODULUS) * (physical * physical * physical)
        mask = jnp.where((at >= 0) & (at < nodes_x), inside, 0.0)
        m_ref[x] = value * mask

    each(1, 22, moduli_of)

    def smooth_of(x, get, i):
        total = corner_sum(m_ref[x] + m_ref[x - 1], z_down)
        inverse = (DAMPING / DIAG) / total
        i_ref[x] = inverse
        for c in range(3):
            free, r = (get(3 + c, i), get(6 + c, i))
            s = scaled(free, inverse) * r
            f_ref[c, x], r_ref[c, x], s_ref[c, x] = (free, r, s)
            u_ref[c, x] = free * s

    each(2, 22, smooth_of)

    def defect_of(x, forces):
        for c in range(3):
            free = f_ref[c, x]
            d_ref[c, x] = r_ref[c, x] - (free * forces[c] + (1.0 - free) * s_ref[c, x])

    sweep(lambda c, x: u_ref[c, x], lambda x: m_ref[x], 2, 21, True, defect_of)

    def keep(x, _):
        m_out[x] = m_ref[x + 6, 4:20, :]
        i_out[x] = i_ref[x + 6, 4:20, :]
        for c in range(3):
            f_out[c, x] = f_ref[c, x + 6, 4:20, :]
            r_out[c, x] = r_ref[c, x + 6, 4:20, :]

    lax.fori_loop(0, 12, keep, None, unroll=2)

    v_ref[:, 24:32, :] = jnp.zeros((64, 8, 128), F32)

    def to_coarse(n, _):
        x = 2 * n + 4
        for c in range(3):
            v = d_ref[c, x] + 0.5 * (d_ref[c, x - 1] + d_ref[c, x + 1])
            v_ref[9 * c + n, 0:24, :] = smooth_rows(v)
            v_ref[27 + 9 * c + n, 0:24, :] = f_ref[c, x]

    lax.fori_loop(0, 9, to_coarse, None, unroll=3)

    def to_coarse_moduli(n, _):
        x = 2 * n + 2
        v = m_ref[x] + m_ref[x + 1]
        v_ref[54 + n, 0:24, :] = v + y_up(v)

    lax.fori_loop(0, 10, to_coarse_moduli, None, unroll=5)

    def half(first, count, matrix):
        v = v_ref[first : first + count, pl.ds(0, 16, stride=2), :]
        return exact_dot(v.reshape(count * 16, 128), matrix).reshape(count, 16, 128)

    restrict, pick, pair = (square("restrict"), square("pick"), square("pair"))
    m1_ref[...] = 0.25 * half(54, 10, pair)
    m1_out[...] = m1_ref[1:10]
    for c in range(3):
        f1_out[c] = half(27 + 9 * c, 9, pick)
        c1_out[c] = f1_out[c] * half(9 * c, 9, restrict)
    _, plain_down = z_shifts(False)

    def smooth1(n, _):
        inverse = (DAMPING / DIAG) / corner_sum(m1_ref[n + 1] + m1_ref[n], plain_down)
        i1_out[n] = inverse
        for c in range(3):
            s = scaled(f1_out[c, n], inverse) * c1_out[c, n]
            s1_ref[c, n] = s
            u1_ref[c, n] = f1_out[c, n] * s

    lax.fori_loop(0, 9, smooth1, None, unroll=True)

    def defect1(n, forces):
        for c in range(3):
            free = f1_out[c, n]
            d1_ref[c, n] = c1_out[c, n] - (free * forces[c] + (1.0 - free) * s1_ref[c, n])

    sweep(lambda c, n: u1_ref[c, n], lambda n: m1_ref[n + 1], 0, 7, False, defect1)

    for n in range(3):
        x = 2 * n + 2
        for c in range(3):
            v2_ref[3 * c + n] = smooth_rows(d1_ref[c, x] + 0.5 * (d1_ref[c, x - 1] + d1_ref[c, x + 1]))
            v2_ref[9 + 3 * c + n] = f1_out[c, x]
    for n in range(4):
        v = m1_ref[2 * n + 1] + m1_ref[2 * n + 2]
        v2_ref[18 + n] = v + y_up(v)

    def half2(first, count, matrix):
        v = v2_ref[first : first + count, pl.ds(0, 8, stride=2), :]
        return exact_dot(v.reshape(count * 8, 128), matrix).reshape(count, 8, 128)

    free2 = half2(9, 9, pick)
    rhs2 = half2(0, 9, restrict) * free2
    moduli2 = 0.25 * half2(18, 4, pair)
    fields = [[moduli2[1 + n] for n in range(3)]]
    fields += [[free2[3 * c + n] for n in range(3)] for c in range(3)]
    fields += [[rhs2[3 * c + n] for n in range(3)] for c in range(3)]
    valid = lanes_of((8, 128)) < 32
    inverse = []
    for n in range(3):
        total = corner_sum(moduli2[n + 1] + moduli2[n], plain_down)
        inverse.append(jnp.where(total > 0.0, (DAMPING / DIAG) / total, 0.0))
    fields.append(inverse)
    for f, slabs in enumerate(fields):
        rows = [None, None]
        for n in range(3):
            v = jnp.where(valid, slabs[n], 0.0)
            for y in range(2):
                piece = v[2 + y : 3 + y]
                q = 2 * (n % 2) + y
                piece = pltpu.roll(piece, 32 * q, 1) if q else piece
                rows[n // 2] = piece if rows[n // 2] is None else rows[n // 2] + piece
        pack_out[f : f + 1, 0:128] = rows[0]
        pack_out[f : f + 1, 128:256] = rows[1]


def first_call(lo, own, hi):
    big = lambda *s: jax.ShapeDtypeStruct(s + (16, 128), F32)
    s24 = lambda *s: pltpu.VMEM(s + (24, 128), F32)
    return pl.pallas_call(
        first_kernel,
        out_shape=[big(12), big(12), big(3, 12), big(3, 12)]
        + [big(9), big(9), big(3, 9), big(3, 9), jax.ShapeDtypeStruct((8, 256), F32)],
        scratch_shapes=[s24(24)] * 4
        + [s24(3, 24)] * 5
        + [
            pltpu.VMEM((64, 32, 128), F32),
            pltpu.VMEM((10, 16, 128), F32),
            pltpu.VMEM((3, 9, 16, 128), F32),
            pltpu.VMEM((3, 9, 16, 128), F32),
            pltpu.VMEM((3, 9, 16, 128), F32),
            pltpu.VMEM((22, 16, 128), F32),
        ],
        compiler_params=PARAMS,
    )(lo, own, hi)


def second_kernel(lo_ref, own_ref, hi_ref, l_out, pack_out, s_ref, u_ref, d_ref, v_ref):
    peers = own_ref.shape[0]
    l_out[...] = jnp.zeros(l_out.shape, F32)
    valid = lanes_of((peers, 128)) < 32
    for ref, base, count in ((lo_ref, 0, 2), (own_ref, 2, 2), (hi_ref, 4, 3)):
        for f in range(8):
            for h in range((count + 1) // 2):
                rows = ref[:, f, 128 * h : 128 * h + 128]
                for n in range(2 * h, min(2 * h + 2, count)):
                    for y in range(2):
                        q = 2 * (n % 2) + y
                        v = pltpu.roll(rows, 128 - 32 * q, 1) if q else rows
                        l_out[f, base + n, pl.ds(y, peers, stride=2), :] = jnp.where(valid, v, 0.0)

    def smooth(n, _):
        inverse = l_out[7, n]
        for c in range(3):
            s = scaled(l_out[1 + c, n], inverse) * l_out[4 + c, n]
            s_ref[c, n] = s
            u_ref[c, n] = l_out[1 + c, n] * s

    lax.fori_loop(0, 5, smooth, None, unroll=True)

    def defect(n, forces):
        for c in range(3):
            free = l_out[1 + c, n]
            d_ref[c, n] = l_out[4 + c, n] - (free * forces[c] + (1.0 - free) * s_ref[c, n])

    sweep(lambda c, n: u_ref[c, n], lambda n: l_out[0, n], 0, 3, False, defect)
    for c in range(3):
        v_ref[c] = smooth_rows(d_ref[c, 2] + 0.5 * (d_ref[c, 1] + d_ref[c, 3]))
        v_ref[3 + c] = l_out[1 + c, 2]
    v = l_out[0, 2] + l_out[0, 3]
    v_ref[6] = v + y_up(v)

    def half(first, count, matrix):
        v = v_ref[first : first + count, pl.ds(0, 16, stride=2), :]
        return exact_dot(v.reshape(count * 16, 128), matrix).reshape(count, 16, 128)

    free = half(3, 3, square("pick", 16))
    rhs = half(0, 3, square("restrict", 16)) * free
    moduli = 0.25 * half(6, 1, square("pair", 16))
    shape = (8, 128)
    own_lane = (lanes_of(shape) // 16) == rows_of(shape)
    fields = []
    for v in (moduli[0], free[0], free[1], free[2], rhs[0], rhs[1], rhs[2]):
        fields.append(
            [
                jnp.sum(jnp.where(own_lane, v[8 * h : 8 * h + 8], 0.0), axis=0, keepdims=True)
                for h in range(2)
            ]
        )
    for t, v in enumerate(pack_rows(fields)):
        pack_out[:, 128 * t : 128 * t + 128] = v


def second_call(lo, own, hi):
    big = lambda *s: jax.ShapeDtypeStruct(s + (32, 128), F32)
    vmem = lambda *s: pltpu.VMEM(s + (32, 128), F32)
    return pl.pallas_call(
        second_kernel,
        out_shape=[big(8, 7), jax.ShapeDtypeStruct((1, 1408), F32)],
        scratch_shapes=[vmem(3, 5), vmem(3, 5), vmem(3, 4), vmem(7)],
        compiler_params=PARAMS,
    )(lo, own, hi)


def pack_rows(fields):
    out = []
    low = lanes_of(fields[0][0].shape) < 64
    turn = lambda v: pltpu.roll(v, 64, 1)
    for k in range(0, 6, 2):
        (a0, a1), (b0, b1) = (fields[k], fields[k + 1])
        middle = turn(b0)
        out += [a0, jnp.where(low, a1, middle), jnp.where(low, middle, turn(b1))]
    return out + fields[6]


def unpack_rows(tiles):
    out = []
    low = lanes_of(tiles[0].shape) < 64
    turn = lambda v: pltpu.roll(v, 64, 1)
    for k in range(0, 9, 3):
        t0, t1, t2 = tiles[k : k + 3]
        r1, r2 = (turn(t1), turn(t2))
        out.append([t0, jnp.where(low, t1, 0.0)])
        out.append([jnp.where(low, r1, r2), jnp.where(low, r2, 0.0)])
    return out + [tiles[9:11]]


def coarse_solve(rows_ref):
    peers = rows_ref.shape[0]
    shape = (peers + 8, 256)

    fields = unpack_rows([rows_ref[:, 128 * t : 128 * t + 128] for t in range(11)])

    def field(f):
        v = jnp.concatenate(fields[f], axis=1)
        return jnp.concatenate([v, jnp.zeros((8, 256), F32)], axis=0)

    depth = lanes_of(shape) & 15
    z_up = lambda v: jnp.where(depth < 15, shift_up(v, 1), 0.0)
    z_down = lambda v: jnp.where(depth > 0, shift_down(v, 1), 0.0)
    side_up = lambda v: pltpu.roll(v, 240, 1)
    side_down = lambda v: pltpu.roll(v, 16, 1)
    moduli = field(0)
    free = [field(1 + c) for c in range(3)]
    resid = [field(4 + c) for c in range(3)]
    total = moduli + z_down(moduli)
    total = total + side_down(total)
    total = DIAG * (total + shift_down(total, 0))
    inverse = [1.0 / jnp.where(f > 0.0, total, 1.0) for f in free]

    def dot(a, b):
        return jnp.sum(a[0] * b[0] + a[1] * b[1] + a[2] * b[2], keepdims=True)

    def operator(v):
        low = [flat_modes(v[c] * free[c], z_up, side_up) for c in range(3)]
        high = [[shift_up(p, 0) for p in low[c]] for c in range(3)]
        own, up = element_modes(low, high, moduli)
        out = []
        for c in range(3):
            parts = [own[c][q] + shift_down(up[c][q], 0) for q in range(4)]
            forces = node_forces(parts, z_down, side_down)
            out.append(free[c] * forces + (1.0 - free[c]) * v[c])
        return out

    precond = [r * i for r, i in zip(resid, inverse)]
    direction = precond
    inner = dot(resid, precond)
    answer = None
    for step in range(COARSE_ITERS):
        image = operator(direction)
        alpha = inner / dot(direction, image)
        moved = [alpha * d for d in direction]
        answer = moved if answer is None else [s + m for s, m in zip(answer, moved)]
        if step + 1 < COARSE_ITERS:
            resid = [r - alpha * q for r, q in zip(resid, image)]
            precond = [r * i for r, i in zip(resid, inverse)]
            inner_new = dot(resid, precond)
            ratio = inner_new / inner
            direction = [z + ratio * d for z, d in zip(precond, direction)]
            inner = inner_new
    return answer


def third_kernel(
    rows_ref, l2_ref, m1_ref, i1_ref, f1_ref, c1_ref, m_ref, i_ref, f_ref, r_ref,
    p_out, q_out, sum_out,
    a_ref, z3_ref, u2_ref, y2_ref, v2_ref, p1_ref, u1_ref, y1_ref, v1_ref, p0_ref, u0_ref, y0_ref,
):
    gx, gy = (lax.axis_index("gx"), lax.axis_index("gy"))
    peers = rows_ref.shape[0]
    answer = coarse_solve(rows_ref)
    for c in range(3):
        a_ref[c, 0:8, :] = jnp.zeros((8, 256), F32)
        a_ref[c, 8 : 16 + peers, :] = answer[c]

    spread3 = prolong_matrix(16)
    shape = (8, 128)
    own_lane = (lanes_of(shape) // 16) == rows_of(shape)
    for c in range(3):
        for i in range(4):
            row = a_ref[c, pl.ds(gx + 7 + i, 1), :]
            halves = [
                jnp.where(own_lane, jnp.broadcast_to(row[:, 128 * h : 128 * h + 128], shape), 0.0)
                for h in range(2)
            ]
            w = exact_dot(jnp.concatenate(halves, axis=0), spread3)
            z3_ref[i, pl.ds(0, 16, stride=2), :] = w
            z3_ref[i, pl.ds(1, 16, stride=2), :] = 0.5 * (w + y_up(w))
        for n in range(7):
            i = n // 2
            p = z3_ref[i] if n % 2 == 0 else 0.5 * (z3_ref[i] + z3_ref[i + 1])
            free = l2_ref[1 + c, n]
            s = scaled(free, l2_ref[7, n]) * l2_ref[4 + c, n] + free * p
            y2_ref[c, n] = s
            u2_ref[c, n] = free * s

    v2_ref[...] = jnp.zeros(v2_ref.shape, F32)

    def level2(n, forces):
        for c in range(3):
            free, s = (l2_ref[1 + c, n], y2_ref[c, n])
            image = free * forces[c] + (1.0 - free) * s
            v2_ref[c, n - 1, 8:40, :] = s + scaled(free, l2_ref[7, n]) * (l2_ref[4 + c, n] - image)

    sweep(lambda c, n: u2_ref[c, n], lambda n: l2_ref[0, n], 0, 5, False, level2)

    spread = prolong_matrix()
    for c in range(3):
        for i in range(5):
            w = exact_dot(v2_ref[c, i, pl.ds(2 * gy + 6, 16), :], spread)
            p1_ref[c, i, pl.ds(0, 8, stride=2), :] = w[0:8]
            p1_ref[c, i, pl.ds(1, 8, stride=2), :] = 0.5 * (w[0:8] + w[1:9])
        for n in range(9):
            i = n // 2
            p = p1_ref[c, i] if n % 2 == 0 else 0.5 * (p1_ref[c, i] + p1_ref[c, i + 1])
            free = f1_ref[c, n]
            s = scaled(free, i1_ref[n]) * c1_ref[c, n] + free * p
            y1_ref[c, n] = s
            u1_ref[c, n] = free * s

    def level1(n, forces):
        for c in range(3):
            free, s = (f1_ref[c, n], y1_ref[c, n])
            image = free * forces[c] + (1.0 - free) * s
            v1_ref[c, n - 1] = s + scaled(free, i1_ref[n]) * (c1_ref[c, n] - image)

    sweep(lambda c, n: u1_ref[c, n], lambda n: m1_ref[n], 0, 7, False, level1)

    for c in range(3):
        w = exact_dot(v1_ref[c].reshape(7 * 16, 128), spread).reshape(7, 16, 128)
        for i in range(7):
            p0_ref[c, i, pl.ds(0, 8, stride=2), :] = w[i, 2:10]
            p0_ref[c, i, pl.ds(1, 8, stride=2), :] = 0.5 * (w[i, 2:10] + w[i, 3:11])
        for n in range(12):
            i = n // 2
            p = p0_ref[c, i] if n % 2 == 0 else 0.5 * (p0_ref[c, i] + p0_ref[c, i + 1])
            free = f_ref[c, n]
            s = scaled(free, i_ref[n]) * r_ref[c, n] + free * p
            y0_ref[c, n] = s
            u0_ref[c, n] = free * s

    def level0(n, forces):
        for c in range(3):
            free, s = (f_ref[c, n], y0_ref[c, n])
            image = free * forces[c] + (1.0 - free) * s
            y0_ref[c, n] = s + scaled(free, i_ref[n]) * (r_ref[c, n] - image)

    sweep(lambda c, n: u0_ref[c, n], lambda n: m_ref[n], 0, 10, True, level0)
    sum_out[...] = jnp.zeros((8, 128), F32)

    def last(n, forces):
        one = two = None
        for c in range(3):
            free, v = (f_ref[c, n], y0_ref[c, n])
            image = (free * forces[c] + (1.0 - free) * v)[4:12]
            v = v[4:12]
            p_out[c, n - 2] = v
            q_out[c, n - 2] = image
            a, b = (r_ref[c, n, 4:12, :] * v, v * image)
            one, two = ((a, b) if one is None else (one + a, two + b))
        sum_out[0:1, :] = sum_out[0:1, :] + jnp.sum(one, axis=0, keepdims=True)
        sum_out[1:2, :] = sum_out[1:2, :] + jnp.sum(two, axis=0, keepdims=True)

    sweep(lambda c, n: f_ref[c, n] * y0_ref[c, n], lambda n: m_ref[n], 1, 9, True, last)
    lane = lanes_of((1, 128))
    one = jnp.sum(sum_out[0:1, :], keepdims=True)
    two = jnp.sum(sum_out[1:2, :], keepdims=True)
    sum_out[0:1, :] = jnp.where(lane == 0, one, jnp.where(lane == 1, two, 0.0))


def third_call(rows, level2, level1, level0):
    own = jax.ShapeDtypeStruct((3, 8, 8, 128), F32)
    peers = rows.shape[0]
    return pl.pallas_call(
        third_kernel,
        out_shape=[own, own, jax.ShapeDtypeStruct((8, 128), F32)],
        scratch_shapes=[
            pltpu.VMEM((3, peers + 16, 256), F32),
            pltpu.VMEM((4, 32, 128), F32),
            pltpu.VMEM((3, 7, 32, 128), F32),
            pltpu.VMEM((3, 7, 32, 128), F32),
            pltpu.VMEM((3, 5, 48, 128), F32),
            pltpu.VMEM((3, 5, 16, 128), F32),
            pltpu.VMEM((3, 9, 16, 128), F32),
            pltpu.VMEM((3, 9, 16, 128), F32),
            pltpu.VMEM((3, 7, 16, 128), F32),
            pltpu.VMEM((3, 7, 16, 128), F32),
            pltpu.VMEM((3, 12, 16, 128), F32),
            pltpu.VMEM((3, 12, 16, 128), F32),
        ],
        compiler_params=PARAMS,
    )(rows, level2, *level1, *level0)


def pack_kernel(density_ref, solid_ref, void_ref, fixed_ref, residual_ref, out_ref, flags_ref, fixed_to, sems):
    copies = [
        pltpu.make_async_copy(solid_ref, flags_ref.at[0], sems.at[0]),
        pltpu.make_async_copy(void_ref, flags_ref.at[1], sems.at[1]),
        pltpu.make_async_copy(fixed_ref, fixed_to, sems.at[2]),
        pltpu.make_async_copy(density_ref, out_ref.at[0], sems.at[3]),
        pltpu.make_async_copy(residual_ref, out_ref.at[pl.ds(6, 3)], sems.at[4]),
    ]
    for copy in copies:
        copy.start()
    copies[0].wait()
    out_ref[1] = flags_ref[0].astype(F32)
    copies[1].wait()
    out_ref[2] = flags_ref[1].astype(F32)
    copies[2].wait()
    out_ref[3:6] = 1.0 - fixed_to[...].astype(F32)
    copies[3].wait()
    copies[4].wait()


def last_kernel(sums_ref, precond_ref, image_ref, packed_ref, update_ref, next_ref):
    total = jnp.sum(sums_ref[...], axis=0, keepdims=True)
    alpha = total[:, 0:1] / total[:, 1:2]
    for c in range(3):
        update_ref[c] = alpha * precond_ref[c]
        next_ref[c] = packed_ref[6 + c] - alpha * image_ref[c]


def from_peer(value, axis, step):
    peers = lax.axis_size(axis)
    return lax.ppermute(value, axis, [(i + step, i) for i in range(peers) if 0 <= i + step < peers])


def spread_all(row, axis):
    peers = lax.axis_size(axis)
    return lax.all_to_all(
        jnp.broadcast_to(row[None], (peers,) + row.shape), axis, 0, 0, tiled=True
    )


def on_device(density, solid, void, fixed, residual):
    packed = pl.pallas_call(
        pack_kernel,
        out_shape=jax.ShapeDtypeStruct((9,) + density.shape, F32),
        in_specs=[pl.BlockSpec(memory_space=pltpu.HBM)] * 5,
        scratch_shapes=[
            pltpu.VMEM((2,) + solid.shape, jnp.int32),
            pltpu.VMEM(fixed.shape, jnp.int32),
            pltpu.SemaphoreType.DMA((5,)),
        ],
        compiler_params=PARAMS,
    )(*[pltpu.with_memory_space_constraint(v, pltpu.HBM) for v in (density, solid, void, fixed, residual)])
    own, up, down = join_call(from_peer(packed, "gy", -1), packed, from_peer(packed, "gy", 1))
    first = first_call(from_peer(up, "gx", -1), own, from_peer(down, "gx", 1))
    level0, level1, piece = (first[0:4], first[4:8], first[8])
    columns = spread_all(piece, "gy")
    second = second_call(
        from_peer(columns, "gx", -1), columns, from_peer(columns, "gx", 1)
    )
    rows = spread_all(second[1].reshape(-1), "gx")
    precond, image, sums = third_call(rows, second[0], level1, level0)
    sums = jnp.sum(spread_all(sums[0], "gx"), axis=0)
    block = jax.ShapeDtypeStruct(residual.shape, F32)
    return tuple(
        pl.pallas_call(last_kernel, out_shape=[block, block], compiler_params=PARAMS)(
            spread_all(sums, "gy"), precond, image, packed
        )
    )


def solution(mesh):
    return jax.shard_map(
        on_device,
        mesh=mesh,
        in_specs=(
            P("gx", "gy", None),
            P("gx", "gy", None),
            P("gx", "gy", None),
            P(None, "gx", "gy", None),
            P(None, "gx", "gy", None),
        ),
        out_specs=(P(None, "gx", "gy", None), P(None, "gx", "gy", None)),
        check_vma=False,
    )
```

```python
import math

import jax
import jax.numpy as jnp
import numpy as np
from jax import lax
from jax.experimental import pallas as pl
from jax.experimental.pallas import tpu as pltpu
from jax.sharding import PartitionSpec as P

COARSE_ITERS = 4
DAMPING = 0.6
VOID_MODULUS = 0.001
F32 = jnp.float32
PARAMS = pltpu.CompilerParams(vmem_limit_bytes=16 * 1024 * 1024)


def corner_list():
    return [(a, b, c) for a in (0, 1) for b in (0, 1) for c in (0, 1)]


def element_stiffness():
    poisson = 0.3
    lame_first = poisson / ((1.0 + poisson) * (1.0 - 2.0 * poisson))
    shear = 0.5 / (1.0 + poisson)
    elastic = np.zeros((6, 6))
    elastic[:3, :3] = lame_first
    for i in range(3):
        elastic[i, i] += 2.0 * shear
        elastic[i + 3, i + 3] = shear
    points = [0.5 - 0.5 / math.sqrt(3.0), 0.5 + 0.5 / math.sqrt(3.0)]
    gauss = [(u, v, w) for u in points for v in points for w in points]
    stiffness = np.zeros((24, 24))
    for coord in gauss:
        strain = np.zeros((6, 24))
        for k, corner in enumerate(corner_list()):
            values = [coord[d] if corner[d] else 1.0 - coord[d] for d in range(3)]
            slopes = [2.0 * corner[d] - 1.0 for d in range(3)]
            grad_x = slopes[0] * values[1] * values[2]
            grad_y = values[0] * slopes[1] * values[2]
            grad_z = values[0] * values[1] * slopes[2]
            strain[0, 3 * k] = grad_x
            strain[1, 3 * k + 1] = grad_y
            strain[2, 3 * k + 2] = grad_z
            strain[3, 3 * k] = grad_y
            strain[3, 3 * k + 1] = grad_x
            strain[4, 3 * k + 1] = grad_z
            strain[4, 3 * k + 2] = grad_y
            strain[5, 3 * k] = grad_z
            strain[5, 3 * k + 2] = grad_x
        stiffness += strain.T @ elastic @ strain / 8.0
    return stiffness


def mode_table():
    corners = corner_list()
    signs = np.array(
        [[math.prod(2 * c[d] - 1 if m[d] else 1 for d in range(3)) for c in corners] for m in corners],
        float,
    )
    wide = np.kron(signs, np.eye(3))
    table = wide @ element_stiffness() @ wide.T / 64.0
    rows = {}
    for i in range(24):
        row = [
            (corners[j // 3], j % 3, float(table[i, j]))
            for j in range(24)
            if abs(table[i, j]) > 1e-12
        ]
        if row:
            rows[(corners[i // 3], i % 3)] = row
    return rows


MODES = mode_table()
DIAG = float(element_stiffness()[0, 0])
PAIRS = ((0, 0), (1, 0), (0, 1), (1, 1))


def flat_modes(field, z_up, y_up):
    after = z_up(field)
    out = {}
    for k, part in ((0, field + after), (1, after - field)):
        after = y_up(part)
        out[(0, k)] = part + after
        out[(1, k)] = after - part
    return [out[p] for p in PAIRS]


def element_modes(low, high, moduli):
    values = {}
    for c in range(3):
        for q, (j, k) in enumerate(PAIRS):
            if (j, k) != (0, 0):
                values[((0, j, k), c)] = low[c][q] + high[c][q]
            values[((1, j, k), c)] = high[c][q] - low[c][q]
    forces = {}
    for key, row in MODES.items():
        total = None
        for mode, c, weight in row:
            term = weight * values[(mode, c)]
            total = term if total is None else total + term
        forces[key] = total * moduli
    to_low, to_high = [], []
    for c in range(3):
        a, b = [], []
        for j, k in PAIRS:
            slope = forces[((1, j, k), c)]
            mean = forces.get(((0, j, k), c))
            a.append(-slope if mean is None else mean - slope)
            b.append(slope if mean is None else mean + slope)
        to_low.append(a)
        to_high.append(b)
    return to_low, to_high


def node_forces(parts, z_down, y_down):
    out = []
    for k in (0, 1):
        mean, slope = (parts[PAIRS.index((0, k))], parts[PAIRS.index((1, k))])
        out.append((mean - slope) + y_down(mean + slope))
    return (out[0] - out[1]) + z_down(out[0] + out[1])


def shift_up(value, axis):
    return pltpu.roll(value, value.shape[axis] - 1, axis)


def shift_down(value, axis):
    return pltpu.roll(value, 1, axis)


def lanes_of(shape):
    return lax.broadcasted_iota(jnp.int32, shape, len(shape) - 1)


def rows_of(shape):
    return lax.broadcasted_iota(jnp.int32, shape, 0)


def z_shifts(full):
    def up(v):
        s = shift_up(v, 1)
        return jnp.where(lanes_of(v.shape) < v.shape[1] - 1, s, 0.0) if full else s

    def down(v):
        s = shift_down(v, 1)
        return jnp.where(lanes_of(v.shape) > 0, s, 0.0) if full else s

    return up, down


def y_up(v):
    return shift_up(v, 0)


def y_down(v):
    return shift_down(v, 0)


def sweep(load, moduli, first, last, full, emit, unroll=True):
    z_up, z_down = z_shifts(full)

    def modes(x):
        return [flat_modes(load(c, x), z_up, y_up) for c in range(3)]

    high = modes(first + 1)
    _, up = element_modes(modes(first), high, moduli(first))

    def body(x, carry):
        low, before = carry
        high = modes(x + 1)
        own, up = element_modes(low, high, moduli(x))
        forces = [
            node_forces([own[c][q] + before[c][q] for q in range(4)], z_down, y_down)
            for c in range(3)
        ]
        emit(x, forces)
        return (high, up)

    lax.fori_loop(first + 1, last + 1, body, (high, up), unroll=unroll)


def exact_dot(a, b):
    return jnp.dot(a, b, precision=lax.Precision.HIGHEST, preferred_element_type=F32)


def tent(shape, fine, coarse):
    gap = jnp.abs(fine - 2 * coarse)
    return jnp.where(gap == 0, 1.0, jnp.where(gap == 1, 0.5, 0.0)).astype(F32)


def square(kind, period=128):
    shape = (128, 128)
    fine, coarse = (rows_of(shape), lax.rem(lanes_of(shape), period))
    if kind == "restrict":
        return tent(shape, fine, coarse)
    if kind == "pick":
        return jnp.where(fine == 2 * coarse, 1.0, 0.0).astype(F32)
    return jnp.where((fine == 2 * coarse) | (fine == 2 * coarse + 1), 1.0, 0.0).astype(F32)


def prolong_matrix(period=128):
    shape = (128, 128)
    return tent(shape, lanes_of(shape), lax.rem(rows_of(shape), period))


def smooth_rows(v):
    return v + 0.5 * (y_up(v) + y_down(v))


def corner_sum(v, z_down):
    v = v + z_down(v)
    return v + y_down(v)


def scaled(free, inverse):
    return jnp.where(free > 0.0, inverse, DAMPING)


def low_slab(f):
    return (0, 7, 14)[f] if f < 3 else 20 + 6 * (f - 3)


def high_slab(f):
    return 0 if f == 0 else 8 + 7 * (f - 1)


def join_kernel(lo_ref, mid_ref, hi_ref, own_ref, up_ref, down_ref):
    for r, ref in enumerate((lo_ref, mid_ref, hi_ref)):
        rows = slice(8 * r, 8 * r + 8)
        for f in range(9):
            v = ref[f]
            own_ref[f, :, rows, :] = v
            first = min(f, 1) if f < 3 else 2
            up_ref[low_slab(f) + first : low_slab(f) + 8, rows, :] = v[first:]
            last = 8 if f == 0 else 7
            down_ref[high_slab(f) : high_slab(f) + last, rows, :] = v[:last]


def join_call(lo, mid, hi):
    shapes = [(9, 8, 24, 128), (58, 24, 128), (64, 24, 128)]
    return pl.pallas_call(
        join_kernel,
        out_shape=[jax.ShapeDtypeStruct(shape, F32) for shape in shapes],
        compiler_params=PARAMS,
    )(lo, mid, hi)


def first_kernel(
    lo_ref, own_ref, hi_ref,
    m_out, i_out, f_out, r_out, m1_out, i1_out, f1_out, c1_out, pack_out,
    t_ref, b_ref, m_ref, i_ref, f_ref, r_ref, s_ref, u_ref, d_ref, v_ref, m1_ref, s1_ref, u1_ref, d1_ref, v2_ref,
):
    pieces = (
        lambda f, i: lo_ref[low_slab(f) + i],
        lambda f, i: own_ref[f, i],
        lambda f, i: hi_ref[high_slab(f) + i],
    )
    slab = (24, 128)
    z_up, z_down = z_shifts(True)
    gx, gy = (lax.axis_index("gx"), lax.axis_index("gy"))
    nodes_x, nodes_y = (8 * lax.axis_size("gx"), 8 * lax.axis_size("gy"))
    w0, w1, w2, w3 = [2.0 - math.sqrt(n) for n in range(4)]

    def each(first, last, body):
        for p, get in enumerate(pieces):
            a, b = (max(first, 8 * p), min(last, 8 * p + 7))
            if a <= b:
                lax.fori_loop(a - 8 * p, b - 8 * p + 1, lambda i, _, get=get, p=p: body(8 * p + i, get, i), None, unroll=True)

    def gather_flat(x, get, i):
        own = get(0, i)
        ring = z_up(own) + z_down(own)
        c1 = y_up(own) + y_down(own) + ring
        c2 = y_up(ring) + y_down(ring)
        b_ref[x] = w0 * own + w1 * c1 + w2 * c2
        t_ref[x] = w1 * own + w2 * c1 + w3 * c2

    each(0, 23, gather_flat)
    row_at = rows_of(slab) + (8 * gy - 8)
    lane_at = lanes_of(slab)
    inside = ((row_at >= 0) & (row_at < nodes_y)).astype(F32)
    ring_y = (row_at > 0).astype(F32) + (row_at < nodes_y - 1).astype(F32)
    ring_z = (lane_at > 0).astype(F32) + (lane_at < 127).astype(F32)
    plain = w0 + w1 * (ring_y + ring_z) + w2 * ring_y * ring_z
    beside = w1 + w2 * (ring_y + ring_z) + w3 * ring_y * ring_z
    inverse_two, inverse_one = (1.0 / (plain + 2.0 * beside), 1.0 / (plain + beside))

    def moduli_of(x, get, i):
        at = 8 * gx - 8 + x
        edge = (at == 0) | (at == nodes_x - 1)
        inverse = jnp.where(edge, inverse_one, inverse_two)
        filtered = (b_ref[x] + (t_ref[x - 1] + t_ref[x + 1])) * inverse
        solid, void = (get(1, i), get(2, i))
        physical = (1.0 - void) * (solid + (1.0 - solid) * filtered)
        value = VOID_MODULUS + (1.0 - VOID_MODULUS) * (physical * physical * physical)
        mask = jnp.where((at >= 0) & (at < nodes_x), inside, 0.0)
        m_ref[x] = value * mask

    each(1, 22, moduli_of)

    def smooth_of(x, get, i):
        total = corner_sum(m_ref[x] + m_ref[x - 1], z_down)
        inverse = (DAMPING / DIAG) / total
        i_ref[x] = inverse
        for c in range(3):
            free, r = (get(3 + c, i), get(6 + c, i))
            s = scaled(free, inverse) * r
            f_ref[c, x], r_ref[c, x], s_ref[c, x] = (free, r, s)
            u_ref[c, x] = free * s

    each(2, 22, smooth_of)

    def defect_of(x, forces):
        for c in range(3):
            free = f_ref[c, x]
            d_ref[c, x] = r_ref[c, x] - (free * forces[c] + (1.0 - free) * s_ref[c, x])

    sweep(lambda c, x: u_ref[c, x], lambda x: m_ref[x], 2, 21, True, defect_of)

    def keep(x, _):
        m_out[x] = m_ref[x + 6, 4:20, :]
        i_out[x] = i_ref[x + 6, 4:20, :]
        for c in range(3):
            f_out[c, x] = f_ref[c, x + 6, 4:20, :]
            r_out[c, x] = r_ref[c, x + 6, 4:20, :]

    lax.fori_loop(0, 12, keep, None, unroll=True)

    v_ref[:, 24:32, :] = jnp.zeros((64, 8, 128), F32)

    def to_coarse(n, _):
        x = 2 * n + 4
        for c in range(3):
            v = d_ref[c, x] + 0.5 * (d_ref[c, x - 1] + d_ref[c, x + 1])
            v_ref[9 * c + n, 0:24, :] = smooth_rows(v)
            v_ref[27 + 9 * c + n, 0:24, :] = f_ref[c, x]

    lax.fori_loop(0, 9, to_coarse, None, unroll=True)

    def to_coarse_moduli(n, _):
        x = 2 * n + 2
        v = m_ref[x] + m_ref[x + 1]
        v_ref[54 + n, 0:24, :] = v + y_up(v)

    lax.fori_loop(0, 10, to_coarse_moduli, None, unroll=True)

    def half(first, count, matrix):
        v = v_ref[first : first + count, pl.ds(0, 16, stride=2), :]
        return exact_dot(v.reshape(count * 16, 128), matrix).reshape(count, 16, 128)

    restrict, pick, pair = (square("restrict"), square("pick"), square("pair"))
    m1_ref[...] = 0.25 * half(54, 10, pair)
    m1_out[...] = m1_ref[1:10]
    for c in range(3):
        f1_out[c] = half(27 + 9 * c, 9, pick)
        c1_out[c] = f1_out[c] * half(9 * c, 9, restrict)
    _, plain_down = z_shifts(False)

    def smooth1(n, _):
        inverse = (DAMPING / DIAG) / corner_sum(m1_ref[n + 1] + m1_ref[n], plain_down)
        i1_out[n] = inverse
        for c in range(3):
            s = scaled(f1_out[c, n], inverse) * c1_out[c, n]
            s1_ref[c, n] = s
            u1_ref[c, n] = f1_out[c, n] * s

    lax.fori_loop(0, 9, smooth1, None, unroll=True)

    def defect1(n, forces):
        for c in range(3):
            free = f1_out[c, n]
            d1_ref[c, n] = c1_out[c, n] - (free * forces[c] + (1.0 - free) * s1_ref[c, n])

    sweep(lambda c, n: u1_ref[c, n], lambda n: m1_ref[n + 1], 0, 7, False, defect1)

    for n in range(3):
        x = 2 * n + 2
        for c in range(3):
            v2_ref[3 * c + n] = smooth_rows(d1_ref[c, x] + 0.5 * (d1_ref[c, x - 1] + d1_ref[c, x + 1]))
            v2_ref[9 + 3 * c + n] = f1_out[c, x]
    for n in range(4):
        v = m1_ref[2 * n + 1] + m1_ref[2 * n + 2]
        v2_ref[18 + n] = v + y_up(v)

    def half2(first, count, matrix):
        v = v2_ref[first : first + count, pl.ds(0, 8, stride=2), :]
        return exact_dot(v.reshape(count * 8, 128), matrix).reshape(count, 8, 128)

    free2 = half2(9, 9, pick)
    rhs2 = half2(0, 9, restrict) * free2
    moduli2 = 0.25 * half2(18, 4, pair)
    fields = [[moduli2[1 + n] for n in range(3)]]
    fields += [[free2[3 * c + n] for n in range(3)] for c in range(3)]
    fields += [[rhs2[3 * c + n] for n in range(3)] for c in range(3)]
    valid = lanes_of((8, 128)) < 32
    inverse = []
    for n in range(3):
        total = corner_sum(moduli2[n + 1] + moduli2[n], plain_down)
        inverse.append(jnp.where(total > 0.0, (DAMPING / DIAG) / total, 0.0))
    fields.append(inverse)
    for f, slabs in enumerate(fields):
        rows = [None, None]
        for n in range(3):
            v = jnp.where(valid, slabs[n], 0.0)
            for y in range(2):
                piece = v[2 + y : 3 + y]
                q = 2 * (n % 2) + y
                piece = pltpu.roll(piece, 32 * q, 1) if q else piece
                rows[n // 2] = piece if rows[n // 2] is None else rows[n // 2] + piece
        pack_out[f : f + 1, 0:128] = rows[0]
        pack_out[f : f + 1, 128:256] = rows[1]


def first_call(lo, own, hi):
    big = lambda *s: jax.ShapeDtypeStruct(s + (16, 128), F32)
    s24 = lambda *s: pltpu.VMEM(s + (24, 128), F32)
    return pl.pallas_call(
        first_kernel,
        out_shape=[big(12), big(12), big(3, 12), big(3, 12)]
        + [big(9), big(9), big(3, 9), big(3, 9), jax.ShapeDtypeStruct((8, 256), F32)],
        scratch_shapes=[s24(24)] * 4
        + [s24(3, 24)] * 5
        + [
            pltpu.VMEM((64, 32, 128), F32),
            pltpu.VMEM((10, 16, 128), F32),
            pltpu.VMEM((3, 9, 16, 128), F32),
            pltpu.VMEM((3, 9, 16, 128), F32),
            pltpu.VMEM((3, 9, 16, 128), F32),
            pltpu.VMEM((22, 16, 128), F32),
        ],
        compiler_params=PARAMS,
    )(lo, own, hi)


def second_kernel(lo_ref, own_ref, hi_ref, l_out, pack_out, s_ref, u_ref, d_ref, v_ref):
    peers = own_ref.shape[0]
    l_out[...] = jnp.zeros(l_out.shape, F32)
    valid = lanes_of((peers, 128)) < 32
    for ref, base, count in ((lo_ref, 0, 2), (own_ref, 2, 2), (hi_ref, 4, 3)):
        for f in range(8):
            for h in range((count + 1) // 2):
                rows = ref[:, f, 128 * h : 128 * h + 128]
                for n in range(2 * h, min(2 * h + 2, count)):
                    for y in range(2):
                        q = 2 * (n % 2) + y
                        v = pltpu.roll(rows, 128 - 32 * q, 1) if q else rows
                        l_out[f, base + n, pl.ds(y, peers, stride=2), :] = jnp.where(valid, v, 0.0)

    def smooth(n, _):
        inverse = l_out[7, n]
        for c in range(3):
            s = scaled(l_out[1 + c, n], inverse) * l_out[4 + c, n]
            s_ref[c, n] = s
            u_ref[c, n] = l_out[1 + c, n] * s

    lax.fori_loop(0, 5, smooth, None, unroll=True)

    def defect(n, forces):
        for c in range(3):
            free = l_out[1 + c, n]
            d_ref[c, n] = l_out[4 + c, n] - (free * forces[c] + (1.0 - free) * s_ref[c, n])

    sweep(lambda c, n: u_ref[c, n], lambda n: l_out[0, n], 0, 3, False, defect)
    for c in range(3):
        v_ref[c] = smooth_rows(d_ref[c, 2] + 0.5 * (d_ref[c, 1] + d_ref[c, 3]))
        v_ref[3 + c] = l_out[1 + c, 2]
    v = l_out[0, 2] + l_out[0, 3]
    v_ref[6] = v + y_up(v)

    def half(first, count, matrix):
        v = v_ref[first : first + count, pl.ds(0, 16, stride=2), :]
        return exact_dot(v.reshape(count * 16, 128), matrix).reshape(count, 16, 128)

    free = half(3, 3, square("pick", 16))
    rhs = half(0, 3, square("restrict", 16)) * free
    moduli = 0.25 * half(6, 1, square("pair", 16))
    shape = (8, 128)
    own_lane = (lanes_of(shape) // 16) == rows_of(shape)
    fields = []
    for v in (moduli[0], free[0], free[1], free[2], rhs[0], rhs[1], rhs[2]):
        fields.append(
            [
                jnp.sum(jnp.where(own_lane, v[8 * h : 8 * h + 8], 0.0), axis=0, keepdims=True)
                for h in range(2)
            ]
        )
    for t, v in enumerate(pack_rows(fields)):
        pack_out[:, 128 * t : 128 * t + 128] = v


def second_call(lo, own, hi):
    big = lambda *s: jax.ShapeDtypeStruct(s + (32, 128), F32)
    vmem = lambda *s: pltpu.VMEM(s + (32, 128), F32)
    return pl.pallas_call(
        second_kernel,
        out_shape=[big(8, 7), jax.ShapeDtypeStruct((1, 1408), F32)],
        scratch_shapes=[vmem(3, 5), vmem(3, 5), vmem(3, 4), vmem(7)],
        compiler_params=PARAMS,
    )(lo, own, hi)


def pack_rows(fields):
    out = []
    low = lanes_of(fields[0][0].shape) < 64
    turn = lambda v: pltpu.roll(v, 64, 1)
    for k in range(0, 6, 2):
        (a0, a1), (b0, b1) = (fields[k], fields[k + 1])
        middle = turn(b0)
        out += [a0, jnp.where(low, a1, middle), jnp.where(low, middle, turn(b1))]
    return out + fields[6]


def unpack_rows(tiles):
    out = []
    low = lanes_of(tiles[0].shape) < 64
    turn = lambda v: pltpu.roll(v, 64, 1)
    for k in range(0, 9, 3):
        t0, t1, t2 = tiles[k : k + 3]
        r1, r2 = (turn(t1), turn(t2))
        out.append([t0, jnp.where(low, t1, 0.0)])
        out.append([jnp.where(low, r1, r2), jnp.where(low, r2, 0.0)])
    return out + [tiles[9:11]]


def coarse_solve(rows_ref):
    peers = rows_ref.shape[0]
    shape = (peers + 8, 256)

    fields = unpack_rows([rows_ref[:, 128 * t : 128 * t + 128] for t in range(11)])

    def field(f):
        v = jnp.concatenate(fields[f], axis=1)
        return jnp.concatenate([v, jnp.zeros((8, 256), F32)], axis=0)

    depth = lanes_of(shape) & 15
    z_up = lambda v: jnp.where(depth < 15, shift_up(v, 1), 0.0)
    z_down = lambda v: jnp.where(depth > 0, shift_down(v, 1), 0.0)
    side_up = lambda v: pltpu.roll(v, 240, 1)
    side_down = lambda v: pltpu.roll(v, 16, 1)
    moduli = field(0)
    free = [field(1 + c) for c in range(3)]
    resid = [field(4 + c) for c in range(3)]
    total = moduli + z_down(moduli)
    total = total + side_down(total)
    total = DIAG * (total + shift_down(total, 0))
    inverse = [1.0 / jnp.where(f > 0.0, total, 1.0) for f in free]

    def dot(a, b):
        return jnp.sum(a[0] * b[0] + a[1] * b[1] + a[2] * b[2], keepdims=True)

    def operator(v):
        low = [flat_modes(v[c] * free[c], z_up, side_up) for c in range(3)]
        high = [[shift_up(p, 0) for p in low[c]] for c in range(3)]
        own, up = element_modes(low, high, moduli)
        out = []
        for c in range(3):
            parts = [own[c][q] + shift_down(up[c][q], 0) for q in range(4)]
            forces = node_forces(parts, z_down, side_down)
            out.append(free[c] * forces + (1.0 - free[c]) * v[c])
        return out

    precond = [r * i for r, i in zip(resid, inverse)]
    direction = precond
    inner = dot(resid, precond)
    answer = None
    for step in range(COARSE_ITERS):
        image = operator(direction)
        alpha = inner / dot(direction, image)
        moved = [alpha * d for d in direction]
        answer = moved if answer is None else [s + m for s, m in zip(answer, moved)]
        if step + 1 < COARSE_ITERS:
            resid = [r - alpha * q for r, q in zip(resid, image)]
            precond = [r * i for r, i in zip(resid, inverse)]
            inner_new = dot(resid, precond)
            ratio = inner_new / inner
            direction = [z + ratio * d for z, d in zip(precond, direction)]
            inner = inner_new
    return answer


def third_kernel(
    rows_ref, l2_ref, m1_ref, i1_ref, f1_ref, c1_ref, m_ref, i_ref, f_ref, r_ref,
    p_out, q_out, sum_out,
    a_ref, z3_ref, u2_ref, y2_ref, v2_ref, p1_ref, u1_ref, y1_ref, v1_ref, p0_ref, u0_ref, y0_ref,
):
    gx, gy = (lax.axis_index("gx"), lax.axis_index("gy"))
    peers = rows_ref.shape[0]
    answer = coarse_solve(rows_ref)
    for c in range(3):
        a_ref[c, 0:8, :] = jnp.zeros((8, 256), F32)
        a_ref[c, 8 : 16 + peers, :] = answer[c]

    spread3 = prolong_matrix(16)
    shape = (8, 128)
    own_lane = (lanes_of(shape) // 16) == rows_of(shape)
    for c in range(3):
        for i in range(4):
            row = a_ref[c, pl.ds(gx + 7 + i, 1), :]
            halves = [
                jnp.where(own_lane, jnp.broadcast_to(row[:, 128 * h : 128 * h + 128], shape), 0.0)
                for h in range(2)
            ]
            w = exact_dot(jnp.concatenate(halves, axis=0), spread3)
            z3_ref[i, pl.ds(0, 16, stride=2), :] = w
            z3_ref[i, pl.ds(1, 16, stride=2), :] = 0.5 * (w + y_up(w))
        for n in range(7):
            i = n // 2
            p = z3_ref[i] if n % 2 == 0 else 0.5 * (z3_ref[i] + z3_ref[i + 1])
            free = l2_ref[1 + c, n]
            s = scaled(free, l2_ref[7, n]) * l2_ref[4 + c, n] + free * p
            y2_ref[c, n] = s
            u2_ref[c, n] = free * s

    v2_ref[...] = jnp.zeros(v2_ref.shape, F32)

    def level2(n, forces):
        for c in range(3):
            free, s = (l2_ref[1 + c, n], y2_ref[c, n])
            image = free * forces[c] + (1.0 - free) * s
            v2_ref[c, n - 1, 8:40, :] = s + scaled(free, l2_ref[7, n]) * (l2_ref[4 + c, n] - image)

    sweep(lambda c, n: u2_ref[c, n], lambda n: l2_ref[0, n], 0, 5, False, level2)

    spread = prolong_matrix()
    for c in range(3):
        for i in range(5):
            w = exact_dot(v2_ref[c, i, pl.ds(2 * gy + 6, 16), :], spread)
            p1_ref[c, i, pl.ds(0, 8, stride=2), :] = w[0:8]
            p1_ref[c, i, pl.ds(1, 8, stride=2), :] = 0.5 * (w[0:8] + w[1:9])
        for n in range(9):
            i = n // 2
            p = p1_ref[c, i] if n % 2 == 0 else 0.5 * (p1_ref[c, i] + p1_ref[c, i + 1])
            free = f1_ref[c, n]
            s = scaled(free, i1_ref[n]) * c1_ref[c, n] + free * p
            y1_ref[c, n] = s
            u1_ref[c, n] = free * s

    def level1(n, forces):
        for c in range(3):
            free, s = (f1_ref[c, n], y1_ref[c, n])
            image = free * forces[c] + (1.0 - free) * s
            v1_ref[c, n - 1] = s + scaled(free, i1_ref[n]) * (c1_ref[c, n] - image)

    sweep(lambda c, n: u1_ref[c, n], lambda n: m1_ref[n], 0, 7, False, level1)

    for c in range(3):
        w = exact_dot(v1_ref[c].reshape(7 * 16, 128), spread).reshape(7, 16, 128)
        for i in range(7):
            p0_ref[c, i, pl.ds(0, 8, stride=2), :] = w[i, 2:10]
            p0_ref[c, i, pl.ds(1, 8, stride=2), :] = 0.5 * (w[i, 2:10] + w[i, 3:11])
        for n in range(12):
            i = n // 2
            p = p0_ref[c, i] if n % 2 == 0 else 0.5 * (p0_ref[c, i] + p0_ref[c, i + 1])
            free = f_ref[c, n]
            s = scaled(free, i_ref[n]) * r_ref[c, n] + free * p
            y0_ref[c, n] = s
            u0_ref[c, n] = free * s

    def level0(n, forces):
        for c in range(3):
            free, s = (f_ref[c, n], y0_ref[c, n])
            image = free * forces[c] + (1.0 - free) * s
            y0_ref[c, n] = s + scaled(free, i_ref[n]) * (r_ref[c, n] - image)

    sweep(lambda c, n: u0_ref[c, n], lambda n: m_ref[n], 0, 10, True, level0)
    sum_out[...] = jnp.zeros((8, 128), F32)

    def last(n, forces):
        one = two = None
        for c in range(3):
            free, v = (f_ref[c, n], y0_ref[c, n])
            image = (free * forces[c] + (1.0 - free) * v)[4:12]
            v = v[4:12]
            p_out[c, n - 2] = v
            q_out[c, n - 2] = image
            a, b = (r_ref[c, n, 4:12, :] * v, v * image)
            one, two = ((a, b) if one is None else (one + a, two + b))
        sum_out[0:1, :] = sum_out[0:1, :] + jnp.sum(one, axis=0, keepdims=True)
        sum_out[1:2, :] = sum_out[1:2, :] + jnp.sum(two, axis=0, keepdims=True)

    sweep(lambda c, n: f_ref[c, n] * y0_ref[c, n], lambda n: m_ref[n], 1, 9, True, last)
    lane = lanes_of((1, 128))
    one = jnp.sum(sum_out[0:1, :], keepdims=True)
    two = jnp.sum(sum_out[1:2, :], keepdims=True)
    sum_out[0:1, :] = jnp.where(lane == 0, one, jnp.where(lane == 1, two, 0.0))


def third_call(rows, level2, level1, level0):
    own = jax.ShapeDtypeStruct((3, 8, 8, 128), F32)
    peers = rows.shape[0]
    return pl.pallas_call(
        third_kernel,
        out_shape=[own, own, jax.ShapeDtypeStruct((8, 128), F32)],
        scratch_shapes=[
            pltpu.VMEM((3, peers + 16, 256), F32),
            pltpu.VMEM((4, 32, 128), F32),
            pltpu.VMEM((3, 7, 32, 128), F32),
            pltpu.VMEM((3, 7, 32, 128), F32),
            pltpu.VMEM((3, 5, 48, 128), F32),
            pltpu.VMEM((3, 5, 16, 128), F32),
            pltpu.VMEM((3, 9, 16, 128), F32),
            pltpu.VMEM((3, 9, 16, 128), F32),
            pltpu.VMEM((3, 7, 16, 128), F32),
            pltpu.VMEM((3, 7, 16, 128), F32),
            pltpu.VMEM((3, 12, 16, 128), F32),
            pltpu.VMEM((3, 12, 16, 128), F32),
        ],
        compiler_params=PARAMS,
    )(rows, level2, *level1, *level0)


def pack_kernel(density_ref, solid_ref, void_ref, fixed_ref, residual_ref, out_ref, flags_ref, fixed_to, sems):
    copies = [
        pltpu.make_async_copy(solid_ref, flags_ref.at[0], sems.at[0]),
        pltpu.make_async_copy(void_ref, flags_ref.at[1], sems.at[1]),
        pltpu.make_async_copy(fixed_ref, fixed_to, sems.at[2]),
        pltpu.make_async_copy(density_ref, out_ref.at[0], sems.at[3]),
        pltpu.make_async_copy(residual_ref, out_ref.at[pl.ds(6, 3)], sems.at[4]),
    ]
    for copy in copies:
        copy.start()
    copies[0].wait()
    out_ref[1] = flags_ref[0].astype(F32)
    copies[1].wait()
    out_ref[2] = flags_ref[1].astype(F32)
    copies[2].wait()
    out_ref[3:6] = 1.0 - fixed_to[...].astype(F32)
    copies[3].wait()
    copies[4].wait()


def last_kernel(sums_ref, precond_ref, image_ref, packed_ref, update_ref, next_ref):
    total = jnp.sum(sums_ref[...], axis=0, keepdims=True)
    alpha = total[:, 0:1] / total[:, 1:2]
    for c in range(3):
        update_ref[c] = alpha * precond_ref[c]
        next_ref[c] = packed_ref[6 + c] - alpha * image_ref[c]


def from_peer(value, axis, step):
    peers = lax.axis_size(axis)
    return lax.ppermute(value, axis, [(i + step, i) for i in range(peers) if 0 <= i + step < peers])


def spread_all(row, axis):
    peers = lax.axis_size(axis)
    return lax.all_to_all(
        jnp.broadcast_to(row[None], (peers,) + row.shape), axis, 0, 0, tiled=True
    )


def on_device(density, solid, void, fixed, residual):
    packed = pl.pallas_call(
        pack_kernel,
        out_shape=jax.ShapeDtypeStruct((9,) + density.shape, F32),
        in_specs=[pl.BlockSpec(memory_space=pltpu.HBM)] * 5,
        scratch_shapes=[
            pltpu.VMEM((2,) + solid.shape, jnp.int32),
            pltpu.VMEM(fixed.shape, jnp.int32),
            pltpu.SemaphoreType.DMA((5,)),
        ],
        compiler_params=PARAMS,
    )(*[pltpu.with_memory_space_constraint(v, pltpu.HBM) for v in (density, solid, void, fixed, residual)])
    own, up, down = join_call(from_peer(packed, "gy", -1), packed, from_peer(packed, "gy", 1))
    first = first_call(from_peer(up, "gx", -1), own, from_peer(down, "gx", 1))
    level0, level1, piece = (first[0:4], first[4:8], first[8])
    columns = spread_all(piece, "gy")
    second = second_call(
        from_peer(columns, "gx", -1), columns, from_peer(columns, "gx", 1)
    )
    rows = spread_all(second[1].reshape(-1), "gx")
    precond, image, sums = third_call(rows, second[0], level1, level0)
    sums = jnp.sum(spread_all(sums[0], "gy"), axis=0)
    block = jax.ShapeDtypeStruct(residual.shape, F32)
    return tuple(
        pl.pallas_call(last_kernel, out_shape=[block, block], compiler_params=PARAMS)(
            spread_all(sums, "gx"), precond, image, packed
        )
    )


def solution(mesh):
    return jax.shard_map(
        on_device,
        mesh=mesh,
        in_specs=(
            P("gx", "gy", None),
            P("gx", "gy", None),
            P("gx", "gy", None),
            P(None, "gx", "gy", None),
            P(None, "gx", "gy", None),
        ),
        out_specs=(P(None, "gx", "gy", None), P(None, "gx", "gy", None)),
        check_vma=False,
    )
```
